512 devices in a mesh: tm: 16 (over y, core), rows: 32 (over z, x).
Axes of the slice: x: 4, y: 8, z: 8, core: 2. Of those that a mesh axis runs over, the one named last changes fastest.
Arguments:
- features: float32 [32, 128, 128, 256], P('tm', 'rows'), may hold values from -60 to 60
- norm_gain: float32 [256], replicated, may hold values from 0.1 to 1.9
- conv_weight: float32 [3, 256, 256], replicated, may hold values from -0.21875 to 0.21875
- proj_weight: float32 [2048, 512], P(None, 'rows'), may hold values from -0.125 to 0.125
- attn_gain: float32 [512], replicated, may hold values from 0.5 to 6
- qkv_weight: float32 [512, 1536], P(None, 'rows'), may hold values from -0.25 to 0.25
- out_weight: float32 [512, 512], replicated, may hold values from -0.25 to 0.25
Outputs:
- encoded: float32 [16, 64, 64, 512], P('tm', 'rows')
The draws below stay inside these ranges and needn't reach their ends.
All inputs are finite; a program needn't handle non-finite values.
Results may differ from the reference program's by a relative error of at most 0.0003.
Values sent between devices are 32-bit elements; how exact they have to be, the bound alone decides.
A program may use at most 128 MiB of HBM per device.

```python
import jax
import jax.numpy as jnp
import numpy as np
from jax import lax

C = 256
D = 512
GROUPS = 32
WD = 128
FRAMES = 32
HEIGHT = 128


def draw_features(key, part):
    key = jax.random.fold_in(key, 11)
    keys_list = jax.random.split(key, 4)
    shape = (FRAMES, HEIGHT, WD, C)
    ramp = 1.0 + 2.0 * jnp.arange(FRAMES, dtype=jnp.float32) / max(FRAMES - 1, 1)
    frame_scale = ramp * jnp.exp(jax.random.uniform(keys_list[1], (FRAMES,), jnp.float32, -0.4, 0.4))
    base = jnp.clip(jax.random.normal(keys_list[0], shape, jnp.float32), -5.0, 5.0)
    chan_scale = jnp.exp(jax.random.uniform(keys_list[2], (C,), jnp.float32, -0.7, 0.7))
    offset = jax.random.uniform(keys_list[3], (FRAMES, 1, 1, C), jnp.float32, -1.0, 1.0)
    return frame_scale[:, None, None, None] * (base * chan_scale + offset)


def draw_attn_gain(key, part):
    key = jax.random.fold_in(key, 23)
    return jax.random.uniform(key, (D,), jnp.float32, 0.5, 1.5)


def block_scale(stream_key, shape, cuts, smallest, top_value):
    level, own = 1.0, jax.random.fold_in(stream_key, 6)
    for axis_at, parts in cuts:
        heights = jnp.exp(jax.random.uniform(jax.random.fold_in(own, axis_at), (parts,), jnp.float32, smallest / len(cuts), top_value / len(cuts)))
        level = level * jnp.repeat(heights, shape[axis_at] // parts).reshape([-1 if axis == axis_at else 1 for axis in range(len(shape))])
    return level


def scatter_about(own_key, extent, width, reach, pieces=(), kind=jnp.bfloat16):
    factor_of = block_scale(own_key, extent, pieces, -0.22, 0.18) if pieces else 1.0
    array = jax.random.normal(own_key, extent, jnp.float32) * width * factor_of
    return jnp.minimum(jnp.maximum(array, -reach), reach).astype(kind)


def setup_inputs(seed: int = 0) -> dict:
    key_list = jax.random.split(jax.random.key(seed), 8)
    features = draw_features(jax.random.fold_in(key_list[7], 71), 0)
    norm_gain = jnp.clip(1.0 + 0.18 * jax.random.normal(key_list[1], (C,), jnp.float32), 0.1, 1.9)
    conv_weight = scatter_about(key_list[2], (3, C, C), (3 * C) ** -0.5, 0.21875, (), jnp.float32)
    proj_weight = scatter_about(key_list[3], (8 * C, D), (8 * C) ** -0.5, 0.125, ((1, 32),), jnp.float32)
    attn_gain = draw_attn_gain(jax.random.fold_in(key_list[7], 71), 0)
    qkv_weight = scatter_about(key_list[5], (D, 3 * D), D ** -0.5, 0.25, ((1, 32),), jnp.float32)
    out_weight = scatter_about(key_list[6], (D, D), D ** -0.5, 0.25, (), jnp.float32)
    return dict(features=features, norm_gain=norm_gain, conv_weight=conv_weight, proj_weight=proj_weight, attn_gain=attn_gain, qkv_weight=qkv_weight, out_weight=out_weight)


epsilon = 1e-06
highest = lax.Precision.HIGHEST

def hadamard_table():
    signs = np.ones((8, 8), np.float32)
    for source in range(8):
        for target in range(8):
            common = source & target
            parity = ((common & 1) + (common >> 1 & 1) + (common >> 2 & 1)) % 2
            signs[source, target] = 1.0 - 2.0 * parity
    return signs / np.sqrt(8.0)

def normalize(values, means, variance, gain):
    frames_now = values.shape[0]
    channels = values.shape[-1]
    grouped = values.reshape(frames_now, -1, GROUPS, channels // GROUPS)
    normed = (grouped - means[:, None, :, None]) * lax.rsqrt(variance + epsilon)[:, None, :, None]
    return normed.reshape(values.shape) * gain

def reference(features, norm_gain, conv_weight, proj_weight, attn_gain, qkv_weight, out_weight):
    frames, height, columns, channels = features.shape
    per_group = channels // GROUPS
    grouped = features.reshape(frames, height * columns, GROUPS, per_group)
    first = lax.optimization_barrier(jnp.sum(grouped, axis=(1, 3)))
    second = lax.optimization_barrier(jnp.sum(grouped * grouped, axis=(1, 3)))
    counts = (jnp.arange(frames, dtype=jnp.int32) + 1).astype(jnp.float32) * float(height * columns * per_group)
    means = jnp.cumsum(first, axis=0) / counts[:, None]
    variance = jnp.cumsum(second, axis=0) / counts[:, None] - means * means
    activated = jax.nn.silu(normalize(features, means, variance, norm_gain))
    zeros_front = jnp.zeros((2, height, columns, channels), jnp.float32)
    padded = jnp.concatenate([zeros_front, activated], axis=0).reshape(frames + 2, height * columns, channels)
    convolved = jnp.zeros((frames, height * columns, channels), jnp.float32)
    for lagged in range(3):
        convolved = convolved + jnp.einsum('fmc,cd->fmd', padded[2 - lagged:2 - lagged + frames], conv_weight[lagged], precision=highest)
    residual = features + convolved.reshape(features.shape)
    half_f, half_h, half_w = (frames // 2, height // 2, columns // 2)
    cell_stack = residual.reshape(half_f, 2, half_h, 2, half_w, 2, channels).transpose(0, 2, 4, 1, 3, 5, 6).reshape(-1, 8, channels)
    subbands = jnp.einsum('jk,nkc->njc', jnp.asarray(hadamard_table()), cell_stack, precision=highest).reshape(-1, 8 * channels)
    tokens = jnp.dot(subbands, proj_weight, precision=highest).reshape(half_f, half_h * half_w, D)
    grouped_tokens = tokens.reshape(half_f, -1, GROUPS, D // GROUPS)
    token_count = float(half_h * half_w * (D // GROUPS))
    token_means = lax.optimization_barrier(jnp.sum(grouped_tokens, axis=(1, 3))) / token_count
    token_variance = lax.optimization_barrier(jnp.sum(grouped_tokens * grouped_tokens, axis=(1, 3))) / token_count - token_means * token_means
    normed = normalize(tokens, token_means, token_variance, attn_gain)
    projected = jnp.einsum('fnd,de->fne', normed, qkv_weight, precision=highest)
    queries = projected[..., :D]
    keys_all = projected[..., D:2 * D]
    values_all = projected[..., 2 * D:]
    score_scale = 1.0 / np.sqrt(float(D))

    def one_frame(operands):
        frame_queries, frame_keys, frame_values = operands
        scores = jnp.dot(frame_queries, frame_keys.T, precision=highest) * score_scale
        return jnp.dot(jax.nn.softmax(scores, axis=-1), frame_values, precision=highest)
    attended = lax.map(one_frame, (queries, keys_all, values_all))
    encoded = tokens + jnp.einsum('fnd,de->fne', attended, out_weight, precision=highest)
    return encoded.reshape(half_f, half_h, half_w, D)
```

```python
import functools
import math

import jax
import jax.numpy as jnp
from jax import lax
from jax.experimental import pallas as pl
from jax.experimental.pallas import tpu as pltpu
from jax.sharding import PartitionSpec as P

GROUPS = 32
X = 4
epsilon = 1e-06
highest = lax.Precision.HIGHEST
f32, bf16 = jnp.float32, jnp.bfloat16
NN = (((1,), (0,)), ((), ()))
NT = (((1,), (1,)), ((), ()))
BOTH = (0, 1)


def split(value):
    high = value.astype(bf16)
    return high, (value - high.astype(f32)).astype(bf16)


def dot(a, b, dims):
    return lax.dot_general(a, b, dims, preferred_element_type=f32)


def dot3(a, b, dims=NN):
    rows = a[0].shape[0]
    if rows > 256:
        deep = (b[0], b[0], b[1])
        return dot(jnp.concatenate((a[0], a[1], a[0]), axis=1), jnp.concatenate(deep, axis=dims[0][1][0]), dims)
    by_high = dot(jnp.concatenate(a, axis=0), b[0], dims)
    return by_high[:rows] + (by_high[rows:] + dot(a[0], b[1], dims))


def exact(a, b):
    return lax.dot_general(a, b, NN, precision=highest, preferred_element_type=f32)


def iota(shape, axis):
    return lax.broadcasted_iota(jnp.int32, shape, axis)


def rsqrt(value):
    return lax.rsqrt(value + epsilon)


def mod(value, size):
    return lax.rem(value + size, size)


class Plan:
    def __init__(self):
        self.now, self.waits = 0.0, []

    def expect(self, time, name, action):
        self.waits.append((time, len(self.waits), name, action))

    def upto(self, time):
        while True:
            due = [wait for wait in self.waits if wait[0] <= time]
            if not due:
                return
            first = min(due, key=lambda wait: wait[:2])
            self.waits.remove(first)
            first[3]()

    def need(self, name):
        times = [wait[0] for wait in self.waits if wait[2] == name]
        if times:
            self.now = max(self.now, max(times))
            self.upto(max(times))

    def run(self, duration, action, *needs):
        for name in needs:
            self.need(name)
        self.upto(self.now)
        result = action()
        self.now += duration
        return result


class Links:
    def __init__(self, z_count, x_count, tm_count):
        self.rows, self.tm = lax.axis_index("rows"), lax.axis_index("tm")
        self.z, self.x = lax.div(self.rows, x_count), lax.rem(self.rows, x_count)
        self.y, self.core = lax.div(self.tm, 2), lax.rem(self.tm, 2)
        self.z_count, self.x_count, self.y_count = z_count, x_count, tm_count // 2

    def z_device(self, by):
        return {"rows": mod(self.z + by, self.z_count) * self.x_count + self.x}

    def x_device(self, by):
        return {"rows": self.z * self.x_count + mod(self.x + by, self.x_count)}

    def y_device(self, by):
        return {"tm": mod(self.y + by, self.y_count) * 2 + self.core}

    def sibling(self):
        return {"tm": self.tm + 1 - 2 * self.core}


def copy(src, dst, send, recv, device):
    return pltpu.make_async_remote_copy(
        src_ref=src, dst_ref=dst, send_sem=send, recv_sem=recv, device_id=device,
        device_id_type=pl.DeviceIdType.MESH,
    )


class Ring:
    def __init__(self, place, count, device, at, send, recv, reach, chunks=1, half=None, arrived=None):
        self.place, self.count, self.device, self.at, self.half = place, count, device, at, half
        self.send, self.recv, self.reach, self.chunks, self.arrived = send, recv, reach, chunks, arrived

    def moves(self, step, way, chunk):
        if step > self.reach[way]:
            return False
        shared = step == self.reach[0] == self.reach[1] and 2 * step == self.count
        return not shared or self.chunks == 1 or chunk == way

    def ref(self, away, step, way, chunk):
        ref = self.at(mod(self.place + away, self.count), chunk)
        return self.half(ref, way) if self.half and 2 * step == self.count else ref

    def copy(self, step, way, chunk, away):
        ref = self.ref(away, step, way, chunk)
        at = (way * self.chunks + chunk, step - 1)
        return copy(ref, ref, self.send.at[at], self.recv.at[at], self.device(1 if way == 0 else -1))

    def outgoing(self, step, way, chunk):
        return self.copy(step, way, chunk, 1 - step if way == 0 else step - 1)

    def start(self, way, chunk):
        self.outgoing(1, way, chunk).start()

    def step(self, step, way, chunk):
        if not self.moves(step, way, chunk):
            return
        away = -step if way == 0 else step
        self.copy(step, way, chunk, away).wait_recv()
        if self.moves(step + 1, way, chunk):
            self.outgoing(step + 1, way, chunk).start()
        if self.arrived:
            self.arrived(self.ref(away, step, way, chunk))

    def each(self):
        for step in range(1, max(self.reach) + 1):
            for chunk in range(self.chunks):
                for way in BOTH:
                    if self.moves(step, way, chunk):
                        yield step, way, chunk

    def finish(self):
        for step, way, chunk in self.each():
            self.outgoing(step, way, chunk).wait_send()


class Sums:
    def __init__(self, slots, index, per, size, device, send, recv):
        self.slots, self.index, self.per, self.size, self.device = slots, index, per, size, device
        self.send, self.recv = send, recv

    def copies(self, by):
        ref = self.slots.at[pl.ds(self.index * self.per, self.per)]
        return copy(ref, ref, self.send, self.recv, self.device(by))

    def everything(self):
        ref = self.slots.at[pl.ds(0, (self.size - 1) * self.per)]
        return copy(ref, ref, self.send, self.recv, self.device(1))

    def start(self):
        for by in range(1, self.size):
            self.copies(by).start()

    def wait(self):
        self.everything().wait_recv()

    def finish(self):
        self.everything().wait_send()


class Proj:
    def __init__(self, links, buf, sems):
        self.k, self.buf = links, buf
        az_s, az_r, self.ax_s, self.ax_r, self.bx_s, self.bx_r, bz_s, bz_r, self.c_s, self.c_r = sems
        self.core = links.core
        rows, xs, steps = buf.shape[4] // 2, links.x_count // 2, links.z_count // 2
        self.first = Ring(links.z, links.z_count, links.z_device, lambda z, chunk: buf.at[self.core, 0, z, links.x],
                          az_s, az_r, (steps, steps), 1, lambda ref, way: ref.at[pl.ds(way * rows, rows)])
        self.second = Ring(links.z, links.z_count, links.z_device,
                           lambda z, chunk: buf.at[self.core, 1, z, pl.ds(chunk * xs, xs)],
                           bz_s, bz_r, (steps, steps), 2, None, self.hand_second)
        self.steps = steps

    def ax(self, away, by):
        ref = self.buf.at[self.core, 0, mod(self.k.z + away, self.k.z_count), self.k.x]
        return copy(ref, ref, self.ax_s.at[by], self.ax_r.at[by], self.k.x_device(by))

    def ax_all(self, by, away):
        ref = self.buf.at[self.core, 0, :, mod(self.k.x + away, self.k.x_count)]
        return copy(ref, ref, self.ax_s.at[by], self.ax_r.at[by], self.k.x_device(by))

    def bx(self, by, away):
        ref = self.buf.at[self.core, 1, self.k.z, mod(self.k.x + away, self.k.x_count)]
        return copy(ref, ref, self.bx_s.at[by], self.bx_r.at[by], self.k.x_device(by))

    def hand(self, part, ref):
        return copy(ref, ref, self.c_s.at[part], self.c_r.at[part], self.k.sibling())

    def hand_second(self, ref):
        self.hand(1, ref).start()

    def start(self):
        for by in range(1, self.k.x_count):
            self.bx(by, 0).start()
        for way in BOTH:
            self.first.start(way, 0)
        for by in range(1, self.k.x_count):
            self.ax(0, by).start()

    def a_step(self, n):
        for way in BOTH:
            self.first.step(n, way, 0)
        for away in (-n, n) if n < self.steps else (n,):
            for by in range(1, self.k.x_count):
                self.ax(away, by).start()

    def b_start(self):
        for by in range(1, self.k.x_count):
            self.bx(by, -by).wait_recv()
        for chunk in range(2):
            for way in BOTH:
                self.second.start(way, chunk)
        self.hand(1, self.buf.at[self.core, 1, self.k.z]).start()

    def b_step(self, n, chunk):
        for way in BOTH:
            self.second.step(n, way, chunk)

    def a_swap(self):
        for by in range(self.k.x_count):
            if by:
                self.ax_all(by, -by).wait_recv()
            self.hand(0, self.buf.at[self.core, 0, :, mod(self.k.x - by, self.k.x_count)]).start()

    def wait(self, part):
        self.hand(part, self.buf.at[1 - self.core, part]).wait_recv()

    def finish(self):
        self.first.finish()
        self.second.finish()
        for by in range(1, self.k.x_count):
            self.ax_all(by, 0).wait_send()
            self.bx(by, 0).wait_send()
        for part in range(2):
            self.hand(part, self.buf.at[self.core, part]).wait_send()


class Qkv:
    def __init__(self, links, piece, buf, sems):
        self.k, self.buf, self.source = links, buf, piece
        self.load_s, self.x_s, self.x_r, self.z_s, self.z_r, e_s, e_r, l_s, l_r, self.c_s, self.c_r = sems
        self.zs, self.xs = buf.shape[2], buf.shape[3]
        self.early = early = self.zs * 3 // 4
        up = (links.y_count - 1) // 3
        reach = (up, links.y_count - 1 - up)
        half = self.xs // 2
        mine = lambda y, *rest: buf.at[(links.core, y, *rest)]
        self.first = Ring(links.y, links.y_count, links.y_device,
                          lambda y, c: mine(y, pl.ds(0, early), pl.ds(c * half, half)),
                          e_s, e_r, reach, 2, None, lambda ref: self.hand(0, ref).start())
        self.last = Ring(links.y, links.y_count, links.y_device, lambda y, c: mine(y, pl.ds(early, self.zs - early)),
                         l_s, l_r, reach, 1, None, lambda ref: self.hand(1, ref).start())
        self.sends = lax.rem(links.z, 2) == links.core
        self.zz = lax.div(links.z, 2)

    def load(self):
        return pltpu.make_async_copy(self.source, self.buf.at[self.k.core, self.k.y, self.zz, self.k.x], self.load_s.at[0])

    def preload(self):
        pl.when(self.sends)(lambda: self.load().start())

    def z_copy(self, by):
        ref = self.buf.at[self.k.core, self.k.y, self.zz, self.k.x]
        return copy(ref, ref, self.z_s.at[0], self.z_r.at[0], self.k.z_device(by))

    def x_copy(self, by):
        ref = self.buf.at[self.k.core, self.k.y, :, self.k.x]
        return copy(ref, ref, self.x_s.at[0], self.x_r.at[0], self.k.x_device(by))

    def x_all(self):
        ref = self.buf.at[self.k.core, self.k.y, :, pl.ds(0, self.xs - 1)]
        return copy(ref, ref, self.x_s.at[0], self.x_r.at[0], self.k.x_device(1))

    def start(self):
        @pl.when(self.sends)
        def _():
            self.load().wait()
            for by in range(1, self.k.z_count):
                self.z_copy(by).start()

    def across(self):
        def got(count):
            ref = self.buf.at[self.k.core, self.k.y, pl.ds(0, count), self.k.x]
            copy(ref, ref, self.z_s.at[0], self.z_r.at[0], self.k.z_device(1)).wait_recv()

        pl.when(self.sends)(lambda: got(self.zs - 1))
        pl.when(jnp.logical_not(self.sends))(lambda: got(self.zs))
        for by in range(1, self.xs):
            self.x_copy(by).start()

    def collect(self):
        self.x_all().wait_recv()
        for chunk in range(2):
            self.first.start(1, chunk)
        for part in range(2):
            self.hand(part, self.part_of(part, self.k.core, self.k.y)).start()

    def up(self):
        for chunk in range(2):
            self.first.start(0, chunk)

    def rest(self):
        for way in BOTH:
            self.last.start(way, 0)

    def hand(self, part, ref):
        return copy(ref, ref, self.c_s.at[part], self.c_r.at[part], self.k.sibling())

    def part_of(self, part, core, y):
        zs = pl.ds(0, self.early) if part == 0 else pl.ds(self.early, self.zs - self.early)
        return self.buf.at[core, y, zs]

    def all_of(self, part, core):
        return self.hand(part, self.part_of(part, core, slice(None)))

    def wait(self, part):
        self.all_of(part, 1 - self.k.core).wait_recv()

    def finish(self):
        self.first.finish()
        self.last.finish()
        for part in range(2):
            self.all_of(part, self.k.core).wait_send()

        self.x_all().wait_send()

        @pl.when(self.sends)
        def _():
            ref = self.buf.at[self.k.core, pl.ds(0, self.k.z_count - 1), 0, self.k.x]
            copy(ref, ref, self.z_s.at[0], self.z_r.at[0], self.k.z_device(1)).wait_send()


def kernel(
    z_count, tm_count,
    features, gain, conv, proj, attn_gain, qkv, out_weight, out,
    feat, halo, conv_in, out_in, x_sums, z_sums, slab_sums, token_x, token_z,
    proj_all, qkv_all, act_hi, act_lo, residual, band_hi, band_lo, tokens, keys, queries, q_hi, q_lo, total, top, mass,
    partial, lse_mine, parts, lse_parts,
    load_s, halo_s, halo_r, sum_s, sum_r, *sems,
):
    proj_sems, qkv_sems, sems = sems[:10], sems[10:21], sems[21:]
    key_s, key_r, query_s, query_r, part_s, part_r, lse_s, lse_r = sems
    k = Links(z_count, X, tm_count)
    rows_count = z_count * X
    tm, z, x = k.tm, k.z, k.x
    frames, height, columns, channels = features.shape
    half_w = columns // 2
    count = (height // 2) * half_w
    width = tokens.shape[1]
    wide = proj_all.shape[5]
    per_half, narrow = qkv_all.shape[4:]
    steps = z_count // 2
    plan = Plan()

    loads = [
        pltpu.make_async_copy(features.at[:, :, :, pl.ds(128 * half, 128)], feat.at[half], load_s.at[half])
        for half in range(2)
    ]
    for load in loads:
        load.start()
    barrier = pltpu.get_barrier_semaphore()
    peers = (
        [k.x_device(by) for by in range(1, X)] + [k.z_device(by) for by in range(1, z_count)]
        + [k.y_device(by) for by in range(1, k.y_count)] + [k.sibling(), {"tm": mod(tm - 1 + 2 * k.core, tm_count)}]
    )
    for peer in peers:
        pl.semaphore_signal(barrier, inc=1, device_id=peer, device_id_type=pl.DeviceIdType.MESH)

    quarters = [
        pltpu.make_async_copy(
            proj.at[:, pl.ds(pl.multiple_of((2 * k.core + part) * wide, wide), wide)],
            proj_all.at[k.core, part, z, x], load_s.at[2 + part],
        )
        for part in range(2)
    ]
    piece = qkv.at[
        pl.ds(pl.multiple_of(lax.div(k.y, 4) * per_half, 8), per_half),
        pl.ds(pl.multiple_of(lax.rem(k.y, 4) * narrow, narrow), narrow),
    ]
    proj_w = Proj(k, proj_all, proj_sems)
    qkv_w = Qkv(k, piece, qkv_all, qkv_sems)
    for one in quarters:
        one.start()
    qkv_w.preload()
    weight_loads = [
        pltpu.make_async_copy(conv, conv_in, load_s.at[4]), pltpu.make_async_copy(out_weight, out_in, load_s.at[5])
    ]
    for one in weight_loads:
        one.start()

    lane = iota((8, 128), 1)
    row = iota((8, 128), 0)
    sums = []
    for load in loads:
        load.wait()
    for frame in range(frames):
        values = jnp.concatenate([feat[half, frame].reshape(height * columns, 128) for half in range(2)], axis=1)
        sums += [jnp.sum(values, axis=0, keepdims=True), jnp.sum(values * values, axis=0, keepdims=True)]
    stacked = jnp.concatenate(sums + [jnp.zeros((4, channels), f32)], axis=0)
    per_group = channels // GROUPS
    fold = (iota((channels, 128), 1) % GROUPS == iota((channels, 128), 0) // per_group).astype(f32)

    def lanes_of(rows_of_sums, table):
        return jnp.sum(jnp.where(lane // GROUPS == row, exact(rows_of_sums, table), 0.0), axis=0, keepdims=True)

    x_sums[x] = lanes_of(stacked, fold)
    for one in quarters:
        one.wait()

    def exchange(slots, index, per, size, device, n):
        return Sums(slots, index, per, size, device, sum_s.at[n], sum_r.at[n])

    over_x = exchange(x_sums, x, 1, X, k.x_device, 0)
    over_z = exchange(z_sums, z, 1, z_count, k.z_device, 1)
    over_y = exchange(slab_sums, k.y, 2, k.y_count, k.y_device, 2)
    tokens_x = exchange(token_x, x, 1, X, k.x_device, 3)
    tokens_z = exchange(token_z, z, 1, z_count, k.z_device, 4)

    def slab_copy(at):
        return copy(slab_sums.at[at], slab_sums.at[at], sum_s.at[5], sum_r.at[5], k.sibling())

    pl.semaphore_wait(barrier, len(peers))
    over_x.start()
    proj_w.start()
    halo_copies = [
        copy(feat.at[:, f], halo.at[:, f], halo_s.at[f], halo_r.at[f], {"tm": mod(tm + 1, tm_count)}) for f in range(frames)
    ]
    for one in halo_copies:
        one.start()
    qkv_w.start()
    plan.now = 6.0

    def summed_x():
        over_x.wait()
        z_sums[z] = jnp.sum(x_sums[...], axis=0)
        over_z.start()

    def summed_z():
        over_z.wait()
        slab_sums[tm] = jnp.sum(z_sums[...], axis=0)
        slab_copy(tm).start()

    def summed_core():
        slab_copy(tm + 1 - 2 * k.core).wait_recv()
        over_y.start()

    plan.expect(7.5, "x", summed_x)
    plan.expect(9.2, "qkv x", qkv_w.across)
    plan.expect(8.5, "b", proj_w.b_start)
    for n in range(1, steps + 1):
        plan.expect(6.0 + 2.2 * n, "a", functools.partial(proj_w.a_step, n))
        for chunk in range(2):
            plan.expect(9.0 + 1.9 * (2 * n - 1 + chunk), "b", functools.partial(proj_w.b_step, n, chunk))
    plan.expect(9.8, "z", summed_z)
    plan.expect(11.5, "core", summed_core)
    plan.expect(11.8, "collect", qkv_w.collect)
    plan.expect(14.5, "y", over_y.wait)
    for frame in range(frames):
        plan.expect(19.0 + 0.1 * frame, "halo", halo_copies[frame].wait_recv)
    plan.expect(19.2, "up", qkv_w.up)
    qkv_done = 14.5
    for step, way, chunk in qkv_w.first.each():
        time = (13.5 if way else 20.0) + 1.8 * (2 * step - 1 + chunk)
        qkv_done = max(qkv_done, time)
        plan.expect(time, "qkv", functools.partial(qkv_w.first.step, step, way, chunk))
    plan.expect(qkv_done + 0.1, "rest", qkv_w.rest)
    plan.expect(qkv_done + 1.0, "qkv", functools.partial(qkv_w.wait, 0))
    for step, way, chunk in qkv_w.last.each():
        plan.expect(qkv_done + 4.0 + 2.5 * step, "qkv last", functools.partial(qkv_w.last.step, step, way, chunk))
    plan.expect(qkv_done + 6.0 + 2.5 * max(qkv_w.last.reach), "qkv last", functools.partial(qkv_w.wait, 1))

    def split_taps():
        weight_loads[0].wait()
        return [split(conv_in[lag]) for lag in range(3)]

    taps = plan.run(0.4, split_taps)

    def statistics():
        everything = slab_sums[...]
        slab = iota(everything.shape, 0)
        earlier = jnp.sum(jnp.where(slab < tm - 1, everything, 0.0), axis=0)
        previous = jnp.sum(jnp.where(slab == tm - 1, everything, 0.0), axis=0)
        own = jnp.sum(jnp.where(slab == tm, everything, 0.0), axis=0)
        kind, upto = row % 2, row // 2
        lane_kind, lane_frame = lane // GROUPS % 2, lane // GROUPS // 2
        mine = lane_kind == kind
        running = (
            jnp.where(mine, earlier, 0.0)
            + jnp.where(mine & (lane_frame <= upto), previous, 0.0)
            + jnp.where(mine & (lane_frame <= upto - 2), own, 0.0)
        )
        unfold = (iota((128, channels), 0) % GROUPS == iota((128, channels), 1) // per_group).astype(f32)
        running = exact(running, unfold)
        means, scales = [], []
        for i in range(4):
            position = jnp.maximum(tm * frames + i - 1, 1).astype(f32)
            cells = position * float(rows_count * height * columns * per_group)
            mean = running[2 * i : 2 * i + 1] / cells
            variance = running[2 * i + 1 : 2 * i + 2] / cells - mean * mean
            means.append(mean)
            scales.append(rsqrt(variance))
        return means, scales

    means, scales = plan.run(0.6, statistics, "y")
    norm_gain = gain[...]

    def cells_of(src, frame, b, c):
        return jnp.concatenate([
            jnp.concatenate([src[half, frame, 2 * h + b, pl.ds(c, half_w, stride=2), :] for half in range(2)], axis=1)
            for h in range(height // 2)
        ], axis=0)

    def activate(src, frame, at):
        for b in range(2):
            for c in range(2):
                value = (cells_of(src, frame, b, c) - means[at]) * scales[at] * norm_gain
                value = value / (1.0 + jnp.exp(-value))
                if at < 2:
                    value = jnp.where(tm > 0, value, 0.0)
                high, low = split(value)
                place = pl.ds((2 * b + c) * count, count)
                act_hi[at, place] = high
                act_lo[at, place] = low

    def activated(at):
        return act_hi[at], act_lo[at]

    def convolve(frame, terms, first=False):
        value = functools.reduce(jnp.add, [dot3(activated(at), taps[lag]) for at, lag in terms])
        residual[frame] = value if first else residual[frame] + value

    plan.run(0.7, lambda: activate(feat, 0, 2))
    plan.run(0.7, lambda: activate(feat, 1, 3))
    plan.run(0.5, lambda: convolve(0, [(2, 0)], True))
    plan.run(1.0, lambda: convolve(1, [(3, 0), (2, 1)], True))
    plan.run(0.7, lambda: activate(halo, 0, 0), "halo")
    plan.run(0.7, lambda: activate(halo, 1, 1))
    plan.run(1.0, lambda: convolve(0, [(1, 1), (0, 2)]))
    plan.run(0.5, lambda: convolve(1, [(1, 2)]))

    def haar():
        bands = [
            residual[a, pl.ds((2 * b + c) * count, count)] + cells_of(feat, a, b, c)
            for a in range(2) for b in range(2) for c in range(2)
        ]
        for bit in (4, 2, 1):
            bands = [
                bands[j] + bands[j | bit] if not j & bit else bands[j ^ bit] - bands[j] for j in range(8)
            ]
        bands = [split(band * (1.0 / math.sqrt(8.0))) for band in bands]
        per_quarter = wide // channels
        for quarter in range(4):
            ours = bands[quarter * per_quarter : (quarter + 1) * per_quarter]
            band_hi[quarter] = jnp.concatenate([band[0] for band in ours], axis=1)
            band_lo[quarter] = jnp.concatenate([band[1] for band in ours], axis=1)

    plan.run(0.7, haar)

    def quarter_of(half, part):
        at = 2 * half + part
        return dot3((band_hi[at], band_lo[at]), split(proj_all[half, part].reshape(width, wide)), NT)

    plan.need("a")
    plan.run(0.3, proj_w.a_swap)
    made = plan.run(0.7, lambda: quarter_of(k.core, 0))
    made = made + plan.run(0.7, lambda: quarter_of(k.core, 1), "b")
    proj_w.wait(0)
    made = made + plan.run(0.7, lambda: quarter_of(1 - k.core, 0))
    proj_w.wait(1)
    made = made + plan.run(0.7, lambda: quarter_of(1 - k.core, 1))
    tokens[...] = made
    keys[z] = made
    queries[x] = made

    part_rows = count // 2
    key_ring = Ring(z, z_count, k.z_device, lambda at, c: keys.at[at, pl.ds(c * part_rows, part_rows)],
                    key_s, key_r, (steps, steps), 2)
    query_ring = Ring(x, X, k.x_device, lambda at, c: queries.at[at], query_s, query_r, (X // 2, X // 2), 1,
                      lambda ref, way: ref.at[pl.ds(way * part_rows, part_rows)])
    for way in BOTH:
        query_ring.start(way, 0)
    for chunk in range(2):
        for way in BOTH:
            key_ring.start(way, chunk)
    begin = plan.now
    for step, way, chunk in key_ring.each():
        plan.expect(begin + 1.5 + 2.9 * (2 * step - 1 + chunk) - (2.9 * chunk if step == steps else 0.0), f"key{step}",
                    functools.partial(key_ring.step, step, way, chunk))
    for step, way, chunk in query_ring.each():
        plan.expect(begin + 4.4 * step + 3.0, "queries", functools.partial(query_ring.step, step, way, chunk))

    token_group = width // GROUPS
    sums = jnp.concatenate(
        [jnp.sum(made, axis=0, keepdims=True), jnp.sum(made * made, axis=0, keepdims=True), jnp.zeros((6, width), f32)],
        axis=0,
    )
    fold = (iota((width, 128), 1) % GROUPS == iota((width, 128), 0) // token_group).astype(f32)
    token_x[x] = lanes_of(sums, fold)
    tokens_x.start()

    def token_summed_x():
        tokens_x.wait()
        token_z[z] = jnp.sum(token_x[...], axis=0)
        tokens_z.start()

    plan.expect(begin + 2.5, "tokens x", token_summed_x)
    plan.expect(begin + 5.0, "tokens z", tokens_z.wait)

    def token_statistics():
        all_sums = jnp.sum(token_z[...], axis=0)
        unfold = (iota((128, width), 0) % GROUPS == iota((128, width), 1) // token_group).astype(f32)
        spread_sums = exact(jnp.where(lane // GROUPS == row, all_sums, 0.0), unfold)
        token_count = float(rows_count * count * token_group)
        mean = spread_sums[0:1] / token_count
        return mean, rsqrt(spread_sums[1:2] / token_count - mean * mean)

    token_mean, token_scale = plan.run(0.6, token_statistics, "tokens z")
    token_gain = attn_gain[...]

    def normed(value):
        return split((value - token_mean) * token_scale * token_gain)

    def columns_of(block):
        lanes = []
        for lane_at in range(4):
            chunks = []
            for at in range(block * width // per_half, (block + 1) * width // per_half + 1):
                owner, part = at // 2, at % 2
                if owner < rows_count:
                    own_z, own_x = owner // X, owner % X
                    chunks.append(qkv_all[own_z % 2, 4 * part + lane_at, own_z // 2, own_x])
            skip = block * width - block * width // per_half * per_half
            lanes.append(jnp.concatenate(chunks, axis=0)[skip : skip + width])
        return split(jnp.concatenate(lanes, axis=1))

    def query_key_weight():
        query_weight = tuple(jnp.transpose(part.astype(f32)).astype(bf16) for part in columns_of(0))
        return split(dot3(query_weight, columns_of(1)) * (1.0 / math.sqrt(float(width))))

    def ask():
        high, low = split(dot3(normed(queries[...].reshape(X * count, width)), query_key))
        q_hi[...], q_lo[...] = high.reshape(q_hi.shape), low.reshape(q_lo.shape)

    query_key = plan.run(2.0, query_key_weight, "qkv")
    plan.run(1.5, ask, "queries")

    sets = [(0, -1, 1)] + [(-step, step) for step in range(2, steps)] + [(steps,)]

    def key_block(at):
        return normed(jnp.concatenate([keys[mod(z + away, z_count)] for away in sets[at]], axis=0))

    def attend(step, at, block):
        rows_of = lambda ref: ref[at].reshape(-1, ref.shape[-1])
        scores = dot3((rows_of(q_hi), rows_of(q_lo)), block, NT)
        here = jnp.max(scores, axis=1, keepdims=True)
        if step == 0:
            new_top = here
            weights = jnp.exp(scores - new_top)
            new_mass = jnp.sum(weights, axis=1, keepdims=True)
            value = dot3(split(weights), block)
        else:
            new_top = jnp.maximum(rows_of(top), here)
            fade = jnp.exp(rows_of(top) - new_top)
            weights = jnp.exp(scores - new_top)
            new_mass = rows_of(mass) * fade + jnp.sum(weights, axis=1, keepdims=True)
            value = rows_of(total) * fade + dot3(split(weights), block)
        return new_top, new_mass, value

    def attend_all(step):
        for ref, value in zip((top, mass, total), attend(step, slice(None), key_block(step))):
            ref[...] = value.reshape(ref.shape)

    for step in range(len(sets) - 1):
        plan.run(3.0 if step == 0 else 2.2, lambda: attend_all(step), f"key{step + 1}")

    def part_copy(by, at):
        return copy(partial.at[mod(x + by, X)], parts.at[at], part_s.at[by], part_r.at[by], k.x_device(by))

    def lse_copy(by, at):
        return copy(lse_mine.at[mod(x + by, X)], lse_parts.at[at], lse_s.at[by], lse_r.at[by], k.x_device(by))

    plan.need(f"key{steps}")
    block = key_block(-1)
    for by in (2, 1, 3, 0):
        at = mod(x + by, X)
        last_top, last_mass, value = attend(steps, pl.ds(at, 1), block)
        partial[at] = value / last_mass
        lse_mine[at] = jnp.transpose(jnp.broadcast_to(last_top + jnp.log(last_mass), (count, 128)))[0:1]
        if by:
            lse_copy(by, x).start()
            part_copy(by, x).start()
        else:
            parts[x] = partial[x]
            lse_parts[x] = lse_mine[x]
    plan.now += 1.5

    def value_to_out():
        weight_loads[1].wait()
        value_weight = columns_of(2)
        value_weight = tuple(jnp.transpose(part.astype(f32)).astype(bf16) for part in value_weight)
        return split(dot3(value_weight, split(out_in[...])))

    value_out = plan.run(2.0, value_to_out, "qkv last")
    plan.upto(1e9)
    proj_w.finish()
    qkv_w.finish()
    for one in halo_copies:
        one.wait_send()
    for one in (over_x, over_z, over_y, tokens_x, tokens_z):
        one.finish()
    slab_copy(tm).wait_send()
    key_ring.finish()
    query_ring.finish()
    for by in range(1, X):
        lse_copy(by, mod(x - by, X)).wait_recv()
    for by in (1, 3, 2):
        part_copy(by, mod(x - by, X)).wait_recv()
    shares = [lse_parts[at] for at in range(X)]
    highest_lse = functools.reduce(jnp.maximum, shares)
    shares = [jnp.exp(share - highest_lse) for share in shares]
    whole = functools.reduce(jnp.add, shares)
    merged = jnp.zeros((count, width), f32)
    for at in range(X):
        share = jnp.transpose(jnp.broadcast_to(shares[at] / whole, (128, count)))
        merged = merged + parts[at] * jnp.concatenate([share] * (width // 128), axis=1)
    encoded = tokens[...] + dot3(split(merged), value_out)
    out[...] = encoded.reshape(out.shape)

    for by in range(1, X):
        part_copy(by, x).wait_send()
        lse_copy(by, x).wait_send()


def shards(z_count, tm_count, features, norm_gain, conv_weight, proj_weight, attn_gain, qkv_weight, out_weight):
    frames, height, columns, channels = features.shape
    width = out_weight.shape[0]
    half_h, half_w = height // 2, columns // 2
    count = half_h * half_w
    steps = z_count // 2
    rows_count = z_count * X
    proj_rows, qkv_rows = proj_weight.shape[1], qkv_weight.shape[1] // 2
    wide, narrow = proj_weight.shape[0] // 4, qkv_weight.shape[0] // 4
    y_count = tm_count // 2
    far = y_count - 1 - (y_count - 1) // 3
    vmem = pltpu.VMEM
    dma = pltpu.SemaphoreType.DMA
    proj_sems = [dma((2, steps)), dma((2, steps)), dma((X,)), dma((X,)), dma((X,)), dma((X,)), dma((4, steps)),
                 dma((4, steps)), dma((2,)), dma((2,))]
    qkv_sems = [dma((1,)), dma((1,)), dma((1,)), dma((1,)), dma((1,)), dma((4, far)), dma((4, far)), dma((2, far)),
                dma((2, far)), dma((2,)), dma((2,))]
    scratch = [
        vmem((2, frames, height, columns, 128), f32), vmem((2, frames, height, columns, 128), f32),
        vmem(conv_weight.shape, f32), vmem(out_weight.shape, f32),
        vmem((X, 1, 128), f32), vmem((z_count, 1, 128), f32), vmem((tm_count, 1, 128), f32),
        vmem((X, 1, 128), f32), vmem((z_count, 1, 128), f32),
        vmem((2, 2, z_count, X, proj_rows, wide), f32),
        vmem((2, y_count, z_count // 2, X, qkv_rows, narrow), f32),
        vmem((4, 4 * count, channels), bf16), vmem((4, 4 * count, channels), bf16),
        vmem((frames, 4 * count, channels), f32),
        vmem((4, count, wide), bf16), vmem((4, count, wide), bf16),
        vmem((count, width), f32),
        vmem((z_count, count, width), f32),
        vmem((X, count, width), f32),
        vmem((X, count, width), bf16), vmem((X, count, width), bf16),
        vmem((X, count, width), f32), vmem((X, count, 1), f32), vmem((X, count, 1), f32),
        vmem((X, count, width), f32), vmem((X, 1, 128), f32),
        vmem((X, count, width), f32), vmem((X, 1, 128), f32),
        dma((6,)), dma((frames,)), dma((frames,)), dma((6,)), dma((6,)),
        *proj_sems, *qkv_sems,
        dma((4, steps)), dma((4, steps)), dma((2, X // 2)), dma((2, X // 2)), dma((X,)), dma((X,)), dma((X,)), dma((X,)),
    ]
    whole = pl.BlockSpec(memory_space=vmem)
    anywhere = pl.BlockSpec(memory_space=pl.ANY)
    return pl.pallas_call(
        functools.partial(kernel, z_count, tm_count),
        out_shape=jax.ShapeDtypeStruct((frames // 2, half_h, half_w, width), f32),
        in_specs=[anywhere, whole, anywhere, anywhere, whole, anywhere, anywhere],
        out_specs=whole,
        scratch_shapes=scratch,
        compiler_params=pltpu.CompilerParams(collective_id=0, has_side_effects=True, vmem_limit_bytes=56 * 2**20),
    )(features, norm_gain[None], conv_weight, proj_weight.T, attn_gain[None], qkv_weight.T, out_weight)


def solution(mesh):
    in_specs = (P("tm", "rows", None, None), P(), P(), P(None, "rows"), P(), P(None, "rows"), P())
    out_specs = P("tm", "rows", None, None)
    body = functools.partial(shards, mesh.shape["rows"] // X, mesh.shape["tm"])
    return jax.shard_map(body, mesh=mesh, in_specs=in_specs, out_specs=out_specs, check_vma=False)
```

```python
import functools
import math

import jax
import jax.numpy as jnp
from jax import lax
from jax.experimental import pallas as pl
from jax.experimental.pallas import tpu as pltpu
from jax.sharding import PartitionSpec as P

GROUPS = 32
X = 4
epsilon = 1e-06
highest = lax.Precision.HIGHEST
f32, bf16 = jnp.float32, jnp.bfloat16
NN = (((1,), (0,)), ((), ()))
NT = (((1,), (1,)), ((), ()))
BOTH = (0, 1)


def split(value):
    high = value.astype(bf16)
    return high, (value - high.astype(f32)).astype(bf16)


def dot(a, b, dims):
    return lax.dot_general(a, b, dims, preferred_element_type=f32)


def dot3(a, b, dims=NN):
    rows = a[0].shape[0]
    if rows > 256:
        deep = (b[0], b[0], b[1])
        return dot(jnp.concatenate((a[0], a[1], a[0]), axis=1), jnp.concatenate(deep, axis=dims[0][1][0]), dims)
    by_high = dot(jnp.concatenate(a, axis=0), b[0], dims)
    return by_high[:rows] + (by_high[rows:] + dot(a[0], b[1], dims))


def exact(a, b):
    return lax.dot_general(a, b, NN, precision=highest, preferred_element_type=f32)


def iota(shape, axis):
    return lax.broadcasted_iota(jnp.int32, shape, axis)


def rsqrt(value):
    return lax.rsqrt(value + epsilon)


def mod(value, size):
    return lax.rem(value + size, size)


class Plan:
    def __init__(self):
        self.now, self.waits = 0.0, []

    def expect(self, time, name, action):
        self.waits.append((time, len(self.waits), name, action))

    def upto(self, time):
        while True:
            due = [wait for wait in self.waits if wait[0] <= time]
            if not due:
                return
            first = min(due, key=lambda wait: wait[:2])
            self.waits.remove(first)
            first[3]()

    def need(self, name):
        times = [wait[0] for wait in self.waits if wait[2] == name]
        if times:
            self.now = max(self.now, max(times))
            self.upto(max(times))

    def run(self, duration, action, *needs):
        for name in needs:
            self.need(name)
        self.upto(self.now)
        result = action()
        self.now += duration
        return result


class Links:
    def __init__(self, z_count, x_count, tm_count):
        self.rows, self.tm = lax.axis_index("rows"), lax.axis_index("tm")
        self.z, self.x = lax.div(self.rows, x_count), lax.rem(self.rows, x_count)
        self.y, self.core = lax.div(self.tm, 2), lax.rem(self.tm, 2)
        self.z_count, self.x_count, self.y_count = z_count, x_count, tm_count // 2

    def z_device(self, by):
        return {"rows": mod(self.z + by, self.z_count) * self.x_count + self.x}

    def x_device(self, by):
        return {"rows": self.z * self.x_count + mod(self.x + by, self.x_count)}

    def y_device(self, by):
        return {"tm": mod(self.y + by, self.y_count) * 2 + self.core}

    def sibling(self):
        return {"tm": self.tm + 1 - 2 * self.core}


def copy(src, dst, send, recv, device):
    return pltpu.make_async_remote_copy(
        src_ref=src, dst_ref=dst, send_sem=send, recv_sem=recv, device_id=device,
        device_id_type=pl.DeviceIdType.MESH,
    )


class Ring:
    def __init__(self, place, count, device, at, send, recv, reach, chunks=1, half=None, arrived=None):
        self.place, self.count, self.device, self.at, self.half = place, count, device, at, half
        self.send, self.recv, self.reach, self.chunks, self.arrived = send, recv, reach, chunks, arrived

    def moves(self, step, way, chunk):
        if step > self.reach[way]:
            return False
        shared = step == self.reach[0] == self.reach[1] and 2 * step == self.count
        return not shared or self.chunks == 1 or chunk == way

    def ref(self, away, step, way, chunk):
        ref = self.at(mod(self.place + away, self.count), chunk)
        return self.half(ref, way) if self.half and 2 * step == self.count else ref

    def copy(self, step, way, chunk, away):
        ref = self.ref(away, step, way, chunk)
        at = (way * self.chunks + chunk, step - 1)
        return copy(ref, ref, self.send.at[at], self.recv.at[at], self.device(1 if way == 0 else -1))

    def outgoing(self, step, way, chunk):
        return self.copy(step, way, chunk, 1 - step if way == 0 else step - 1)

    def start(self, way, chunk):
        self.outgoing(1, way, chunk).start()

    def step(self, step, way, chunk):
        if not self.moves(step, way, chunk):
            return
        away = -step if way == 0 else step
        self.copy(step, way, chunk, away).wait_recv()
        if self.moves(step + 1, way, chunk):
            self.outgoing(step + 1, way, chunk).start()
        if self.arrived:
            self.arrived(self.ref(away, step, way, chunk))

    def each(self):
        for step in range(1, max(self.reach) + 1):
            for chunk in range(self.chunks):
                for way in BOTH:
                    if self.moves(step, way, chunk):
                        yield step, way, chunk

    def finish(self):
        for step, way, chunk in self.each():
            self.outgoing(step, way, chunk).wait_send()


class Sums:
    def __init__(self, slots, index, per, size, device, send, recv):
        self.slots, self.index, self.per, self.size, self.device = slots, index, per, size, device
        self.send, self.recv = send, recv

    def copies(self, by):
        ref = self.slots.at[pl.ds(self.index * self.per, self.per)]
        return copy(ref, ref, self.send, self.recv, self.device(by))

    def everything(self):
        ref = self.slots.at[pl.ds(0, (self.size - 1) * self.per)]
        return copy(ref, ref, self.send, self.recv, self.device(1))

    def start(self):
        for by in range(1, self.size):
            self.copies(by).start()

    def wait(self):
        self.everything().wait_recv()

    def finish(self):
        self.everything().wait_send()


class Proj:
    def __init__(self, links, buf, sems):
        self.k, self.buf = links, buf
        az_s, az_r, self.ax_s, self.ax_r, self.bx_s, self.bx_r, bz_s, bz_r, self.c_s, self.c_r = sems
        self.core = links.core
        rows, xs, steps = buf.shape[4] // 2, links.x_count // 2, links.z_count // 2
        self.first = Ring(links.z, links.z_count, links.z_device, lambda z, chunk: buf.at[self.core, 0, z, links.x],
                          az_s, az_r, (steps, steps), 1, lambda ref, way: ref.at[pl.ds(way * rows, rows)])
        self.second = Ring(links.z, links.z_count, links.z_device,
                           lambda z, chunk: buf.at[self.core, 1, z, pl.ds(chunk * xs, xs)],
                           bz_s, bz_r, (steps, steps), 2, None, self.hand_second)
        self.steps = steps

    def block(self, away, x_away):
        return self.buf.at[self.core, 0, mod(self.k.z + away, self.k.z_count), mod(self.k.x + x_away, self.k.x_count)]

    def ax(self, kind, away, x_away):
        ref = self.block(away, x_away)
        up = self.goes_up(away) if kind == 2 else kind == 0
        at = (kind, away % self.k.z_count)
        return copy(ref, ref, self.ax_s.at[at], self.ax_r.at[at], self.k.x_device(1 if up else -1))

    def goes_up(self, away):
        return away % self.k.z_count < self.steps

    def a_out(self, away):
        for kind in range(2):
            self.ax(kind, away, 0).start()

    def a_on(self, away):
        for kind, x_away in enumerate((-1, 1)):
            self.ax(kind, away, x_away).wait_recv()
        self.ax(2, away, -1 if self.goes_up(away) else 1).start()

    def aways(self, n):
        return (0,) if n == 0 else (-n, n) if n < self.steps else (n,)

    def bx(self, by, away):
        ref = self.buf.at[self.core, 1, self.k.z, mod(self.k.x + away, self.k.x_count)]
        return copy(ref, ref, self.bx_s.at[by], self.bx_r.at[by], self.k.x_device(by))

    def hand(self, part, ref):
        return copy(ref, ref, self.c_s.at[part], self.c_r.at[part], self.k.sibling())

    def hand_second(self, ref):
        self.hand(1, ref).start()

    def start(self):
        for by in range(1, self.k.x_count):
            self.bx(by, 0).start()
        for way in BOTH:
            self.first.start(way, 0)
        self.a_out(0)

    def a_step(self, n):
        for way in BOTH:
            self.first.step(n, way, 0)
        for away in self.aways(n):
            self.a_out(away)

    def a_pass(self, n):
        for away in self.aways(n):
            self.a_on(away)

    def b_start(self):
        for by in range(1, self.k.x_count):
            self.bx(by, -by).wait_recv()
        for chunk in range(2):
            for way in BOTH:
                self.second.start(way, chunk)
        self.hand(1, self.buf.at[self.core, 1, self.k.z]).start()

    def b_step(self, n, chunk):
        for way in BOTH:
            self.second.step(n, way, chunk)

    def a_hand(self, by):
        self.hand(0, self.buf.at[self.core, 0, :, mod(self.k.x + by, self.k.x_count)]).start()

    def a_near(self):
        for by in (0, -1, 1):
            self.a_hand(by)

    def a_far(self):
        for away in range(self.k.z_count):
            self.ax(2, away, 2).wait_recv()
        self.a_hand(2)

    def wait(self, part):
        self.hand(part, self.buf.at[1 - self.core, part]).wait_recv()

    def finish(self):
        self.first.finish()
        self.second.finish()
        for by in range(1, self.k.x_count):
            self.bx(by, 0).wait_send()
        for away in range(self.k.z_count):
            for kind in range(3):
                self.ax(kind, away, 0).wait_send()
        for part in range(2):
            self.hand(part, self.buf.at[self.core, part]).wait_send()


class Qkv:
    def __init__(self, links, piece, buf, sems):
        self.k, self.buf, self.source = links, buf, piece
        self.load_s, self.x_s, self.x_r, self.z_s, self.z_r, e_s, e_r, l_s, l_r, self.c_s, self.c_r = sems
        self.zs, self.xs = buf.shape[2], buf.shape[3]
        self.early = early = self.zs * 3 // 4
        up = (links.y_count - 1) // 3
        reach = (up, links.y_count - 1 - up)
        half = self.xs // 2
        mine = lambda y, *rest: buf.at[(links.core, y, *rest)]
        self.first = Ring(links.y, links.y_count, links.y_device,
                          lambda y, c: mine(y, pl.ds(0, early), pl.ds(c * half, half)),
                          e_s, e_r, reach, 2, None, lambda ref: self.hand(0, ref).start())
        self.last = Ring(links.y, links.y_count, links.y_device, lambda y, c: mine(y, pl.ds(early, self.zs - early)),
                         l_s, l_r, reach, 1, None, lambda ref: self.hand(1, ref).start())
        self.sends = lax.rem(links.z, 2) == links.core
        self.zz = lax.div(links.z, 2)

    def load(self):
        return pltpu.make_async_copy(self.source, self.buf.at[self.k.core, self.k.y, self.zz, self.k.x], self.load_s.at[0])

    def preload(self):
        pl.when(self.sends)(lambda: self.load().start())

    def z_copy(self, by):
        ref = self.buf.at[self.k.core, self.k.y, self.zz, self.k.x]
        return copy(ref, ref, self.z_s.at[0], self.z_r.at[0], self.k.z_device(by))

    def x_copy(self, by):
        ref = self.buf.at[self.k.core, self.k.y, :, self.k.x]
        return copy(ref, ref, self.x_s.at[0], self.x_r.at[0], self.k.x_device(by))

    def x_all(self):
        ref = self.buf.at[self.k.core, self.k.y, :, pl.ds(0, self.xs - 1)]
        return copy(ref, ref, self.x_s.at[0], self.x_r.at[0], self.k.x_device(1))

    def start(self):
        @pl.when(self.sends)
        def _():
            self.load().wait()
            for by in range(1, self.k.z_count):
                self.z_copy(by).start()

    def across(self):
        def got(count):
            ref = self.buf.at[self.k.core, self.k.y, pl.ds(0, count), self.k.x]
            copy(ref, ref, self.z_s.at[0], self.z_r.at[0], self.k.z_device(1)).wait_recv()

        pl.when(self.sends)(lambda: got(self.zs - 1))
        pl.when(jnp.logical_not(self.sends))(lambda: got(self.zs))
        for by in range(1, self.xs):
            self.x_copy(by).start()

    def collect(self):
        self.x_all().wait_recv()
        for chunk in range(2):
            self.first.start(1, chunk)
        for part in range(2):
            self.hand(part, self.part_of(part, self.k.core, self.k.y)).start()

    def up(self):
        for chunk in range(2):
            self.first.start(0, chunk)

    def rest(self):
        for way in BOTH:
            self.last.start(way, 0)

    def hand(self, part, ref):
        return copy(ref, ref, self.c_s.at[part], self.c_r.at[part], self.k.sibling())

    def part_of(self, part, core, y):
        zs = pl.ds(0, self.early) if part == 0 else pl.ds(self.early, self.zs - self.early)
        return self.buf.at[core, y, zs]

    def all_of(self, part, core):
        return self.hand(part, self.part_of(part, core, slice(None)))

    def wait(self, part):
        self.all_of(part, 1 - self.k.core).wait_recv()

    def finish(self):
        self.first.finish()
        self.last.finish()
        for part in range(2):
            self.all_of(part, self.k.core).wait_send()

        self.x_all().wait_send()

        @pl.when(self.sends)
        def _():
            ref = self.buf.at[self.k.core, pl.ds(0, self.k.z_count - 1), 0, self.k.x]
            copy(ref, ref, self.z_s.at[0], self.z_r.at[0], self.k.z_device(1)).wait_send()


def kernel(
    z_count, tm_count,
    features, gain, conv, proj, attn_gain, qkv, out_weight, out,
    feat, halo, conv_in, out_in, x_sums, z_sums, slab_sums, token_x, token_z,
    proj_all, qkv_all, act_hi, act_lo, residual, band_hi, band_lo, tokens, keys, queries, q_hi, q_lo, total, top, mass,
    partial, lse_mine, relay, relay_lse, joint, joint_lse, parts, parts_lse,
    load_s, halo_s, halo_r, sum_s, sum_r, *sems,
):
    proj_sems, qkv_sems, sems = sems[:10], sems[10:21], sems[21:]
    key_s, key_r, query_s, query_r, part_s, part_r = sems
    k = Links(z_count, X, tm_count)
    rows_count = z_count * X
    tm, z, x = k.tm, k.z, k.x
    frames, height, columns, channels = features.shape
    half_w = columns // 2
    count = (height // 2) * half_w
    width = tokens.shape[1]
    wide = proj_all.shape[5]
    per_half, narrow = qkv_all.shape[4:]
    steps = z_count // 2
    plan = Plan()

    loads = [
        pltpu.make_async_copy(features.at[:, :, :, pl.ds(128 * half, 128)], feat.at[half], load_s.at[half])
        for half in range(2)
    ]
    for load in loads:
        load.start()
    barrier = pltpu.get_barrier_semaphore()
    peers = (
        [k.x_device(by) for by in range(1, X)] + [k.z_device(by) for by in range(1, z_count)]
        + [k.y_device(by) for by in range(1, k.y_count)] + [k.sibling(), {"tm": mod(tm - 1 + 2 * k.core, tm_count)}]
    )
    for peer in peers:
        pl.semaphore_signal(barrier, inc=1, device_id=peer, device_id_type=pl.DeviceIdType.MESH)

    quarters = [
        pltpu.make_async_copy(
            proj.at[:, pl.ds(pl.multiple_of((2 * k.core + part) * wide, wide), wide)],
            proj_all.at[k.core, part, z, x], load_s.at[2 + part],
        )
        for part in range(2)
    ]
    piece = qkv.at[
        pl.ds(pl.multiple_of(lax.div(k.y, 4) * per_half, 8), per_half),
        pl.ds(pl.multiple_of(lax.rem(k.y, 4) * narrow, narrow), narrow),
    ]
    proj_w = Proj(k, proj_all, proj_sems)
    qkv_w = Qkv(k, piece, qkv_all, qkv_sems)
    for one in quarters:
        one.start()
    qkv_w.preload()
    weight_loads = [
        pltpu.make_async_copy(conv, conv_in, load_s.at[4]), pltpu.make_async_copy(out_weight, out_in, load_s.at[5])
    ]
    for one in weight_loads:
        one.start()

    lane = iota((8, 128), 1)
    row = iota((8, 128), 0)
    sums = []
    for load in loads:
        load.wait()
    for frame in range(frames):
        values = jnp.concatenate([feat[half, frame].reshape(height * columns, 128) for half in range(2)], axis=1)
        sums += [jnp.sum(values, axis=0, keepdims=True), jnp.sum(values * values, axis=0, keepdims=True)]
    stacked = jnp.concatenate(sums + [jnp.zeros((4, channels), f32)], axis=0)
    per_group = channels // GROUPS
    fold = (iota((channels, 128), 1) % GROUPS == iota((channels, 128), 0) // per_group).astype(f32)

    def lanes_of(rows_of_sums, table):
        return jnp.sum(jnp.where(lane // GROUPS == row, exact(rows_of_sums, table), 0.0), axis=0, keepdims=True)

    x_sums[x] = lanes_of(stacked, fold)
    for one in quarters:
        one.wait()

    def exchange(slots, index, per, size, device, n):
        return Sums(slots, index, per, size, device, sum_s.at[n], sum_r.at[n])

    over_x = exchange(x_sums, x, 1, X, k.x_device, 0)
    over_z = exchange(z_sums, z, 1, z_count, k.z_device, 1)
    over_y = exchange(slab_sums, k.y, 2, k.y_count, k.y_device, 2)
    tokens_x = exchange(token_x, x, 1, X, k.x_device, 3)
    tokens_z = exchange(token_z, z, 1, z_count, k.z_device, 4)

    def slab_copy(at):
        return copy(slab_sums.at[at], slab_sums.at[at], sum_s.at[5], sum_r.at[5], k.sibling())

    pl.semaphore_wait(barrier, len(peers))
    over_x.start()
    pairs = height // 2

    def halo_copy(f, h):
        at = (slice(None), f, pl.ds(2 * h, 2))
        return copy(feat.at[at], halo.at[at], halo_s.at[f, h], halo_r.at[f, h], {"tm": mod(tm + 1, tm_count)})

    halo_copies = [halo_copy(f, h) for h in range(pairs) for f in range(frames)]
    for one in halo_copies:
        one.start()
    proj_w.start()
    qkv_w.start()
    plan.now = 6.0

    def summed_x():
        over_x.wait()
        z_sums[z] = jnp.sum(x_sums[...], axis=0)
        over_z.start()

    def summed_z():
        over_z.wait()
        slab_sums[tm] = jnp.sum(z_sums[...], axis=0)
        slab_copy(tm).start()

    def summed_core():
        slab_copy(tm + 1 - 2 * k.core).wait_recv()
        over_y.start()

    plan.expect(7.5, "x", summed_x)
    plan.expect(9.2, "qkv x", qkv_w.across)
    plan.expect(8.5, "b", proj_w.b_start)
    plan.expect(9.0, "a", functools.partial(proj_w.a_pass, 0))
    plan.expect(8.9 + 2.4 * steps, "a", proj_w.a_near)
    plan.expect(11.5 + 2.4 * steps, "a far", proj_w.a_far)
    for n in range(1, steps + 1):
        plan.expect(6.0 + 2.4 * n, "a", functools.partial(proj_w.a_step, n))
        plan.expect(8.8 + 2.4 * n, "a", functools.partial(proj_w.a_pass, n))
        for chunk in range(2):
            plan.expect(9.0 + 1.9 * (2 * n - 1 + chunk), "b", functools.partial(proj_w.b_step, n, chunk))
    plan.expect(9.8, "z", summed_z)
    plan.expect(11.5, "core", summed_core)
    plan.expect(11.8, "collect", qkv_w.collect)
    plan.expect(14.5, "y", over_y.wait)
    for h in range(pairs):
        for frame in range(frames):
            plan.expect(13.5 + 5.8 * h + 0.1 * frame, f"halo{h}", halo_copy(frame, h).wait_recv)
    plan.expect(19.2, "up", qkv_w.up)
    qkv_done = 14.5
    for step, way, chunk in qkv_w.first.each():
        time = (13.5 if way else 20.0) + 1.8 * (2 * step - 1 + chunk)
        qkv_done = max(qkv_done, time)
        plan.expect(time, "qkv", functools.partial(qkv_w.first.step, step, way, chunk))
    plan.expect(qkv_done + 0.1, "rest", qkv_w.rest)
    plan.expect(qkv_done + 1.0, "qkv", functools.partial(qkv_w.wait, 0))
    for step, way, chunk in qkv_w.last.each():
        plan.expect(qkv_done + 4.0 + 2.5 * step, "qkv last", functools.partial(qkv_w.last.step, step, way, chunk))
    plan.expect(qkv_done + 6.0 + 2.5 * max(qkv_w.last.reach), "qkv last", functools.partial(qkv_w.wait, 1))

    def split_taps():
        weight_loads[0].wait()
        return [split(conv_in[lag]) for lag in range(3)]

    taps = plan.run(0.4, split_taps)

    def statistics():
        everything = slab_sums[...]
        slab = iota(everything.shape, 0)
        earlier = jnp.sum(jnp.where(slab < tm - 1, everything, 0.0), axis=0)
        previous = jnp.sum(jnp.where(slab == tm - 1, everything, 0.0), axis=0)
        own = jnp.sum(jnp.where(slab == tm, everything, 0.0), axis=0)
        kind, upto = row % 2, row // 2
        lane_kind, lane_frame = lane // GROUPS % 2, lane // GROUPS // 2
        mine = lane_kind == kind
        running = (
            jnp.where(mine, earlier, 0.0)
            + jnp.where(mine & (lane_frame <= upto), previous, 0.0)
            + jnp.where(mine & (lane_frame <= upto - 2), own, 0.0)
        )
        unfold = (iota((128, channels), 0) % GROUPS == iota((128, channels), 1) // per_group).astype(f32)
        running = exact(running, unfold)
        means, scales = [], []
        for i in range(4):
            position = jnp.maximum(tm * frames + i - 1, 1).astype(f32)
            cells = position * float(rows_count * height * columns * per_group)
            mean = running[2 * i : 2 * i + 1] / cells
            variance = running[2 * i + 1 : 2 * i + 2] / cells - mean * mean
            means.append(mean)
            scales.append(rsqrt(variance))
        return means, scales

    means, scales = plan.run(0.6, statistics, "y")
    norm_gain = gain[...]

    def cells_of(src, frame, h, b, c):
        return jnp.concatenate([src[half, frame, 2 * h + b, pl.ds(c, half_w, stride=2), :] for half in range(2)], axis=1)

    def activate(src, frame, h, at):
        for b in range(2):
            for c in range(2):
                value = (cells_of(src, frame, h, b, c) - means[at]) * scales[at] * norm_gain
                value = value / (1.0 + jnp.exp(-value))
                if at < 2:
                    value = jnp.where(tm > 0, value, 0.0)
                high, low = split(value)
                place = pl.ds((2 * b + c) * half_w, half_w)
                act_hi[at, h, place] = high
                act_lo[at, h, place] = low

    def activated(at, h):
        return tuple(ref[at, h].reshape(-1, channels) for ref in (act_hi, act_lo))

    def convolve(frame, h, terms, first=False):
        value = functools.reduce(jnp.add, [dot3(activated(at, h), taps[lag]) for at, lag in terms])
        value = value.reshape((-1, 4 * half_w, channels))
        residual[frame, h] = value if first else residual[frame, h] + value

    every = pl.ds(0, pairs)
    for frame in range(frames):
        plan.run(0.7, lambda: [activate(feat, frame, h, 2 + frame) for h in range(pairs)])
    plan.run(0.5, lambda: convolve(0, every, [(2, 0)], True))
    plan.run(1.0, lambda: convolve(1, every, [(3, 0), (2, 1)], True))
    for h in range(pairs):
        for frame in range(frames):
            plan.run(0.35, lambda: activate(halo, frame, h, frame), f"halo{h}")
        plan.run(0.6, lambda: convolve(0, pl.ds(h, 1), [(1, 1), (0, 2)]))
        plan.run(0.3, lambda: convolve(1, pl.ds(h, 1), [(1, 2)]))

    def haar():
        bands = [
            jnp.concatenate([
                residual[a, h, pl.ds((2 * b + c) * half_w, half_w)] + cells_of(feat, a, h, b, c) for h in range(pairs)
            ], axis=0)
            for a in range(2) for b in range(2) for c in range(2)
        ]
        for bit in (4, 2, 1):
            bands = [
                bands[j] + bands[j | bit] if not j & bit else bands[j ^ bit] - bands[j] for j in range(8)
            ]
        bands = [split(band * (1.0 / math.sqrt(8.0))) for band in bands]
        per_quarter = wide // channels
        for quarter in range(4):
            ours = bands[quarter * per_quarter : (quarter + 1) * per_quarter]
            band_hi[quarter] = jnp.concatenate([band[0] for band in ours], axis=1)
            band_lo[quarter] = jnp.concatenate([band[1] for band in ours], axis=1)

    plan.run(0.7, haar)

    def quarter_of(half, part):
        at = 2 * half + part
        return dot3((band_hi[at], band_lo[at]), split(proj_all[half, part].reshape(width, wide)), NT)

    made = plan.run(0.7, lambda: quarter_of(k.core, 0), "a far")
    made = made + plan.run(0.7, lambda: quarter_of(k.core, 1), "b")
    proj_w.wait(0)
    made = made + plan.run(0.7, lambda: quarter_of(1 - k.core, 0))
    proj_w.wait(1)
    made = made + plan.run(0.7, lambda: quarter_of(1 - k.core, 1))
    tokens[...] = made
    keys[z] = made
    queries[x] = made

    part_rows = count // 2
    key_ring = Ring(z, z_count, k.z_device, lambda at, c: keys.at[at, pl.ds(c * part_rows, part_rows)],
                    key_s, key_r, (steps, steps), 2)
    query_ring = Ring(x, X, k.x_device, lambda at, c: queries.at[at], query_s, query_r, (X // 2, X // 2), 1,
                      lambda ref, way: ref.at[pl.ds(way * part_rows, part_rows)])
    for way in BOTH:
        query_ring.start(way, 0)
    for chunk in range(2):
        for way in BOTH:
            key_ring.start(way, chunk)
    begin = plan.now
    for step, way, chunk in key_ring.each():
        plan.expect(begin + 1.5 + 2.9 * (2 * step - 1 + chunk) - (2.9 * chunk if step == steps else 0.0), f"key{step}",
                    functools.partial(key_ring.step, step, way, chunk))
    for step, way, chunk in query_ring.each():
        plan.expect(begin + 4.4 * step + 3.0, "queries", functools.partial(query_ring.step, step, way, chunk))

    token_group = width // GROUPS
    sums = jnp.concatenate(
        [jnp.sum(made, axis=0, keepdims=True), jnp.sum(made * made, axis=0, keepdims=True), jnp.zeros((6, width), f32)],
        axis=0,
    )
    fold = (iota((width, 128), 1) % GROUPS == iota((width, 128), 0) // token_group).astype(f32)
    token_x[x] = lanes_of(sums, fold)
    tokens_x.start()

    def token_summed_x():
        tokens_x.wait()
        token_z[z] = jnp.sum(token_x[...], axis=0)
        tokens_z.start()

    plan.expect(begin + 2.5, "tokens x", token_summed_x)
    plan.expect(begin + 5.0, "tokens z", tokens_z.wait)

    def token_statistics():
        all_sums = jnp.sum(token_z[...], axis=0)
        unfold = (iota((128, width), 0) % GROUPS == iota((128, width), 1) // token_group).astype(f32)
        spread_sums = exact(jnp.where(lane // GROUPS == row, all_sums, 0.0), unfold)
        token_count = float(rows_count * count * token_group)
        mean = spread_sums[0:1] / token_count
        return mean, rsqrt(spread_sums[1:2] / token_count - mean * mean)

    token_mean, token_scale = plan.run(0.6, token_statistics, "tokens z")
    token_gain = attn_gain[...]

    def normed(value):
        return split((value - token_mean) * token_scale * token_gain)

    def columns_of(block):
        lanes = []
        for lane_at in range(4):
            chunks = []
            for at in range(block * width // per_half, (block + 1) * width // per_half + 1):
                owner, part = at // 2, at % 2
                if owner < rows_count:
                    own_z, own_x = owner // X, owner % X
                    chunks.append(qkv_all[own_z % 2, 4 * part + lane_at, own_z // 2, own_x])
            skip = block * width - block * width // per_half * per_half
            lanes.append(jnp.concatenate(chunks, axis=0)[skip : skip + width])
        return split(jnp.concatenate(lanes, axis=1))

    def query_key_weight():
        query_weight = tuple(jnp.transpose(part.astype(f32)).astype(bf16) for part in columns_of(0))
        return split(dot3(query_weight, columns_of(1)) * (1.0 / math.sqrt(float(width))))

    def ask():
        high, low = split(dot3(normed(queries[...].reshape(X * count, width)), query_key))
        q_hi[...], q_lo[...] = high.reshape(q_hi.shape), low.reshape(q_lo.shape)

    query_key = plan.run(2.0, query_key_weight, "qkv")
    plan.run(1.5, ask, "queries")

    sets = [(0, -1, 1)] + [(-step, step) for step in range(2, steps)] + [(steps,)]

    def key_block(at):
        return normed(jnp.concatenate([keys[mod(z + away, z_count)] for away in sets[at]], axis=0))

    def attend(step, at, block):
        rows_of = lambda ref: ref[at].reshape(-1, ref.shape[-1])
        scores = dot3((rows_of(q_hi), rows_of(q_lo)), block, NT)
        here = jnp.max(scores, axis=1, keepdims=True)
        if step == 0:
            new_top = here
            weights = jnp.exp(scores - new_top)
            new_mass = jnp.sum(weights, axis=1, keepdims=True)
            value = dot3(split(weights), block)
        else:
            new_top = jnp.maximum(rows_of(top), here)
            fade = jnp.exp(rows_of(top) - new_top)
            weights = jnp.exp(scores - new_top)
            new_mass = rows_of(mass) * fade + jnp.sum(weights, axis=1, keepdims=True)
            value = rows_of(total) * fade + dot3(split(weights), block)
        return new_top, new_mass, value

    def attend_all(step):
        for ref, value in zip((top, mass, total), attend(step, slice(None), key_block(step))):
            ref[...] = value.reshape(ref.shape)

    for step in range(len(sets) - 1):
        plan.run(3.0 if step == 0 else 2.2, lambda: attend_all(step), f"key{step + 1}")

    half_rows = [pl.ds(way * part_rows, part_rows) for way in BOTH]
    toward = (1, -1)

    def send(kind, way, src, dst):
        return copy(src, dst, part_s.at[kind, way], part_r.at[kind, way], k.x_device(toward[way]))

    def opposite(way):
        at = mod(x + 2, X)
        return (send(0, way, partial.at[at, half_rows[way]], relay.at[way]),
                send(1, way, lse_mine.at[at], relay_lse.at[way]))

    def plain(way):
        return (send(2, way, partial.at[mod(x + toward[way], X), half_rows[1 - way]], parts.at[way, half_rows[1 - way]]),)

    def joined(way):
        return (send(3, way, joint.at[way], parts.at[way, half_rows[way]]), send(4, way, joint_lse.at[way], parts_lse.at[way]))

    def as_column(lanes):
        return jnp.transpose(jnp.broadcast_to(lanes, (count, 128)))

    def across(column):
        return jnp.concatenate([column] * (width // 128), axis=1)

    plan.need(f"key{steps}")
    block = key_block(-1)
    for by in (2, 1, 3, 0):
        at = mod(x + by, X)
        last_top, last_mass, value = attend(steps, pl.ds(at, 1), block)
        partial[at] = value / last_mass
        lse_mine[at] = jnp.transpose(jnp.broadcast_to(last_top + jnp.log(last_mass), (count, 128)))[0:1]
        if by == 2:
            for one in (*opposite(0), *opposite(1)):
                one.start()
        elif by:
            plain(0 if by == 1 else 1)[0].start()
    plan.now += 1.5

    def value_to_out():
        weight_loads[1].wait()
        value_weight = columns_of(2)
        value_weight = tuple(jnp.transpose(part.astype(f32)).astype(bf16) for part in value_weight)
        return split(dot3(value_weight, split(out_in[...])))

    value_out = plan.run(2.0, value_to_out, "qkv last")
    plan.upto(1e9)
    lane_row = iota((1, 128), 1)
    for way in BOTH:
        for one in opposite(way):
            one.wait_recv()
        at = mod(x + toward[way], X)
        own, theirs = lse_mine[at], relay_lse[way]
        both = jnp.maximum(own, theirs)
        both = both + jnp.log(jnp.exp(own - both) + jnp.exp(theirs - both))
        rows_of_way = slice(way * part_rows, (way + 1) * part_rows)
        joint[way] = (
            partial[at, half_rows[way]] * across(as_column(jnp.exp(own - both))[rows_of_way])
            + relay[way] * across(as_column(jnp.exp(theirs - both))[rows_of_way])
        )
        joint_lse[way] = jnp.where(lane_row // part_rows == way, both, own)
        for one in joined(way):
            one.start()

    proj_w.finish()
    qkv_w.finish()
    for one in halo_copies:
        one.wait_send()
    for one in (over_x, over_z, over_y, tokens_x, tokens_z):
        one.finish()
    slab_copy(tm).wait_send()
    key_ring.finish()
    query_ring.finish()
    for way in BOTH:
        for one in (*plain(way), *joined(way)):
            one.wait_recv()
    given = [(lse_mine[x], partial[x])] + [(parts_lse[way], parts[way]) for way in BOTH]
    highest_lse = functools.reduce(jnp.maximum, [lse for lse, _ in given])
    shares = [jnp.exp(lse - highest_lse) for lse, _ in given]
    whole = functools.reduce(jnp.add, shares)
    merged = jnp.zeros((count, width), f32)
    for share, (_, value) in zip(shares, given):
        merged = merged + value * across(as_column(share / whole))
    encoded = tokens[...] + dot3(split(merged), value_out)
    out[...] = encoded.reshape(out.shape)

    for way in BOTH:
        for one in (*opposite(way), *plain(way), *joined(way)):
            one.wait_send()


def shards(z_count, tm_count, features, norm_gain, conv_weight, proj_weight, attn_gain, qkv_weight, out_weight):
    frames, height, columns, channels = features.shape
    width = out_weight.shape[0]
    half_h, half_w = height // 2, columns // 2
    count = half_h * half_w
    steps = z_count // 2
    rows_count = z_count * X
    proj_rows, qkv_rows = proj_weight.shape[1], qkv_weight.shape[1] // 2
    wide, narrow = proj_weight.shape[0] // 4, qkv_weight.shape[0] // 4
    y_count = tm_count // 2
    far = y_count - 1 - (y_count - 1) // 3
    vmem = pltpu.VMEM
    dma = pltpu.SemaphoreType.DMA
    proj_sems = [dma((2, steps)), dma((2, steps)), dma((3, z_count)), dma((3, z_count)), dma((X,)), dma((X,)), dma((4, steps)),
                 dma((4, steps)), dma((2,)), dma((2,))]
    qkv_sems = [dma((1,)), dma((1,)), dma((1,)), dma((1,)), dma((1,)), dma((4, far)), dma((4, far)), dma((2, far)),
                dma((2, far)), dma((2,)), dma((2,))]
    scratch = [
        vmem((2, frames, height, columns, 128), f32), vmem((2, frames, height, columns, 128), f32),
        vmem(conv_weight.shape, f32), vmem(out_weight.shape, f32),
        vmem((X, 1, 128), f32), vmem((z_count, 1, 128), f32), vmem((tm_count, 1, 128), f32),
        vmem((X, 1, 128), f32), vmem((z_count, 1, 128), f32),
        vmem((2, 2, z_count, X, proj_rows, wide), f32),
        vmem((2, y_count, z_count // 2, X, qkv_rows, narrow), f32),
        vmem((4, half_h, 4 * half_w, channels), bf16), vmem((4, half_h, 4 * half_w, channels), bf16),
        vmem((frames, half_h, 4 * half_w, channels), f32),
        vmem((4, count, wide), bf16), vmem((4, count, wide), bf16),
        vmem((count, width), f32),
        vmem((z_count, count, width), f32),
        vmem((X, count, width), f32),
        vmem((X, count, width), bf16), vmem((X, count, width), bf16),
        vmem((X, count, width), f32), vmem((X, count, 1), f32), vmem((X, count, 1), f32),
        vmem((X, count, width), f32), vmem((X, 1, 128), f32),
        vmem((2, count // 2, width), f32), vmem((2, 1, 128), f32),
        vmem((2, count // 2, width), f32), vmem((2, 1, 128), f32),
        vmem((2, count, width), f32), vmem((2, 1, 128), f32),
        dma((6,)), dma((frames, half_h)), dma((frames, half_h)), dma((6,)), dma((6,)),
        *proj_sems, *qkv_sems,
        dma((4, steps)), dma((4, steps)), dma((2, X // 2)), dma((2, X // 2)), dma((5, 2)), dma((5, 2)),
    ]
    whole = pl.BlockSpec(memory_space=vmem)
    anywhere = pl.BlockSpec(memory_space=pl.ANY)
    return pl.pallas_call(
        functools.partial(kernel, z_count, tm_count),
        out_shape=jax.ShapeDtypeStruct((frames // 2, half_h, half_w, width), f32),
        in_specs=[anywhere, whole, anywhere, anywhere, whole, anywhere, anywhere],
        out_specs=whole,
        scratch_shapes=scratch,
        compiler_params=pltpu.CompilerParams(collective_id=0, has_side_effects=True, vmem_limit_bytes=56 * 2**20),
    )(features, norm_gain[None], conv_weight, proj_weight.T, attn_gain[None], qkv_weight.T, out_weight)


def solution(mesh):
    in_specs = (P("tm", "rows", None, None), P(), P(), P(None, "rows"), P(), P(None, "rows"), P())
    out_specs = P("tm", "rows", None, None)
    body = functools.partial(shards, mesh.shape["rows"] // X, mesh.shape["tm"])
    return jax.shard_map(body, mesh=mesh, in_specs=in_specs, out_specs=out_specs, check_vma=False)
```

```python
import functools
import math

import jax
import jax.numpy as jnp
from jax import lax
from jax.experimental import pallas as pl
from jax.experimental.pallas import tpu as pltpu
from jax.sharding import PartitionSpec as P

GROUPS = 32
X = 4
epsilon = 1e-06
highest = lax.Precision.HIGHEST
f32, bf16 = jnp.float32, jnp.bfloat16
NN = (((1,), (0,)), ((), ()))
NT = (((1,), (1,)), ((), ()))
BOTH = (0, 1)


def split(value):
    high = value.astype(bf16)
    return high, (value - high.astype(f32)).astype(bf16)


def dot(a, b, dims):
    return lax.dot_general(a, b, dims, preferred_element_type=f32)


def dot3(a, b, dims=NN):
    rows = a[0].shape[0]
    if rows > 256:
        deep = (b[0], b[0], b[1])
        return dot(jnp.concatenate((a[0], a[1], a[0]), axis=1), jnp.concatenate(deep, axis=dims[0][1][0]), dims)
    by_high = dot(jnp.concatenate(a, axis=0), b[0], dims)
    return by_high[:rows] + (by_high[rows:] + dot(a[0], b[1], dims))


def exact(a, b):
    return lax.dot_general(a, b, NN, precision=highest, preferred_element_type=f32)


def iota(shape, axis):
    return lax.broadcasted_iota(jnp.int32, shape, axis)


def rsqrt(value):
    return lax.rsqrt(value + epsilon)


def mod(value, size):
    return lax.rem(value + size, size)


class Plan:
    def __init__(self):
        self.now, self.waits = 0.0, []

    def expect(self, time, name, action):
        self.waits.append((time, len(self.waits), name, action))

    def upto(self, time):
        while True:
            due = [wait for wait in self.waits if wait[0] <= time]
            if not due:
                return
            first = min(due, key=lambda wait: wait[:2])
            self.waits.remove(first)
            first[3]()

    def need(self, name):
        times = [wait[0] for wait in self.waits if wait[2] == name]
        if times:
            self.now = max(self.now, max(times))
            self.upto(max(times))

    def run(self, duration, action, *needs):
        for name in needs:
            self.need(name)
        self.upto(self.now)
        result = action()
        self.now += duration
        return result


class Links:
    def __init__(self, z_count, x_count, tm_count):
        self.rows, self.tm = lax.axis_index("rows"), lax.axis_index("tm")
        self.z, self.x = lax.div(self.rows, x_count), lax.rem(self.rows, x_count)
        self.y, self.core = lax.div(self.tm, 2), lax.rem(self.tm, 2)
        self.z_count, self.x_count, self.y_count = z_count, x_count, tm_count // 2

    def z_device(self, by):
        return {"rows": mod(self.z + by, self.z_count) * self.x_count + self.x}

    def x_device(self, by):
        return {"rows": self.z * self.x_count + mod(self.x + by, self.x_count)}

    def y_device(self, by):
        return {"tm": mod(self.y + by, self.y_count) * 2 + self.core}

    def sibling(self):
        return {"tm": self.tm + 1 - 2 * self.core}


def copy(src, dst, send, recv, device):
    return pltpu.make_async_remote_copy(
        src_ref=src, dst_ref=dst, send_sem=send, recv_sem=recv, device_id=device,
        device_id_type=pl.DeviceIdType.MESH,
    )


class Ring:
    def __init__(self, place, count, device, at, send, recv, reach, chunks=1, half=None, arrived=None):
        self.place, self.count, self.device, self.at, self.half = place, count, device, at, half
        self.send, self.recv, self.reach, self.chunks, self.arrived = send, recv, reach, chunks, arrived

    def moves(self, step, way, chunk):
        if step > self.reach[way]:
            return False
        shared = step == self.reach[0] == self.reach[1] and 2 * step == self.count
        return not shared or self.chunks == 1 or chunk // (self.chunks // 2) == way

    def ref(self, away, step, way, chunk):
        ref = self.at(mod(self.place + away, self.count), chunk)
        return self.half(ref, way) if self.half and 2 * step == self.count else ref

    def copy(self, step, way, chunk, away):
        ref = self.ref(away, step, way, chunk)
        at = (way * self.chunks + chunk, step - 1)
        return copy(ref, ref, self.send.at[at], self.recv.at[at], self.device(1 if way == 0 else -1))

    def outgoing(self, step, way, chunk):
        return self.copy(step, way, chunk, 1 - step if way == 0 else step - 1)

    def start(self, way, chunk):
        self.outgoing(1, way, chunk).start()

    def step(self, step, way, chunk):
        if not self.moves(step, way, chunk):
            return
        away = -step if way == 0 else step
        self.copy(step, way, chunk, away).wait_recv()
        if self.moves(step + 1, way, chunk):
            self.outgoing(step + 1, way, chunk).start()
        if self.arrived:
            self.arrived(self.ref(away, step, way, chunk))

    def each(self):
        for step in range(1, max(self.reach) + 1):
            for chunk in range(self.chunks):
                for way in BOTH:
                    if self.moves(step, way, chunk):
                        yield step, way, chunk

    def finish(self):
        for step, way, chunk in self.each():
            self.outgoing(step, way, chunk).wait_send()


class Sums:
    def __init__(self, slots, index, per, size, device, send, recv):
        self.slots, self.index, self.per, self.size, self.device = slots, index, per, size, device
        self.send, self.recv = send, recv

    def copies(self, by):
        ref = self.slots.at[pl.ds(self.index * self.per, self.per)]
        return copy(ref, ref, self.send, self.recv, self.device(by))

    def everything(self):
        ref = self.slots.at[pl.ds(0, (self.size - 1) * self.per)]
        return copy(ref, ref, self.send, self.recv, self.device(1))

    def start(self):
        for by in range(1, self.size):
            self.copies(by).start()

    def wait(self):
        self.everything().wait_recv()

    def finish(self):
        self.everything().wait_send()


class Proj:
    def __init__(self, links, buf, sems):
        self.k, self.buf = links, buf
        az_s, az_r, self.ax_s, self.ax_r, self.bx_s, self.bx_r, bz_s, bz_r, self.c_s, self.c_r = sems
        self.core = links.core
        rows, xs, steps = buf.shape[4] // 2, links.x_count // 2, links.z_count // 2
        self.first = Ring(links.z, links.z_count, links.z_device, lambda z, chunk: buf.at[self.core, 0, z, links.x],
                          az_s, az_r, (steps, steps), 1, lambda ref, way: ref.at[pl.ds(way * rows, rows)])
        self.second = Ring(links.z, links.z_count, links.z_device,
                           lambda z, chunk: buf.at[self.core, 1, z, pl.ds(chunk * xs, xs)],
                           bz_s, bz_r, (steps, steps), 2, None, self.hand_second)
        self.steps = steps

    def block(self, away, x_away):
        return self.buf.at[self.core, 0, mod(self.k.z + away, self.k.z_count), mod(self.k.x + x_away, self.k.x_count)]

    def ax(self, kind, away, x_away):
        ref = self.block(away, x_away)
        up = self.goes_up(away) if kind == 2 else kind == 0
        at = (kind, away % self.k.z_count)
        return copy(ref, ref, self.ax_s.at[at], self.ax_r.at[at], self.k.x_device(1 if up else -1))

    def goes_up(self, away):
        return away % self.k.z_count < self.steps

    def a_out(self, away):
        for kind in range(2):
            self.ax(kind, away, 0).start()

    def a_on(self, away):
        for kind, x_away in enumerate((-1, 1)):
            self.ax(kind, away, x_away).wait_recv()
        self.ax(2, away, -1 if self.goes_up(away) else 1).start()

    def aways(self, n):
        return (0,) if n == 0 else (-n, n) if n < self.steps else (n,)

    def bx(self, by, away):
        ref = self.buf.at[self.core, 1, self.k.z, mod(self.k.x + away, self.k.x_count)]
        return copy(ref, ref, self.bx_s.at[by], self.bx_r.at[by], self.k.x_device(by))

    def hand(self, part, ref):
        return copy(ref, ref, self.c_s.at[part], self.c_r.at[part], self.k.sibling())

    def hand_second(self, ref):
        self.hand(1, ref).start()

    def start(self):
        for by in range(1, self.k.x_count):
            self.bx(by, 0).start()
        for way in BOTH:
            self.first.start(way, 0)
        self.a_out(0)

    def a_step(self, n):
        for way in BOTH:
            self.first.step(n, way, 0)
        for away in self.aways(n):
            self.a_out(away)

    def a_pass(self, n):
        for away in self.aways(n):
            self.a_on(away)

    def b_start(self):
        for by in range(1, self.k.x_count):
            self.bx(by, -by).wait_recv()
        for chunk in range(2):
            for way in BOTH:
                self.second.start(way, chunk)
        self.hand(1, self.buf.at[self.core, 1, self.k.z]).start()

    def b_step(self, n, chunk):
        for way in BOTH:
            self.second.step(n, way, chunk)

    def a_hand(self, by):
        self.hand(0, self.buf.at[self.core, 0, :, mod(self.k.x + by, self.k.x_count)]).start()

    def a_near(self):
        for by in (0, -1, 1):
            self.a_hand(by)

    def a_far(self):
        for away in range(self.k.z_count):
            self.ax(2, away, 2).wait_recv()
        self.a_hand(2)

    def wait(self, part):
        self.hand(part, self.buf.at[1 - self.core, part]).wait_recv()

    def finish(self):
        self.first.finish()
        self.second.finish()
        for by in range(1, self.k.x_count):
            self.bx(by, 0).wait_send()
        for away in range(self.k.z_count):
            for kind in range(3):
                self.ax(kind, away, 0).wait_send()
        for part in range(2):
            self.hand(part, self.buf.at[self.core, part]).wait_send()


class Qkv:
    def __init__(self, links, piece, buf, sems):
        self.k, self.buf, self.source = links, buf, piece
        self.load_s, self.x_s, self.x_r, self.z_s, self.z_r, e_s, e_r, l_s, l_r, self.c_s, self.c_r = sems
        self.zs, self.xs = buf.shape[2], buf.shape[3]
        self.early = early = self.zs * 3 // 4
        up = (links.y_count - 1) // 3
        reach = (up, links.y_count - 1 - up)
        half = self.xs // 2
        mine = lambda y, *rest: buf.at[(links.core, y, *rest)]
        self.first = Ring(links.y, links.y_count, links.y_device,
                          lambda y, c: mine(y, pl.ds(0, early), pl.ds(c * half, half)),
                          e_s, e_r, reach, 2, None, lambda ref: self.hand(0, ref).start())
        self.last = Ring(links.y, links.y_count, links.y_device, lambda y, c: mine(y, pl.ds(early, self.zs - early)),
                         l_s, l_r, reach, 1, None, lambda ref: self.hand(1, ref).start())
        self.sends = lax.rem(links.z, 2) == links.core
        self.zz = lax.div(links.z, 2)

    def load(self):
        return pltpu.make_async_copy(self.source, self.buf.at[self.k.core, self.k.y, self.zz, self.k.x], self.load_s.at[0])

    def preload(self):
        pl.when(self.sends)(lambda: self.load().start())

    def z_copy(self, by):
        ref = self.buf.at[self.k.core, self.k.y, self.zz, self.k.x]
        return copy(ref, ref, self.z_s.at[0], self.z_r.at[0], self.k.z_device(by))

    def x_copy(self, by):
        ref = self.buf.at[self.k.core, self.k.y, :, self.k.x]
        return copy(ref, ref, self.x_s.at[0], self.x_r.at[0], self.k.x_device(by))

    def x_all(self):
        ref = self.buf.at[self.k.core, self.k.y, :, pl.ds(0, self.xs - 1)]
        return copy(ref, ref, self.x_s.at[0], self.x_r.at[0], self.k.x_device(1))

    def start(self):
        @pl.when(self.sends)
        def _():
            self.load().wait()
            for by in range(1, self.k.z_count):
                self.z_copy(by).start()

    def across(self):
        def got(count):
            ref = self.buf.at[self.k.core, self.k.y, pl.ds(0, count), self.k.x]
            copy(ref, ref, self.z_s.at[0], self.z_r.at[0], self.k.z_device(1)).wait_recv()

        pl.when(self.sends)(lambda: got(self.zs - 1))
        pl.when(jnp.logical_not(self.sends))(lambda: got(self.zs))
        for by in range(1, self.xs):
            self.x_copy(by).start()

    def collect(self):
        self.x_all().wait_recv()
        for chunk in range(2):
            self.first.start(1, chunk)
        for part in range(2):
            self.hand(part, self.part_of(part, self.k.core, self.k.y)).start()

    def up(self):
        for chunk in range(2):
            self.first.start(0, chunk)

    def rest(self):
        for way in BOTH:
            self.last.start(way, 0)

    def hand(self, part, ref):
        return copy(ref, ref, self.c_s.at[part], self.c_r.at[part], self.k.sibling())

    def part_of(self, part, core, y):
        zs = pl.ds(0, self.early) if part == 0 else pl.ds(self.early, self.zs - self.early)
        return self.buf.at[core, y, zs]

    def all_of(self, part, core):
        return self.hand(part, self.part_of(part, core, slice(None)))

    def wait(self, part):
        self.all_of(part, 1 - self.k.core).wait_recv()

    def finish(self):
        self.first.finish()
        self.last.finish()
        for part in range(2):
            self.all_of(part, self.k.core).wait_send()

        self.x_all().wait_send()

        @pl.when(self.sends)
        def _():
            ref = self.buf.at[self.k.core, pl.ds(0, self.k.z_count - 1), 0, self.k.x]
            copy(ref, ref, self.z_s.at[0], self.z_r.at[0], self.k.z_device(1)).wait_send()


def kernel(
    z_count, tm_count,
    features, gain, conv, proj, attn_gain, qkv, out_weight, out,
    feat, halo, conv_in, out_in, x_sums, z_sums, slab_sums, token_x, token_z,
    proj_all, qkv_all, act_hi, act_lo, residual, band_hi, band_lo, proj_hi, proj_lo, tokens, keys, queries, q_hi, q_lo, total, top, mass,
    partial, lse_mine, relay, relay_lse, joint, joint_lse, parts, parts_lse,
    load_s, halo_s, halo_r, sum_s, sum_r, *sems,
):
    proj_sems, qkv_sems, sems = sems[:10], sems[10:21], sems[21:]
    key_s, key_r, query_s, query_r, part_s, part_r = sems
    k = Links(z_count, X, tm_count)
    rows_count = z_count * X
    tm, z, x = k.tm, k.z, k.x
    frames, height, columns, channels = features.shape
    half_w = columns // 2
    count = (height // 2) * half_w
    width = tokens.shape[1]
    wide = proj_all.shape[5]
    per_half, narrow = qkv_all.shape[4:]
    steps = z_count // 2
    plan = Plan()

    loads = [
        pltpu.make_async_copy(features.at[:, :, :, pl.ds(128 * half, 128)], feat.at[half], load_s.at[half])
        for half in range(2)
    ]
    for load in loads:
        load.start()
    barrier = pltpu.get_barrier_semaphore()
    peers = (
        [k.x_device(by) for by in range(1, X)] + [k.z_device(by) for by in range(1, z_count)]
        + [k.y_device(by) for by in range(1, k.y_count)] + [k.sibling(), {"tm": mod(tm - 1 + 2 * k.core, tm_count)}]
    )
    for peer in peers:
        pl.semaphore_signal(barrier, inc=1, device_id=peer, device_id_type=pl.DeviceIdType.MESH)

    quarters = [
        pltpu.make_async_copy(
            proj.at[:, pl.ds(pl.multiple_of((2 * k.core + part) * wide, wide), wide)],
            proj_all.at[k.core, part, z, x], load_s.at[2 + part],
        )
        for part in range(2)
    ]
    piece = qkv.at[
        pl.ds(pl.multiple_of(lax.div(k.y, 4) * per_half, 8), per_half),
        pl.ds(pl.multiple_of(lax.rem(k.y, 4) * narrow, narrow), narrow),
    ]
    proj_w = Proj(k, proj_all, proj_sems)
    qkv_w = Qkv(k, piece, qkv_all, qkv_sems)
    for one in quarters:
        one.start()
    qkv_w.preload()
    weight_loads = [
        pltpu.make_async_copy(conv, conv_in, load_s.at[4]), pltpu.make_async_copy(out_weight, out_in, load_s.at[5])
    ]
    for one in weight_loads:
        one.start()

    lane = iota((8, 128), 1)
    row = iota((8, 128), 0)
    sums = []
    for load in loads:
        load.wait()
    for frame in range(frames):
        values = jnp.concatenate([feat[half, frame].reshape(height * columns, 128) for half in range(2)], axis=1)
        sums += [jnp.sum(values, axis=0, keepdims=True), jnp.sum(values * values, axis=0, keepdims=True)]
    stacked = jnp.concatenate(sums + [jnp.zeros((4, channels), f32)], axis=0)
    per_group = channels // GROUPS
    fold = (iota((channels, 128), 1) % GROUPS == iota((channels, 128), 0) // per_group).astype(f32)

    def lanes_of(rows_of_sums, table):
        return jnp.sum(jnp.where(lane // GROUPS == row, exact(rows_of_sums, table), 0.0), axis=0, keepdims=True)

    x_sums[x] = lanes_of(stacked, fold)
    for one in quarters:
        one.wait()

    def exchange(slots, index, per, size, device, n):
        return Sums(slots, index, per, size, device, sum_s.at[n], sum_r.at[n])

    over_x = exchange(x_sums, x, 1, X, k.x_device, 0)
    over_z = exchange(z_sums, z, 1, z_count, k.z_device, 1)
    over_y = exchange(slab_sums, k.y, 2, k.y_count, k.y_device, 2)
    tokens_x = exchange(token_x, x, 1, X, k.x_device, 3)
    tokens_z = exchange(token_z, z, 1, z_count, k.z_device, 4)

    def slab_copy(at):
        return copy(slab_sums.at[at], slab_sums.at[at], sum_s.at[5], sum_r.at[5], k.sibling())

    pl.semaphore_wait(barrier, len(peers))
    over_x.start()
    pairs = height // 2

    def halo_copy(f, h):
        at = (slice(None), f, pl.ds(2 * h, 2))
        return copy(feat.at[at], halo.at[at], halo_s.at[f, h], halo_r.at[f, h], {"tm": mod(tm + 1, tm_count)})

    halo_copies = [halo_copy(f, h) for h in range(pairs) for f in range(frames)]
    for one in halo_copies:
        one.start()
    proj_w.start()
    qkv_w.start()
    plan.now = 4.0

    def summed_x():
        over_x.wait()
        z_sums[z] = jnp.sum(x_sums[...], axis=0)
        over_z.start()

    def summed_z():
        over_z.wait()
        slab_sums[tm] = jnp.sum(z_sums[...], axis=0)
        slab_copy(tm).start()

    def summed_core():
        slab_copy(tm + 1 - 2 * k.core).wait_recv()
        over_y.start()

    plan.expect(6.3, "x", summed_x)
    plan.expect(7.8, "qkv x", qkv_w.across)
    plan.expect(6.8, "b", proj_w.b_start)
    plan.expect(7.5, "a", functools.partial(proj_w.a_pass, 0))
    for n in range(1, steps + 1):
        plan.expect(4.0 + 2.7 * n, "a", functools.partial(proj_w.a_step, n))
        plan.expect(7.0 + 2.7 * n, "a", functools.partial(proj_w.a_pass, n))
        for chunk in range(2):
            plan.expect(8.8 + 1.8 * (2 * n - 1 + chunk), "b", functools.partial(proj_w.b_step, n, chunk))
    plan.expect(7.1 + 2.7 * steps, "a", proj_w.a_near)
    plan.expect(10.0 + 2.7 * steps, "a far", proj_w.a_far)
    plan.expect(8.8, "z", summed_z)
    plan.expect(10.5, "core", summed_core)
    plan.expect(10.6, "collect", qkv_w.collect)
    plan.expect(13.0, "y", over_y.wait)
    for h in range(pairs):
        for frame in range(frames):
            plan.expect(11.8 + 5.8 * h + 0.1 * frame, f"halo{h}", halo_copy(frame, h).wait_recv)
    plan.expect(6.1 + 5.8 * pairs, "up", qkv_w.up)
    qkv_done = 12.6
    for step, way, chunk in qkv_w.first.each():
        time = (12.6 if way else 8.1 + 5.8 * pairs) + 1.7 * (2 * step - 1 + chunk)
        qkv_done = max(qkv_done, time)
        plan.expect(time, "qkv", functools.partial(qkv_w.first.step, step, way, chunk))
    plan.expect(qkv_done + 0.1, "rest", qkv_w.rest)
    plan.expect(qkv_done + 3.6, "qkv", functools.partial(qkv_w.wait, 0))
    for step, way, chunk in qkv_w.last.each():
        plan.expect(qkv_done + 5.0 + 2.5 * step, "qkv last", functools.partial(qkv_w.last.step, step, way, chunk))
    plan.expect(qkv_done + 7.0 + 2.5 * max(qkv_w.last.reach), "qkv last", functools.partial(qkv_w.wait, 1))

    def split_taps():
        weight_loads[0].wait()
        return [split(conv_in[lag]) for lag in range(3)]

    taps = plan.run(0.4, split_taps)

    def statistics():
        everything = slab_sums[...]
        slab = iota(everything.shape, 0)
        earlier = jnp.sum(jnp.where(slab < tm - 1, everything, 0.0), axis=0)
        previous = jnp.sum(jnp.where(slab == tm - 1, everything, 0.0), axis=0)
        own = jnp.sum(jnp.where(slab == tm, everything, 0.0), axis=0)
        kind, upto = row % 2, row // 2
        lane_kind, lane_frame = lane // GROUPS % 2, lane // GROUPS // 2
        mine = lane_kind == kind
        running = (
            jnp.where(mine, earlier, 0.0)
            + jnp.where(mine & (lane_frame <= upto), previous, 0.0)
            + jnp.where(mine & (lane_frame <= upto - 2), own, 0.0)
        )
        unfold = (iota((128, channels), 0) % GROUPS == iota((128, channels), 1) // per_group).astype(f32)
        running = exact(running, unfold)
        means, scales = [], []
        for i in range(4):
            position = jnp.maximum(tm * frames + i - 1, 1).astype(f32)
            cells = position * float(rows_count * height * columns * per_group)
            mean = running[2 * i : 2 * i + 1] / cells
            variance = running[2 * i + 1 : 2 * i + 2] / cells - mean * mean
            means.append(mean)
            scales.append(rsqrt(variance))
        return means, scales

    means, scales = plan.run(0.6, statistics, "y")
    norm_gain = gain[...]

    def cells_of(src, frame, h, b, c):
        return jnp.concatenate([src[half, frame, 2 * h + b, pl.ds(c, half_w, stride=2), :] for half in range(2)], axis=1)

    def activate(src, frame, h, at):
        for b in range(2):
            for c in range(2):
                value = (cells_of(src, frame, h, b, c) - means[at]) * scales[at] * norm_gain
                value = value / (1.0 + jnp.exp(-value))
                if at < 2:
                    value = jnp.where(tm > 0, value, 0.0)
                high, low = split(value)
                place = pl.ds((2 * b + c) * half_w, half_w)
                act_hi[at, h, place] = high
                act_lo[at, h, place] = low

    def activated(at, h):
        return tuple(ref[at, h].reshape(-1, channels) for ref in (act_hi, act_lo))

    def convolve(frame, h, terms, first=False):
        value = functools.reduce(jnp.add, [dot3(activated(at, h), taps[lag]) for at, lag in terms])
        value = value.reshape((-1, 4 * half_w, channels))
        residual[frame, h] = value if first else residual[frame, h] + value

    every = pl.ds(0, pairs)
    for frame in range(frames):
        plan.run(0.7, lambda: [activate(feat, frame, h, 2 + frame) for h in range(pairs)])
    plan.run(0.5, lambda: convolve(0, every, [(2, 0)], True))
    plan.run(1.0, lambda: convolve(1, every, [(3, 0), (2, 1)], True))
    def split_quarter(half, part):
        at = 2 * half + part
        high, low = split(proj_all[half, part].reshape(width, wide))
        proj_hi[at] = high
        proj_lo[at] = low

    for h in range(pairs):
        for frame in range(frames):
            plan.run(0.35, lambda: activate(halo, frame, h, frame), f"halo{h}")
        plan.run(0.6, lambda: convolve(0, pl.ds(h, 1), [(1, 1), (0, 2)]))
        plan.run(0.3, lambda: convolve(1, pl.ds(h, 1), [(1, 2)]))

    def haar():
        bands = [
            jnp.concatenate([
                residual[a, h, pl.ds((2 * b + c) * half_w, half_w)] + cells_of(feat, a, h, b, c) for h in range(pairs)
            ], axis=0)
            for a in range(2) for b in range(2) for c in range(2)
        ]
        for bit in (4, 2, 1):
            bands = [
                bands[j] + bands[j | bit] if not j & bit else bands[j ^ bit] - bands[j] for j in range(8)
            ]
        bands = [split(band * (1.0 / math.sqrt(8.0))) for band in bands]
        per_quarter = wide // channels
        for quarter in range(4):
            ours = bands[quarter * per_quarter : (quarter + 1) * per_quarter]
            band_hi[quarter] = jnp.concatenate([band[0] for band in ours], axis=1)
            band_lo[quarter] = jnp.concatenate([band[1] for band in ours], axis=1)

    plan.run(0.7, haar)

    def quarter_of(half, part):
        at = 2 * half + part
        return dot3((band_hi[at], band_lo[at]), (proj_hi[at], proj_lo[at]), NT)

    other = 1 - k.core
    plan.run(0.3, lambda: split_quarter(k.core, 0), "a far")
    made = plan.run(0.5, lambda: quarter_of(k.core, 0))
    proj_w.wait(0)
    plan.run(0.3, lambda: split_quarter(other, 0))
    made = made + plan.run(0.5, lambda: quarter_of(other, 0))
    plan.run(0.3, lambda: split_quarter(k.core, 1), "b")
    made = made + plan.run(0.5, lambda: quarter_of(k.core, 1))
    proj_w.wait(1)
    plan.run(0.3, lambda: split_quarter(other, 1))
    made = made + plan.run(0.5, lambda: quarter_of(other, 1))
    tokens[...] = made
    keys[z] = made
    queries[x] = made

    part_rows = count // 2
    key_chunks = 4
    key_rows = count // key_chunks
    key_ring = Ring(z, z_count, k.z_device, lambda at, c: keys.at[at, pl.ds(c * key_rows, key_rows)],
                    key_s, key_r, (steps, steps), key_chunks)
    query_ring = Ring(x, X, k.x_device, lambda at, c: queries.at[at], query_s, query_r, (X // 2, X // 2), 1,
                      lambda ref, way: ref.at[pl.ds(way * part_rows, part_rows)])
    for way in BOTH:
        query_ring.start(way, 0)
    for chunk in range(key_chunks):
        for way in BOTH:
            key_ring.start(way, chunk)
    begin = plan.now
    for step, way, chunk in key_ring.each():
        turn = chunk if step < steps else chunk % (key_chunks // 2)
        plan.expect(begin + 2.0 + 1.5 * (key_chunks * (step - 1) + turn + 1), f"key{step}",
                    functools.partial(key_ring.step, step, way, chunk))
    for step, way, chunk in query_ring.each():
        plan.expect(begin + 4.9 * step + 2.9, "queries", functools.partial(query_ring.step, step, way, chunk))

    token_group = width // GROUPS
    sums = jnp.concatenate(
        [jnp.sum(made, axis=0, keepdims=True), jnp.sum(made * made, axis=0, keepdims=True), jnp.zeros((6, width), f32)],
        axis=0,
    )
    fold = (iota((width, 128), 1) % GROUPS == iota((width, 128), 0) // token_group).astype(f32)
    token_x[x] = lanes_of(sums, fold)
    tokens_x.start()

    def token_summed_x():
        tokens_x.wait()
        token_z[z] = jnp.sum(token_x[...], axis=0)
        tokens_z.start()

    plan.expect(begin + 2.5, "tokens x", token_summed_x)
    plan.expect(begin + 5.0, "tokens z", tokens_z.wait)

    def token_statistics():
        all_sums = jnp.sum(token_z[...], axis=0)
        unfold = (iota((128, width), 0) % GROUPS == iota((128, width), 1) // token_group).astype(f32)
        spread_sums = exact(jnp.where(lane // GROUPS == row, all_sums, 0.0), unfold)
        token_count = float(rows_count * count * token_group)
        mean = spread_sums[0:1] / token_count
        return mean, rsqrt(spread_sums[1:2] / token_count - mean * mean)

    token_mean, token_scale = plan.run(0.6, token_statistics, "tokens z")
    token_gain = attn_gain[...]

    def normed(value):
        return split((value - token_mean) * token_scale * token_gain)

    def columns_of(block):
        lanes = []
        for lane_at in range(4):
            chunks = []
            for at in range(block * width // per_half, (block + 1) * width // per_half + 1):
                owner, part = at // 2, at % 2
                if owner < rows_count:
                    own_z, own_x = owner // X, owner % X
                    chunks.append(qkv_all[own_z % 2, 4 * part + lane_at, own_z // 2, own_x])
            skip = block * width - block * width // per_half * per_half
            lanes.append(jnp.concatenate(chunks, axis=0)[skip : skip + width])
        return split(jnp.concatenate(lanes, axis=1))

    def query_key_weight():
        query_weight = tuple(jnp.transpose(part.astype(f32)).astype(bf16) for part in columns_of(0))
        return split(dot3(query_weight, columns_of(1)) * (1.0 / math.sqrt(float(width))))

    def ask():
        high, low = split(dot3(normed(queries[...].reshape(X * count, width)), query_key))
        q_hi[...], q_lo[...] = high.reshape(q_hi.shape), low.reshape(q_lo.shape)

    query_key = plan.run(2.0, query_key_weight, "qkv")
    plan.run(1.5, ask, "queries")

    sets = [(0, -1, 1)] + [(-step, step) for step in range(2, steps)] + [(steps,)]

    def key_block(at):
        return normed(jnp.concatenate([keys[mod(z + away, z_count)] for away in sets[at]], axis=0))

    def rows_of(ref, at):
        return ref[at].reshape(-1, ref.shape[-1])

    def scores_of(at, block):
        return dot3((rows_of(q_hi, at), rows_of(q_lo, at)), block, NT)

    def attend(first, at, block, scores):
        here = jnp.max(scores, axis=1, keepdims=True)
        if first:
            weights = jnp.exp(scores - here)
            return here, jnp.sum(weights, axis=1, keepdims=True), dot3(split(weights), block)
        new_top = jnp.maximum(rows_of(top, at), here)
        fade = jnp.exp(rows_of(top, at) - new_top)
        weights = jnp.exp(scores - new_top)
        new_mass = rows_of(mass, at) * fade + jnp.sum(weights, axis=1, keepdims=True)
        return new_top, new_mass, rows_of(total, at) * fade + dot3(split(weights), block)

    def attend_all(step, block, scores):
        for ref, value in zip((top, mass, total), attend(step == 0, slice(None), block, scores)):
            ref[...] = value.reshape(ref.shape)

    for step in range(len(sets) - 1):
        block = plan.run(0.2, lambda: key_block(step), f"key{step + 1}")
        scores = plan.run(1.2 if step == 0 else 0.9, lambda: scores_of(slice(None), block))
        plan.run(1.6 if step == 0 else 1.2, lambda: attend_all(step, block, scores))

    half_rows = [pl.ds(way * part_rows, part_rows) for way in BOTH]
    toward = (1, -1)

    def send(kind, way, src, dst):
        return copy(src, dst, part_s.at[kind, way], part_r.at[kind, way], k.x_device(toward[way]))

    def opposite(way):
        at = mod(x + 2, X)
        return (send(0, way, partial.at[at, half_rows[way]], relay.at[way]),
                send(1, way, lse_mine.at[at], relay_lse.at[way]))

    def plain(way):
        return (send(2, way, partial.at[mod(x + toward[way], X), half_rows[1 - way]], parts.at[way, half_rows[1 - way]]),)

    def joined(way):
        return (send(3, way, joint.at[way], parts.at[way, half_rows[way]]), send(4, way, joint_lse.at[way], parts_lse.at[way]))

    def as_column(lanes):
        return jnp.transpose(jnp.broadcast_to(lanes, (count, 128)))

    def across(column):
        return jnp.concatenate([column] * (width // 128), axis=1)

    plan.need(f"key{steps}")
    block = key_block(-1)
    for by in (2, 1, 3, 0):
        at = mod(x + by, X)
        this = pl.ds(at, 1)
        last_top, last_mass, value = attend(False, this, block, scores_of(this, block))
        partial[at] = value / last_mass
        lse_mine[at] = jnp.transpose(jnp.broadcast_to(last_top + jnp.log(last_mass), (count, 128)))[0:1]
        if by == 2:
            for one in (*opposite(0), *opposite(1)):
                one.start()
        elif by:
            plain(0 if by == 1 else 1)[0].start()
    plan.now += 1.5

    def value_to_out():
        weight_loads[1].wait()
        value_weight = columns_of(2)
        value_weight = tuple(jnp.transpose(part.astype(f32)).astype(bf16) for part in value_weight)
        return split(dot3(value_weight, split(out_in[...])))

    value_out = plan.run(2.0, value_to_out, "qkv last")
    plan.upto(1e9)
    lane_row = iota((1, 128), 1)
    for way in BOTH:
        for one in opposite(way):
            one.wait_recv()
        at = mod(x + toward[way], X)
        own, theirs = lse_mine[at], relay_lse[way]
        both = jnp.maximum(own, theirs)
        both = both + jnp.log(jnp.exp(own - both) + jnp.exp(theirs - both))
        rows_of_way = slice(way * part_rows, (way + 1) * part_rows)
        joint[way] = (
            partial[at, half_rows[way]] * across(as_column(jnp.exp(own - both))[rows_of_way])
            + relay[way] * across(as_column(jnp.exp(theirs - both))[rows_of_way])
        )
        joint_lse[way] = jnp.where(lane_row // part_rows == way, both, own)
        for one in joined(way):
            one.start()

    proj_w.finish()
    qkv_w.finish()
    for one in halo_copies:
        one.wait_send()
    for one in (over_x, over_z, over_y, tokens_x, tokens_z):
        one.finish()
    slab_copy(tm).wait_send()
    key_ring.finish()
    query_ring.finish()
    for way in BOTH:
        for one in (*plain(way), *joined(way)):
            one.wait_recv()
    given = [(lse_mine[x], partial[x])] + [(parts_lse[way], parts[way]) for way in BOTH]
    highest_lse = functools.reduce(jnp.maximum, [lse for lse, _ in given])
    shares = [jnp.exp(lse - highest_lse) for lse, _ in given]
    whole = functools.reduce(jnp.add, shares)
    merged = jnp.zeros((count, width), f32)
    for share, (_, value) in zip(shares, given):
        merged = merged + value * across(as_column(share / whole))
    encoded = tokens[...] + dot3(split(merged), value_out)
    out[...] = encoded.reshape(out.shape)

    for way in BOTH:
        for one in (*opposite(way), *plain(way), *joined(way)):
            one.wait_send()


def shards(z_count, tm_count, features, norm_gain, conv_weight, proj_weight, attn_gain, qkv_weight, out_weight):
    frames, height, columns, channels = features.shape
    width = out_weight.shape[0]
    half_h, half_w = height // 2, columns // 2
    count = half_h * half_w
    steps = z_count // 2
    rows_count = z_count * X
    proj_rows, qkv_rows = proj_weight.shape[1], qkv_weight.shape[1] // 2
    wide, narrow = proj_weight.shape[0] // 4, qkv_weight.shape[0] // 4
    y_count = tm_count // 2
    far = y_count - 1 - (y_count - 1) // 3
    vmem = pltpu.VMEM
    dma = pltpu.SemaphoreType.DMA
    proj_sems = [dma((2, steps)), dma((2, steps)), dma((3, z_count)), dma((3, z_count)), dma((X,)), dma((X,)), dma((4, steps)),
                 dma((4, steps)), dma((2,)), dma((2,))]
    qkv_sems = [dma((1,)), dma((1,)), dma((1,)), dma((1,)), dma((1,)), dma((4, far)), dma((4, far)), dma((2, far)),
                dma((2, far)), dma((2,)), dma((2,))]
    scratch = [
        vmem((2, frames, height, columns, 128), f32), vmem((2, frames, height, columns, 128), f32),
        vmem(conv_weight.shape, f32), vmem(out_weight.shape, f32),
        vmem((X, 1, 128), f32), vmem((z_count, 1, 128), f32), vmem((tm_count, 1, 128), f32),
        vmem((X, 1, 128), f32), vmem((z_count, 1, 128), f32),
        vmem((2, 2, z_count, X, proj_rows, wide), f32),
        vmem((2, y_count, z_count // 2, X, qkv_rows, narrow), f32),
        vmem((4, half_h, 4 * half_w, channels), bf16), vmem((4, half_h, 4 * half_w, channels), bf16),
        vmem((frames, half_h, 4 * half_w, channels), f32),
        vmem((4, count, wide), bf16), vmem((4, count, wide), bf16),
        vmem((4, width, wide), bf16), vmem((4, width, wide), bf16),
        vmem((count, width), f32),
        vmem((z_count, count, width), f32),
        vmem((X, count, width), f32),
        vmem((X, count, width), bf16), vmem((X, count, width), bf16),
        vmem((X, count, width), f32), vmem((X, count, 1), f32), vmem((X, count, 1), f32),
        vmem((X, count, width), f32), vmem((X, 1, 128), f32),
        vmem((2, count // 2, width), f32), vmem((2, 1, 128), f32),
        vmem((2, count // 2, width), f32), vmem((2, 1, 128), f32),
        vmem((2, count, width), f32), vmem((2, 1, 128), f32),
        dma((6,)), dma((frames, half_h)), dma((frames, half_h)), dma((6,)), dma((6,)),
        *proj_sems, *qkv_sems,
        dma((8, steps)), dma((8, steps)), dma((2, X // 2)), dma((2, X // 2)), dma((5, 2)), dma((5, 2)),
    ]
    whole = pl.BlockSpec(memory_space=vmem)
    anywhere = pl.BlockSpec(memory_space=pl.ANY)
    return pl.pallas_call(
        functools.partial(kernel, z_count, tm_count),
        out_shape=jax.ShapeDtypeStruct((frames // 2, half_h, half_w, width), f32),
        in_specs=[anywhere, whole, anywhere, anywhere, whole, anywhere, anywhere],
        out_specs=whole,
        scratch_shapes=scratch,
        compiler_params=pltpu.CompilerParams(collective_id=0, has_side_effects=True, vmem_limit_bytes=56 * 2**20),
    )(features, norm_gain[None], conv_weight, proj_weight.T, attn_gain[None], qkv_weight.T, out_weight)


def solution(mesh):
    in_specs = (P("tm", "rows", None, None), P(), P(), P(None, "rows"), P(), P(None, "rows"), P())
    out_specs = P("tm", "rows", None, None)
    body = functools.partial(shards, mesh.shape["rows"] // X, mesh.shape["tm"])
    return jax.shard_map(body, mesh=mesh, in_specs=in_specs, out_specs=out_specs, check_vma=False)
```

```python
import functools
import math

import jax
import jax.numpy as jnp
from jax import lax
from jax.experimental import pallas as pl
from jax.experimental.pallas import tpu as pltpu
from jax.sharding import PartitionSpec as P

GROUPS = 32
X = 4
epsilon = 1e-06
f32, bf16 = jnp.float32, jnp.bfloat16
NN = (((1,), (0,)), ((), ()))
NT = (((1,), (1,)), ((), ()))
BOTH = (0, 1)


def split(value):
    high = value.astype(bf16)
    return high, (value - high.astype(f32)).astype(bf16)


def dot(a, b, dims):
    return lax.dot_general(a, b, dims, preferred_element_type=f32)


def dot3(a, b, dims=NN):
    rows = a[0].shape[0]
    if rows > 256:
        deep = (b[0], b[0], b[1])
        return dot(jnp.concatenate((a[0], a[1], a[0]), axis=1), jnp.concatenate(deep, axis=dims[0][1][0]), dims)
    by_high = dot(jnp.concatenate(a, axis=0), b[0], dims)
    return by_high[:rows] + (by_high[rows:] + dot(a[0], b[1], dims))


def dot3_turned(a, b):
    rows = a[0].shape[0]
    by_high = dot(b[0], jnp.concatenate(a, axis=0), NT)
    return by_high[:, :rows] + (by_high[:, rows:] + dot(b[1], a[0], NT))


def exact(a, table):
    high = a.astype(bf16)
    rest = a - high.astype(f32)
    middle = rest.astype(bf16)
    low = (rest - middle.astype(f32)).astype(bf16)
    rows = a.shape[0]
    parts = jnp.concatenate([part.astype(f32) for part in (high, middle, low)] + [jnp.zeros_like(a)], axis=0).astype(bf16)
    by_part = dot(parts, table.astype(bf16), NN)
    return by_part[:rows] + (by_part[rows : 2 * rows] + by_part[2 * rows : 3 * rows])


def iota(shape, axis):
    return lax.broadcasted_iota(jnp.int32, shape, axis)


def rsqrt(value):
    return lax.rsqrt(value + epsilon)


def mod(value, size):
    return lax.rem(value + size, size)


class Plan:
    def __init__(self):
        self.now, self.waits = 0.0, []

    def expect(self, time, name, action):
        self.waits.append((time, len(self.waits), name, action))

    def upto(self, time):
        while True:
            due = [wait for wait in self.waits if wait[0] <= time]
            if not due:
                return
            first = min(due, key=lambda wait: wait[:2])
            self.waits.remove(first)
            first[3]()

    def need(self, name):
        times = [wait[0] for wait in self.waits if wait[2] == name]
        if times:
            self.now = max(self.now, max(times))
            self.upto(max(times))

    def run(self, duration, action, *needs):
        for name in needs:
            self.need(name)
        self.upto(self.now)
        result = action()
        self.now += duration
        return result


class Links:
    def __init__(self, z_count, x_count, tm_count):
        self.rows, self.tm = lax.axis_index("rows"), lax.axis_index("tm")
        self.z, self.x = lax.div(self.rows, x_count), lax.rem(self.rows, x_count)
        self.y, self.core = lax.div(self.tm, 2), lax.rem(self.tm, 2)
        self.z_count, self.x_count, self.y_count = z_count, x_count, tm_count // 2

    def z_device(self, by):
        return {"rows": mod(self.z + by, self.z_count) * self.x_count + self.x}

    def x_device(self, by):
        return {"rows": self.z * self.x_count + mod(self.x + by, self.x_count)}

    def y_device(self, by):
        return {"tm": mod(self.y + by, self.y_count) * 2 + self.core}

    def sibling(self):
        return {"tm": self.tm + 1 - 2 * self.core}


def copy(src, dst, send, recv, device):
    return pltpu.make_async_remote_copy(
        src_ref=src, dst_ref=dst, send_sem=send, recv_sem=recv, device_id=device,
        device_id_type=pl.DeviceIdType.MESH,
    )


class Ring:
    def __init__(self, place, count, device, at, send, recv, reach, chunks=1, half=None, arrived=None):
        self.place, self.count, self.device, self.at, self.half = place, count, device, at, half
        self.send, self.recv, self.reach, self.chunks, self.arrived = send, recv, reach, chunks, arrived

    def moves(self, step, way, chunk):
        if step > self.reach[way]:
            return False
        shared = step == self.reach[0] == self.reach[1] and 2 * step == self.count
        return not shared or self.chunks == 1 or chunk // (self.chunks // 2) == way

    def ref(self, away, step, way, chunk):
        ref = self.at(mod(self.place + away, self.count), chunk)
        return self.half(ref, way) if self.half and 2 * step == self.count else ref

    def copy(self, step, way, chunk, away):
        ref = self.ref(away, step, way, chunk)
        at = (way * self.chunks + chunk, step - 1)
        return copy(ref, ref, self.send.at[at], self.recv.at[at], self.device(1 if way == 0 else -1))

    def outgoing(self, step, way, chunk):
        return self.copy(step, way, chunk, 1 - step if way == 0 else step - 1)

    def start(self, way, chunk):
        self.outgoing(1, way, chunk).start()

    def step(self, step, way, chunk):
        if not self.moves(step, way, chunk):
            return
        away = -step if way == 0 else step
        self.copy(step, way, chunk, away).wait_recv()
        if self.moves(step + 1, way, chunk):
            self.outgoing(step + 1, way, chunk).start()
        if self.arrived:
            self.arrived(self.ref(away, step, way, chunk))

    def each(self):
        for step in range(1, max(self.reach) + 1):
            for chunk in range(self.chunks):
                for way in BOTH:
                    if self.moves(step, way, chunk):
                        yield step, way, chunk

    def finish(self):
        for step, way, chunk in self.each():
            self.outgoing(step, way, chunk).wait_send()


class Sums:
    def __init__(self, slots, index, per, size, device, send, recv):
        self.slots, self.index, self.per, self.size, self.device = slots, index, per, size, device
        self.send, self.recv = send, recv

    def copies(self, by):
        ref = self.slots.at[pl.ds(self.index * self.per, self.per)]
        return copy(ref, ref, self.send, self.recv, self.device(by))

    def everything(self):
        ref = self.slots.at[pl.ds(0, (self.size - 1) * self.per)]
        return copy(ref, ref, self.send, self.recv, self.device(1))

    def start(self):
        for by in range(1, self.size):
            self.copies(by).start()

    def wait(self):
        self.everything().wait_recv()

    def finish(self):
        self.everything().wait_send()


class Proj:
    def __init__(self, links, buf, sems):
        self.k, self.buf = links, buf
        az_s, az_r, self.ax_s, self.ax_r, self.bx_s, self.bx_r, bz_s, bz_r, self.c_s, self.c_r = sems
        self.core = links.core
        rows, xs, steps = buf.shape[4] // 2, links.x_count // 2, links.z_count // 2
        self.first = Ring(links.z, links.z_count, links.z_device, lambda z, chunk: buf.at[self.core, 0, z, links.x],
                          az_s, az_r, (steps, steps), 1, lambda ref, way: ref.at[pl.ds(way * rows, rows)])
        self.second = Ring(links.z, links.z_count, links.z_device,
                           lambda z, chunk: buf.at[self.core, 1, z, pl.ds(chunk * xs, xs)],
                           bz_s, bz_r, (steps, steps), 2, None, self.hand_second)
        self.steps = steps

    def block(self, away, x_away):
        return self.buf.at[self.core, 0, mod(self.k.z + away, self.k.z_count), mod(self.k.x + x_away, self.k.x_count)]

    def ax(self, kind, away, x_away):
        ref = self.block(away, x_away)
        up = self.goes_up(away) if kind == 2 else kind == 0
        at = (kind, away % self.k.z_count)
        return copy(ref, ref, self.ax_s.at[at], self.ax_r.at[at], self.k.x_device(1 if up else -1))

    def goes_up(self, away):
        return away % self.k.z_count < self.steps

    def a_out(self, away):
        for kind in range(2):
            self.ax(kind, away, 0).start()

    def a_on(self, away):
        for kind, x_away in enumerate((-1, 1)):
            self.ax(kind, away, x_away).wait_recv()
        self.ax(2, away, -1 if self.goes_up(away) else 1).start()

    def aways(self, n):
        return (0,) if n == 0 else (-n, n) if n < self.steps else (n,)

    def bx(self, by, away):
        ref = self.buf.at[self.core, 1, self.k.z, mod(self.k.x + away, self.k.x_count)]
        return copy(ref, ref, self.bx_s.at[by], self.bx_r.at[by], self.k.x_device(by))

    def hand(self, part, ref):
        return copy(ref, ref, self.c_s.at[part], self.c_r.at[part], self.k.sibling())

    def hand_second(self, ref):
        self.hand(1, ref).start()

    def start(self):
        for by in range(1, self.k.x_count):
            self.bx(by, 0).start()
        for way in BOTH:
            self.first.start(way, 0)
        self.a_out(0)

    def a_step(self, n):
        for way in BOTH:
            self.first.step(n, way, 0)
        for away in self.aways(n):
            self.a_out(away)

    def a_pass(self, n):
        for away in self.aways(n):
            self.a_on(away)

    def b_start(self):
        for by in range(1, self.k.x_count):
            self.bx(by, -by).wait_recv()
        for chunk in range(2):
            for way in BOTH:
                self.second.start(way, chunk)
        self.hand(1, self.buf.at[self.core, 1, self.k.z]).start()

    def b_step(self, n, chunk):
        for way in BOTH:
            self.second.step(n, way, chunk)

    def a_hand(self, by):
        self.hand(0, self.buf.at[self.core, 0, :, mod(self.k.x + by, self.k.x_count)]).start()

    def a_near(self):
        for by in (0, -1, 1):
            self.a_hand(by)

    def a_far(self):
        for away in range(self.k.z_count):
            self.ax(2, away, 2).wait_recv()
        self.a_hand(2)

    def wait(self, part):
        self.hand(part, self.buf.at[1 - self.core, part]).wait_recv()

    def finish(self):
        self.first.finish()
        self.second.finish()
        for by in range(1, self.k.x_count):
            self.bx(by, 0).wait_send()
        for away in range(self.k.z_count):
            for kind in range(3):
                self.ax(kind, away, 0).wait_send()
        for part in range(2):
            self.hand(part, self.buf.at[self.core, part]).wait_send()


class Qkv:
    def __init__(self, links, piece, buf, sems):
        self.k, self.buf, self.source = links, buf, piece
        self.load_s, self.x_s, self.x_r, self.z_s, self.z_r, e_s, e_r, l_s, l_r, self.c_s, self.c_r = sems
        self.zs, self.xs = buf.shape[2], buf.shape[3]
        self.early = early = self.zs * 3 // 4
        up = (links.y_count - 1) // 3
        reach = (up, links.y_count - 1 - up)
        half = self.xs // 2
        mine = lambda y, *rest: buf.at[(links.core, y, *rest)]
        self.first = Ring(links.y, links.y_count, links.y_device,
                          lambda y, c: mine(y, pl.ds(0, early), pl.ds(c * half, half)),
                          e_s, e_r, reach, 2, None, lambda ref: self.hand(0, ref).start())
        self.last = Ring(links.y, links.y_count, links.y_device, lambda y, c: mine(y, pl.ds(early, self.zs - early)),
                         l_s, l_r, reach, 1, None, lambda ref: self.hand(1, ref).start())
        self.sends = lax.rem(links.z, 2) == links.core
        self.zz = lax.div(links.z, 2)

    def load(self):
        return pltpu.make_async_copy(self.source, self.buf.at[self.k.core, self.k.y, self.zz, self.k.x], self.load_s.at[0])

    def preload(self):
        pl.when(self.sends)(lambda: self.load().start())

    def z_copy(self, by):
        ref = self.buf.at[self.k.core, self.k.y, self.zz, self.k.x]
        return copy(ref, ref, self.z_s.at[0], self.z_r.at[0], self.k.z_device(by))

    def x_copy(self, by):
        ref = self.buf.at[self.k.core, self.k.y, :, self.k.x]
        return copy(ref, ref, self.x_s.at[0], self.x_r.at[0], self.k.x_device(by))

    def x_all(self):
        ref = self.buf.at[self.k.core, self.k.y, :, pl.ds(0, self.xs - 1)]
        return copy(ref, ref, self.x_s.at[0], self.x_r.at[0], self.k.x_device(1))

    def start(self):
        @pl.when(self.sends)
        def _():
            self.load().wait()
            for by in range(1, self.k.z_count):
                self.z_copy(by).start()

    def across(self):
        def got(count):
            ref = self.buf.at[self.k.core, self.k.y, pl.ds(0, count), self.k.x]
            copy(ref, ref, self.z_s.at[0], self.z_r.at[0], self.k.z_device(1)).wait_recv()

        pl.when(self.sends)(lambda: got(self.zs - 1))
        pl.when(jnp.logical_not(self.sends))(lambda: got(self.zs))
        for by in range(1, self.xs):
            self.x_copy(by).start()

    def collect(self):
        self.x_all().wait_recv()
        for chunk in range(2):
            self.first.start(1, chunk)
        for part in range(2):
            self.hand(part, self.part_of(part, self.k.core, self.k.y)).start()

    def up(self):
        for chunk in range(2):
            self.first.start(0, chunk)

    def rest(self):
        for way in BOTH:
            self.last.start(way, 0)

    def hand(self, part, ref):
        return copy(ref, ref, self.c_s.at[part], self.c_r.at[part], self.k.sibling())

    def part_of(self, part, core, y):
        zs = pl.ds(0, self.early) if part == 0 else pl.ds(self.early, self.zs - self.early)
        return self.buf.at[core, y, zs]

    def all_of(self, part, core):
        return self.hand(part, self.part_of(part, core, slice(None)))

    def wait(self, part):
        self.all_of(part, 1 - self.k.core).wait_recv()

    def finish(self):
        self.first.finish()
        self.last.finish()
        for part in range(2):
            self.all_of(part, self.k.core).wait_send()

        self.x_all().wait_send()

        @pl.when(self.sends)
        def _():
            ref = self.buf.at[self.k.core, pl.ds(0, self.k.z_count - 1), 0, self.k.x]
            copy(ref, ref, self.z_s.at[0], self.z_r.at[0], self.k.z_device(1)).wait_send()


def kernel(
    z_count, tm_count,
    features, gain, conv, proj, attn_gain, qkv, out_weight, out,
    feat, halo, conv_in, out_in, x_sums, z_sums, slab_sums, token_x, token_z,
    proj_all, qkv_all, act_hi, act_lo, residual, band_hi, band_lo, proj_hi, proj_lo, tokens, keys, queries, q_hi, q_lo, total, top, mass,
    partial, lse_mine, relay, relay_lse, joint, joint_lse, parts, parts_lse,
    load_s, halo_s, halo_r, sum_s, sum_r, *sems,
):
    proj_sems, qkv_sems, sems = sems[:10], sems[10:21], sems[21:]
    key_s, key_r, query_s, query_r, part_s, part_r = sems
    k = Links(z_count, X, tm_count)
    rows_count = z_count * X
    tm, z, x = k.tm, k.z, k.x
    frames, height, columns, channels = features.shape
    half_w = columns // 2
    count = (height // 2) * half_w
    width = tokens.shape[1]
    wide = proj_all.shape[5]
    per_half, narrow = qkv_all.shape[4:]
    steps = z_count // 2
    plan = Plan()

    loads = [
        pltpu.make_async_copy(features.at[:, :, :, pl.ds(128 * half, 128)], feat.at[half], load_s.at[half])
        for half in range(2)
    ]
    for load in loads:
        load.start()
    barrier = pltpu.get_barrier_semaphore()
    peers = (
        [k.x_device(by) for by in range(1, X)] + [k.z_device(by) for by in range(1, z_count)]
        + [k.y_device(by) for by in range(1, k.y_count)] + [k.sibling(), {"tm": mod(tm - 1 + 2 * k.core, tm_count)}]
    )
    for peer in peers:
        pl.semaphore_signal(barrier, inc=1, device_id=peer, device_id_type=pl.DeviceIdType.MESH)

    quarters = [
        pltpu.make_async_copy(
            proj.at[:, pl.ds(pl.multiple_of((2 * k.core + part) * wide, wide), wide)],
            proj_all.at[k.core, part, z, x], load_s.at[2 + part],
        )
        for part in range(2)
    ]
    piece = qkv.at[
        pl.ds(pl.multiple_of(lax.div(k.y, 4) * per_half, 8), per_half),
        pl.ds(pl.multiple_of(lax.rem(k.y, 4) * narrow, narrow), narrow),
    ]
    proj_w = Proj(k, proj_all, proj_sems)
    qkv_w = Qkv(k, piece, qkv_all, qkv_sems)
    for one in quarters:
        one.start()
    qkv_w.preload()
    weight_loads = [
        pltpu.make_async_copy(conv, conv_in, load_s.at[4]), pltpu.make_async_copy(out_weight, out_in, load_s.at[5])
    ]
    for one in weight_loads:
        one.start()

    lane = iota((8, 128), 1)
    row = iota((8, 128), 0)
    sums = []
    for load in loads:
        load.wait()
    for frame in range(frames):
        values = jnp.concatenate([feat[half, frame].reshape(height * columns, 128) for half in range(2)], axis=1)
        sums += [jnp.sum(values, axis=0, keepdims=True), jnp.sum(values * values, axis=0, keepdims=True)]
    stacked = jnp.concatenate(sums + [jnp.zeros((4, channels), f32)], axis=0)
    per_group = channels // GROUPS
    fold = (iota((channels, 128), 1) % GROUPS == iota((channels, 128), 0) // per_group).astype(f32)

    def lanes_of(rows_of_sums, table):
        return jnp.sum(jnp.where(lane // GROUPS == row, exact(rows_of_sums, table), 0.0), axis=0, keepdims=True)

    x_sums[x] = lanes_of(stacked, fold)
    for one in quarters:
        one.wait()

    def exchange(slots, index, per, size, device, n):
        return Sums(slots, index, per, size, device, sum_s.at[n], sum_r.at[n])

    over_x = exchange(x_sums, x, 1, X, k.x_device, 0)
    over_z = exchange(z_sums, z, 1, z_count, k.z_device, 1)
    over_y = exchange(slab_sums, k.y, 2, k.y_count, k.y_device, 2)
    tokens_x = exchange(token_x, x, 1, X, k.x_device, 3)
    tokens_z = exchange(token_z, z, 1, z_count, k.z_device, 4)

    def slab_copy(at):
        return copy(slab_sums.at[at], slab_sums.at[at], sum_s.at[5], sum_r.at[5], k.sibling())

    pl.semaphore_wait(barrier, len(peers))
    over_x.start()
    pairs = height // 2

    def halo_copy(f, h):
        at = (slice(None), f, pl.ds(2 * h, 2))
        return copy(feat.at[at], halo.at[at], halo_s.at[f, h], halo_r.at[f, h], {"tm": mod(tm + 1, tm_count)})

    halo_copies = [halo_copy(f, h) for h in range(pairs) for f in range(frames)]
    for one in halo_copies:
        one.start()
    proj_w.start()
    qkv_w.start()
    plan.now = 4.0

    def summed_x():
        over_x.wait()
        z_sums[z] = jnp.sum(x_sums[...], axis=0)
        over_z.start()

    def summed_z():
        over_z.wait()
        slab_sums[tm] = jnp.sum(z_sums[...], axis=0)
        slab_copy(tm).start()

    def summed_core():
        slab_copy(tm + 1 - 2 * k.core).wait_recv()
        over_y.start()

    plan.expect(6.3, "x", summed_x)
    plan.expect(7.8, "qkv x", qkv_w.across)
    plan.expect(6.8, "b", proj_w.b_start)
    plan.expect(7.5, "a", functools.partial(proj_w.a_pass, 0))
    for n in range(1, steps + 1):
        plan.expect(4.0 + 2.7 * n, "a", functools.partial(proj_w.a_step, n))
        plan.expect(7.0 + 2.7 * n, "a", functools.partial(proj_w.a_pass, n))
        for chunk in range(2):
            plan.expect(8.8 + 1.8 * (2 * n - 1 + chunk), "b", functools.partial(proj_w.b_step, n, chunk))
    plan.expect(7.1 + 2.7 * steps, "a", proj_w.a_near)
    plan.expect(10.0 + 2.7 * steps, "a far", proj_w.a_far)
    plan.expect(8.8, "z", summed_z)
    plan.expect(10.5, "core", summed_core)
    plan.expect(10.6, "collect", qkv_w.collect)
    plan.expect(13.0, "y", over_y.wait)
    for h in range(pairs):
        for frame in range(frames):
            plan.expect(11.8 + 5.8 * h + 0.1 * frame, f"halo{h}", halo_copy(frame, h).wait_recv)
    plan.expect(6.1 + 5.8 * pairs, "up", qkv_w.up)
    qkv_done = 12.6
    for step, way, chunk in qkv_w.first.each():
        time = (12.6 if way else 8.1 + 5.8 * pairs) + 1.7 * (2 * step - 1 + chunk)
        qkv_done = max(qkv_done, time)
        plan.expect(time, "qkv", functools.partial(qkv_w.first.step, step, way, chunk))
    plan.expect(qkv_done + 0.1, "rest", qkv_w.rest)
    plan.expect(qkv_done + 3.6, "qkv", functools.partial(qkv_w.wait, 0))
    for step, way, chunk in qkv_w.last.each():
        plan.expect(qkv_done + 5.0 + 2.5 * step, "qkv last", functools.partial(qkv_w.last.step, step, way, chunk))
    plan.expect(qkv_done + 7.0 + 2.5 * max(qkv_w.last.reach), "qkv last", functools.partial(qkv_w.wait, 1))

    def split_taps():
        weight_loads[0].wait()
        return [split(conv_in[lag]) for lag in range(3)]

    taps = plan.run(0.4, split_taps)

    def statistics():
        everything = slab_sums[...]
        slab = iota(everything.shape, 0)
        earlier = jnp.sum(jnp.where(slab < tm - 1, everything, 0.0), axis=0)
        previous = jnp.sum(jnp.where(slab == tm - 1, everything, 0.0), axis=0)
        own = jnp.sum(jnp.where(slab == tm, everything, 0.0), axis=0)
        kind, upto = row % 2, row // 2
        lane_kind, lane_frame = lane // GROUPS % 2, lane // GROUPS // 2
        mine = lane_kind == kind
        running = (
            jnp.where(mine, earlier, 0.0)
            + jnp.where(mine & (lane_frame <= upto), previous, 0.0)
            + jnp.where(mine & (lane_frame <= upto - 2), own, 0.0)
        )
        unfold = (iota((128, channels), 0) % GROUPS == iota((128, channels), 1) // per_group).astype(f32)
        running = exact(running, unfold)
        means, scales = [], []
        for i in range(4):
            position = jnp.maximum(tm * frames + i - 1, 1).astype(f32)
            cells = position * float(rows_count * height * columns * per_group)
            mean = running[2 * i : 2 * i + 1] / cells
            variance = running[2 * i + 1 : 2 * i + 2] / cells - mean * mean
            means.append(mean)
            scales.append(rsqrt(variance))
        return means, scales

    means, scales = plan.run(0.6, statistics, "y")
    norm_gain = gain[...]

    def cells_of(src, frame, h, b, c):
        return jnp.concatenate([src[half, frame, 2 * h + b, pl.ds(c, half_w, stride=2), :] for half in range(2)], axis=1)

    def activate(src, frame, h, at):
        for b in range(2):
            for c in range(2):
                value = (cells_of(src, frame, h, b, c) - means[at]) * scales[at] * norm_gain
                value = value / (1.0 + jnp.exp(-value))
                if at < 2:
                    value = jnp.where(tm > 0, value, 0.0)
                high, low = split(value)
                place = pl.ds((2 * b + c) * half_w, half_w)
                act_hi[at, h, place] = high
                act_lo[at, h, place] = low

    def activated(at, h):
        return tuple(ref[at, h].reshape(-1, channels) for ref in (act_hi, act_lo))

    def convolve(frame, h, terms, first=False):
        value = functools.reduce(jnp.add, [dot3(activated(at, h), taps[lag]) for at, lag in terms])
        value = value.reshape((-1, 4 * half_w, channels))
        residual[frame, h] = value if first else residual[frame, h] + value

    every = pl.ds(0, pairs)
    for frame in range(frames):
        plan.run(0.7, lambda: [activate(feat, frame, h, 2 + frame) for h in range(pairs)])
    plan.run(0.5, lambda: convolve(0, every, [(2, 0)], True))
    plan.run(1.0, lambda: convolve(1, every, [(3, 0), (2, 1)], True))
    def split_quarter(half, part):
        at = 2 * half + part
        high, low = split(proj_all[half, part].reshape(width, wide))
        proj_hi[at] = high
        proj_lo[at] = low

    for h in range(pairs):
        for frame in range(frames):
            plan.run(0.35, lambda: activate(halo, frame, h, frame), f"halo{h}")
        plan.run(0.6, lambda: convolve(0, pl.ds(h, 1), [(1, 1), (0, 2)]))
        plan.run(0.3, lambda: convolve(1, pl.ds(h, 1), [(1, 2)]))

    def haar():
        bands = [
            jnp.concatenate([
                residual[a, h, pl.ds((2 * b + c) * half_w, half_w)] + cells_of(feat, a, h, b, c) for h in range(pairs)
            ], axis=0)
            for a in range(2) for b in range(2) for c in range(2)
        ]
        for bit in (4, 2, 1):
            bands = [
                bands[j] + bands[j | bit] if not j & bit else bands[j ^ bit] - bands[j] for j in range(8)
            ]
        bands = [split(band * (1.0 / math.sqrt(8.0))) for band in bands]
        per_quarter = wide // channels
        for quarter in range(4):
            ours = bands[quarter * per_quarter : (quarter + 1) * per_quarter]
            band_hi[quarter] = jnp.concatenate([band[0] for band in ours], axis=1)
            band_lo[quarter] = jnp.concatenate([band[1] for band in ours], axis=1)

    plan.run(0.7, haar)

    def quarter_of(half, part):
        at = 2 * half + part
        return dot3_turned((band_hi[at], band_lo[at]), (proj_hi[at], proj_lo[at]))

    other = 1 - k.core
    plan.run(0.3, lambda: split_quarter(k.core, 0), "a far")
    made = plan.run(0.5, lambda: quarter_of(k.core, 0))
    proj_w.wait(0)
    plan.run(0.3, lambda: split_quarter(other, 0))
    made = made + plan.run(0.5, lambda: quarter_of(other, 0))
    plan.run(0.3, lambda: split_quarter(k.core, 1), "b")
    made = made + plan.run(0.5, lambda: quarter_of(k.core, 1))
    proj_w.wait(1)
    plan.run(0.3, lambda: split_quarter(other, 1))
    made = made + plan.run(0.5, lambda: quarter_of(other, 1))
    made = jnp.transpose(made)
    tokens[...] = made
    keys[z] = made
    queries[x] = made

    part_rows = count // 2
    key_chunks = 4
    key_rows = count // key_chunks
    key_ring = Ring(z, z_count, k.z_device, lambda at, c: keys.at[at, pl.ds(c * key_rows, key_rows)],
                    key_s, key_r, (steps, steps), key_chunks)
    query_ring = Ring(x, X, k.x_device, lambda at, c: queries.at[at], query_s, query_r, (X // 2, X // 2), 1,
                      lambda ref, way: ref.at[pl.ds(way * part_rows, part_rows)])
    for way in BOTH:
        query_ring.start(way, 0)
    for chunk in range(key_chunks):
        for way in BOTH:
            key_ring.start(way, chunk)
    begin = plan.now
    for step, way, chunk in key_ring.each():
        turn = chunk if step < steps else chunk % (key_chunks // 2)
        plan.expect(begin + 2.0 + 1.5 * (key_chunks * (step - 1) + turn + 1), f"key{step}",
                    functools.partial(key_ring.step, step, way, chunk))
    for step, way, chunk in query_ring.each():
        plan.expect(begin + 4.9 * step + 2.9, "queries", functools.partial(query_ring.step, step, way, chunk))

    token_group = width // GROUPS
    sums = jnp.concatenate(
        [jnp.sum(made, axis=0, keepdims=True), jnp.sum(made * made, axis=0, keepdims=True), jnp.zeros((6, width), f32)],
        axis=0,
    )
    fold = (iota((width, 128), 1) % GROUPS == iota((width, 128), 0) // token_group).astype(f32)
    token_x[x] = lanes_of(sums, fold)
    tokens_x.start()

    def token_summed_x():
        tokens_x.wait()
        token_z[z] = jnp.sum(token_x[...], axis=0)
        tokens_z.start()

    plan.expect(begin + 2.5, "tokens x", token_summed_x)
    plan.expect(begin + 5.0, "tokens z", tokens_z.wait)

    def token_statistics():
        all_sums = jnp.sum(token_z[...], axis=0)
        unfold = (iota((128, width), 0) % GROUPS == iota((128, width), 1) // token_group).astype(f32)
        spread_sums = exact(jnp.where(lane // GROUPS == row, all_sums, 0.0), unfold)
        token_count = float(rows_count * count * token_group)
        mean = spread_sums[0:1] / token_count
        return mean, rsqrt(spread_sums[1:2] / token_count - mean * mean)

    token_mean, token_scale = plan.run(0.6, token_statistics, "tokens z")
    token_gain = attn_gain[...]

    def normed(value):
        return split((value - token_mean) * token_scale * token_gain)

    def columns_of(block):
        lanes = []
        for lane_at in range(4):
            chunks = []
            for at in range(block * width // per_half, (block + 1) * width // per_half + 1):
                owner, part = at // 2, at % 2
                if owner < rows_count:
                    own_z, own_x = owner // X, owner % X
                    chunks.append(qkv_all[own_z % 2, 4 * part + lane_at, own_z // 2, own_x])
            skip = block * width - block * width // per_half * per_half
            lanes.append(jnp.concatenate(chunks, axis=0)[skip : skip + width])
        return split(jnp.concatenate(lanes, axis=1))

    def query_key_weight():
        query_weight = tuple(jnp.transpose(part.astype(f32)).astype(bf16) for part in columns_of(0))
        return split(dot3(query_weight, columns_of(1)) * (1.0 / math.sqrt(float(width))))

    order = (2, 1, 3, 0)

    def ask():
        asking = jnp.concatenate([queries[mod(x + by, X)] for by in order], axis=0)
        high, low = split(dot3(normed(asking), query_key))
        q_hi[...], q_lo[...] = high.reshape(q_hi.shape), low.reshape(q_lo.shape)

    query_key = plan.run(2.0, query_key_weight, "qkv")
    plan.run(1.5, ask, "queries")

    sets = [(0, -1, 1)] + [(-step, step) for step in range(2, steps)] + [(steps,)]

    def key_block(at):
        return normed(jnp.concatenate([keys[mod(z + away, z_count)] for away in sets[at]], axis=0))

    def rows_of(ref, at):
        return ref[at].reshape(-1, ref.shape[-1])

    def scores_of(at, block):
        return dot3((rows_of(q_hi, at), rows_of(q_lo, at)), block, NT)

    def attend(first, at, block, scores):
        here = jnp.max(scores, axis=1, keepdims=True)
        if first:
            weights = jnp.exp(scores - here)
            return here, jnp.sum(weights, axis=1, keepdims=True), dot3(split(weights), block)
        new_top = jnp.maximum(rows_of(top, at), here)
        fade = jnp.exp(rows_of(top, at) - new_top)
        weights = jnp.exp(scores - new_top)
        new_mass = rows_of(mass, at) * fade + jnp.sum(weights, axis=1, keepdims=True)
        return new_top, new_mass, rows_of(total, at) * fade + dot3(split(weights), block)

    def attend_all(step, block, scores):
        for ref, value in zip((top, mass, total), attend(step == 0, slice(None), block, scores)):
            ref[...] = value.reshape(ref.shape)

    for step in range(len(sets) - 1):
        block = plan.run(0.2, lambda: key_block(step), f"key{step + 1}")
        scores = plan.run(1.2 if step == 0 else 0.9, lambda: scores_of(slice(None), block))
        plan.run(1.6 if step == 0 else 1.2, lambda: attend_all(step, block, scores))

    half_rows = [pl.ds(way * part_rows, part_rows) for way in BOTH]
    toward = (1, -1)

    def send(kind, way, src, dst):
        return copy(src, dst, part_s.at[kind, way], part_r.at[kind, way], k.x_device(toward[way]))

    def opposite(way):
        return (send(0, way, partial.at[0, half_rows[way]], relay.at[way]),
                send(1, way, lse_mine.at[0], relay_lse.at[way]))

    def plain(way):
        return (send(2, way, partial.at[1 + way, half_rows[1 - way]], parts.at[way, half_rows[1 - way]]),)

    def joined(way):
        return (send(3, way, joint.at[way], parts.at[way, half_rows[way]]), send(4, way, joint_lse.at[way], parts_lse.at[way]))

    def as_column(lanes):
        return jnp.transpose(jnp.broadcast_to(lanes, (count, 128)))

    def across(column):
        return jnp.concatenate([column] * (width // 128), axis=1)

    plan.need(f"key{steps}")
    block = key_block(-1)
    for first, last in ((0, 1), (1, X)):
        at = slice(first, last)
        last_top, last_mass, value = attend(False, at, block, scores_of(at, block))
        partial[at] = (value / last_mass).reshape(last - first, count, width)
        lse = last_top + jnp.log(last_mass)
        for i in range(first, last):
            column = lse[(i - first) * count : (i + 1 - first) * count]
            lse_mine[i] = jnp.transpose(jnp.broadcast_to(column, (count, 128)))[0:1]
        for way in BOTH:
            for one in opposite(way) if first == 0 else plain(way):
                one.start()
    plan.now += 1.5

    def value_to_out():
        weight_loads[1].wait()
        return split(dot3(split(jnp.transpose(out_in[...])), columns_of(2)))

    value_out = plan.run(2.0, value_to_out, "qkv last")
    plan.upto(1e9)
    lane_row = iota((1, 128), 1)
    for way in BOTH:
        for one in opposite(way):
            one.wait_recv()
        at = 1 + way
        own, theirs = lse_mine[at], relay_lse[way]
        both = jnp.maximum(own, theirs)
        both = both + jnp.log(jnp.exp(own - both) + jnp.exp(theirs - both))
        rows_of_way = slice(way * part_rows, (way + 1) * part_rows)
        joint[way] = (
            partial[at, half_rows[way]] * across(as_column(jnp.exp(own - both))[rows_of_way])
            + relay[way] * across(as_column(jnp.exp(theirs - both))[rows_of_way])
        )
        joint_lse[way] = jnp.where(lane_row // part_rows == way, both, own)
        for one in joined(way):
            one.start()

    proj_w.finish()
    qkv_w.finish()
    for one in halo_copies:
        one.wait_send()
    for one in (over_x, over_z, over_y, tokens_x, tokens_z):
        one.finish()
    slab_copy(tm).wait_send()
    key_ring.finish()
    query_ring.finish()
    for way in BOTH:
        for one in (*plain(way), *joined(way)):
            one.wait_recv()
    given = [(lse_mine[3], partial[3])] + [(parts_lse[way], parts[way]) for way in BOTH]
    highest_lse = functools.reduce(jnp.maximum, [lse for lse, _ in given])
    shares = [jnp.exp(lse - highest_lse) for lse, _ in given]
    whole = functools.reduce(jnp.add, shares)
    merged = jnp.zeros((count, width), f32)
    for share, (_, value) in zip(shares, given):
        merged = merged + value * across(as_column(share / whole))
    encoded = tokens[...] + jnp.transpose(dot3_turned(split(merged), value_out))
    out[...] = encoded.reshape(out.shape)

    for way in BOTH:
        for one in (*opposite(way), *plain(way), *joined(way)):
            one.wait_send()


def shards(z_count, tm_count, features, norm_gain, conv_weight, proj_weight, attn_gain, qkv_weight, out_weight):
    frames, height, columns, channels = features.shape
    width = out_weight.shape[0]
    half_h, half_w = height // 2, columns // 2
    count = half_h * half_w
    steps = z_count // 2
    rows_count = z_count * X
    proj_rows, qkv_rows = proj_weight.shape[1], qkv_weight.shape[1] // 2
    wide, narrow = proj_weight.shape[0] // 4, qkv_weight.shape[0] // 4
    y_count = tm_count // 2
    far = y_count - 1 - (y_count - 1) // 3
    vmem = pltpu.VMEM
    dma = pltpu.SemaphoreType.DMA
    proj_sems = [dma((2, steps)), dma((2, steps)), dma((3, z_count)), dma((3, z_count)), dma((X,)), dma((X,)), dma((4, steps)),
                 dma((4, steps)), dma((2,)), dma((2,))]
    qkv_sems = [dma((1,)), dma((1,)), dma((1,)), dma((1,)), dma((1,)), dma((4, far)), dma((4, far)), dma((2, far)),
                dma((2, far)), dma((2,)), dma((2,))]
    scratch = [
        vmem((2, frames, height, columns, 128), f32), vmem((2, frames, height, columns, 128), f32),
        vmem(conv_weight.shape, f32), vmem(out_weight.shape, f32),
        vmem((X, 1, 128), f32), vmem((z_count, 1, 128), f32), vmem((tm_count, 1, 128), f32),
        vmem((X, 1, 128), f32), vmem((z_count, 1, 128), f32),
        vmem((2, 2, z_count, X, proj_rows, wide), f32),
        vmem((2, y_count, z_count // 2, X, qkv_rows, narrow), f32),
        vmem((4, half_h, 4 * half_w, channels), bf16), vmem((4, half_h, 4 * half_w, channels), bf16),
        vmem((frames, half_h, 4 * half_w, channels), f32),
        vmem((4, count, wide), bf16), vmem((4, count, wide), bf16),
        vmem((4, width, wide), bf16), vmem((4, width, wide), bf16),
        vmem((count, width), f32),
        vmem((z_count, count, width), f32),
        vmem((X, count, width), f32),
        vmem((X, count, width), bf16), vmem((X, count, width), bf16),
        vmem((X, count, width), f32), vmem((X, count, 1), f32), vmem((X, count, 1), f32),
        vmem((X, count, width), f32), vmem((X, 1, 128), f32),
        vmem((2, count // 2, width), f32), vmem((2, 1, 128), f32),
        vmem((2, count // 2, width), f32), vmem((2, 1, 128), f32),
        vmem((2, count, width), f32), vmem((2, 1, 128), f32),
        dma((6,)), dma((frames, half_h)), dma((frames, half_h)), dma((6,)), dma((6,)),
        *proj_sems, *qkv_sems,
        dma((8, steps)), dma((8, steps)), dma((2, X // 2)), dma((2, X // 2)), dma((5, 2)), dma((5, 2)),
    ]
    whole = pl.BlockSpec(memory_space=vmem)
    anywhere = pl.BlockSpec(memory_space=pl.ANY)
    return pl.pallas_call(
        functools.partial(kernel, z_count, tm_count),
        out_shape=jax.ShapeDtypeStruct((frames // 2, half_h, half_w, width), f32),
        in_specs=[anywhere, whole, anywhere, anywhere, whole, anywhere, anywhere],
        out_specs=whole,
        scratch_shapes=scratch,
        compiler_params=pltpu.CompilerParams(collective_id=0, has_side_effects=True, vmem_limit_bytes=56 * 2**20),
    )(features, norm_gain[None], conv_weight, proj_weight.T, attn_gain[None], qkv_weight.T, out_weight)


def solution(mesh):
    in_specs = (P("tm", "rows", None, None), P(), P(), P(None, "rows"), P(), P(None, "rows"), P())
    out_specs = P("tm", "rows", None, None)
    body = functools.partial(shards, mesh.shape["rows"] // X, mesh.shape["tm"])
    return jax.shard_map(body, mesh=mesh, in_specs=in_specs, out_specs=out_specs, check_vma=False)
```

```python
import functools
import math

import jax
import jax.numpy as jnp
from jax import lax
from jax.experimental import pallas as pl
from jax.experimental.pallas import tpu as pltpu
from jax.sharding import PartitionSpec as P

GROUPS = 32
X = 4
epsilon = 1e-06
f32, bf16 = jnp.float32, jnp.bfloat16
NN = (((1,), (0,)), ((), ()))
NT = (((1,), (1,)), ((), ()))
BOTH = (0, 1)


def split(value):
    high = value.astype(bf16)
    return high, (value - high.astype(f32)).astype(bf16)


def dot(a, b, dims):
    return lax.dot_general(a, b, dims, preferred_element_type=f32)


def dot3(a, b, dims=NN):
    rows = a[0].shape[0]
    if rows > 256:
        deep = (b[0], b[0], b[1])
        return dot(jnp.concatenate((a[0], a[1], a[0]), axis=1), jnp.concatenate(deep, axis=dims[0][1][0]), dims)
    by_high = dot(jnp.concatenate(a, axis=0), b[0], dims)
    return by_high[:rows] + (by_high[rows:] + dot(a[0], b[1], dims))


def exact(a, table):
    high = a.astype(bf16)
    rest = a - high.astype(f32)
    middle = rest.astype(bf16)
    low = (rest - middle.astype(f32)).astype(bf16)
    rows = a.shape[0]
    parts = jnp.concatenate([part.astype(f32) for part in (high, middle, low)] + [jnp.zeros_like(a)], axis=0).astype(bf16)
    by_part = dot(parts, table.astype(bf16), NN)
    return by_part[:rows] + (by_part[rows : 2 * rows] + by_part[2 * rows : 3 * rows])


def iota(shape, axis):
    return lax.broadcasted_iota(jnp.int32, shape, axis)


def rsqrt(value):
    return lax.rsqrt(value + epsilon)


def mod(value, size):
    return lax.rem(value + size, size)


class Plan:
    def __init__(self):
        self.now, self.waits = 0.0, []

    def expect(self, time, name, action):
        self.waits.append((time, len(self.waits), name, action))

    def upto(self, time):
        while True:
            due = [wait for wait in self.waits if wait[0] <= time]
            if not due:
                return
            first = min(due, key=lambda wait: wait[:2])
            self.waits.remove(first)
            first[3]()

    def need(self, name):
        times = [wait[0] for wait in self.waits if wait[2] == name]
        if times:
            self.now = max(self.now, max(times))
            self.upto(max(times))

    def run(self, duration, action, *needs):
        for name in needs:
            self.need(name)
        self.upto(self.now)
        result = action()
        self.now += duration
        return result


class Links:
    def __init__(self, z_count, x_count, tm_count):
        self.rows, self.tm = lax.axis_index("rows"), lax.axis_index("tm")
        self.z, self.x = lax.div(self.rows, x_count), lax.rem(self.rows, x_count)
        self.y, self.core = lax.div(self.tm, 2), lax.rem(self.tm, 2)
        self.z_count, self.x_count, self.y_count = z_count, x_count, tm_count // 2

    def z_device(self, by):
        return {"rows": mod(self.z + by, self.z_count) * self.x_count + self.x}

    def x_device(self, by):
        return {"rows": self.z * self.x_count + mod(self.x + by, self.x_count)}

    def y_device(self, by):
        return {"tm": mod(self.y + by, self.y_count) * 2 + self.core}

    def tm_device(self, by):
        return {"tm": mod(self.tm + by, 2 * self.y_count)}

    def sibling(self):
        return {"tm": self.tm + 1 - 2 * self.core}


def copy(src, dst, send, recv, device):
    return pltpu.make_async_remote_copy(
        src_ref=src, dst_ref=dst, send_sem=send, recv_sem=recv, device_id=device,
        device_id_type=pl.DeviceIdType.MESH,
    )


class Ring:
    def __init__(self, place, count, device, at, send, recv, reach, chunks=1, half=None, arrived=None):
        self.place, self.count, self.device, self.at, self.half = place, count, device, at, half
        self.send, self.recv, self.reach, self.chunks, self.arrived = send, recv, reach, chunks, arrived

    def moves(self, step, way, chunk):
        if step > self.reach[way]:
            return False
        shared = step == self.reach[0] == self.reach[1] and 2 * step == self.count
        return not shared or self.chunks == 1 or chunk // (self.chunks // 2) == way

    def ref(self, away, step, way, chunk):
        ref = self.at(mod(self.place + away, self.count), chunk)
        return self.half(ref, way) if self.half and 2 * step == self.count else ref

    def copy(self, step, way, chunk, away):
        ref = self.ref(away, step, way, chunk)
        at = (way * self.chunks + chunk, step - 1)
        return copy(ref, ref, self.send.at[at], self.recv.at[at], self.device(1 if way == 0 else -1))

    def outgoing(self, step, way, chunk):
        return self.copy(step, way, chunk, 1 - step if way == 0 else step - 1)

    def start(self, way, chunk):
        self.outgoing(1, way, chunk).start()

    def step(self, step, way, chunk):
        if not self.moves(step, way, chunk):
            return
        away = -step if way == 0 else step
        self.copy(step, way, chunk, away).wait_recv()
        if self.moves(step + 1, way, chunk):
            self.outgoing(step + 1, way, chunk).start()
        if self.arrived:
            self.arrived(self.ref(away, step, way, chunk))

    def each(self):
        for step in range(1, max(self.reach) + 1):
            for chunk in range(self.chunks):
                for way in BOTH:
                    if self.moves(step, way, chunk):
                        yield step, way, chunk

    def finish(self):
        for step, way, chunk in self.each():
            self.outgoing(step, way, chunk).wait_send()


class Sums:
    def __init__(self, slots, index, per, size, device, send, recv):
        self.slots, self.index, self.per, self.size, self.device = slots, index, per, size, device
        self.send, self.recv = send, recv

    def copies(self, by):
        ref = self.slots.at[pl.ds(self.index * self.per, self.per)]
        return copy(ref, ref, self.send, self.recv, self.device(by))

    def everything(self):
        ref = self.slots.at[pl.ds(0, (self.size - 1) * self.per)]
        return copy(ref, ref, self.send, self.recv, self.device(1))

    def start(self):
        for by in range(1, self.size):
            self.copies(by).start()

    def wait(self):
        self.everything().wait_recv()

    def finish(self):
        self.everything().wait_send()


class Proj:
    def __init__(self, links, buf, sems):
        self.k, self.buf = links, buf
        az_s, az_r, self.ax_s, self.ax_r, self.bx_s, self.bx_r, bz_s, bz_r, self.c_s, self.c_r = sems
        self.core = links.core
        rows, xs, steps = buf.shape[4] // 2, links.x_count // 2, links.z_count // 2
        self.first = Ring(links.z, links.z_count, links.z_device, lambda z, chunk: buf.at[self.core, 0, z, links.x],
                          az_s, az_r, (steps, steps), 1, lambda ref, way: ref.at[pl.ds(way * rows, rows)])
        self.second = Ring(links.z, links.z_count, links.z_device,
                           lambda z, chunk: buf.at[self.core, 1, z, pl.ds(chunk * xs, xs)],
                           bz_s, bz_r, (steps, steps), 2, None, self.hand_second)
        self.steps = steps

    def block(self, away, x_away):
        return self.buf.at[self.core, 0, mod(self.k.z + away, self.k.z_count), mod(self.k.x + x_away, self.k.x_count)]

    def ax(self, kind, away, x_away):
        ref = self.block(away, x_away)
        up = self.goes_up(away) if kind == 2 else kind == 0
        at = (kind, away % self.k.z_count)
        return copy(ref, ref, self.ax_s.at[at], self.ax_r.at[at], self.k.x_device(1 if up else -1))

    def goes_up(self, away):
        return away % self.k.z_count < self.steps

    def a_out(self, away):
        for kind in range(2):
            self.ax(kind, away, 0).start()

    def a_on(self, away):
        for kind, x_away in enumerate((-1, 1)):
            self.ax(kind, away, x_away).wait_recv()
        self.ax(2, away, -1 if self.goes_up(away) else 1).start()

    def aways(self, n):
        return (0,) if n == 0 else (-n, n) if n < self.steps else (n,)

    def bx(self, by, away):
        ref = self.buf.at[self.core, 1, self.k.z, mod(self.k.x + away, self.k.x_count)]
        return copy(ref, ref, self.bx_s.at[by], self.bx_r.at[by], self.k.x_device(by))

    def hand(self, part, ref):
        return copy(ref, ref, self.c_s.at[part], self.c_r.at[part], self.k.sibling())

    def hand_second(self, ref):
        self.hand(1, ref).start()

    def start(self):
        for by in range(1, self.k.x_count):
            self.bx(by, 0).start()
        for way in BOTH:
            self.first.start(way, 0)
        self.a_out(0)

    def a_step(self, n):
        for way in BOTH:
            self.first.step(n, way, 0)
        for away in self.aways(n):
            self.a_out(away)

    def a_pass(self, n):
        for away in self.aways(n):
            self.a_on(away)

    def b_start(self):
        for by in range(1, self.k.x_count):
            self.bx(by, -by).wait_recv()
        for chunk in range(2):
            for way in BOTH:
                self.second.start(way, chunk)
        self.hand(1, self.buf.at[self.core, 1, self.k.z]).start()

    def b_step(self, n, chunk):
        for way in BOTH:
            self.second.step(n, way, chunk)

    def a_hand(self, by):
        self.hand(0, self.buf.at[self.core, 0, :, mod(self.k.x + by, self.k.x_count)]).start()

    def a_near(self):
        for by in (0, -1, 1):
            self.a_hand(by)

    def a_far(self):
        for away in range(self.k.z_count):
            self.ax(2, away, 2).wait_recv()
        self.a_hand(2)

    def wait(self, part):
        self.hand(part, self.buf.at[1 - self.core, part]).wait_recv()

    def finish(self):
        self.first.finish()
        self.second.finish()
        for by in range(1, self.k.x_count):
            self.bx(by, 0).wait_send()
        for away in range(self.k.z_count):
            for kind in range(3):
                self.ax(kind, away, 0).wait_send()
        for part in range(2):
            self.hand(part, self.buf.at[self.core, part]).wait_send()


class Qkv:
    def __init__(self, links, piece, buf, sems):
        self.k, self.buf, self.source = links, buf, piece
        self.load_s, self.x_s, self.x_r, self.z_s, self.z_r, e_s, e_r, l_s, l_r, self.c_s, self.c_r = sems
        self.zs, self.xs = buf.shape[2], buf.shape[3]
        self.early = early = self.zs * 3 // 4
        up = (links.y_count - 1) // 3
        reach = (up, links.y_count - 1 - up)
        half = self.xs // 2
        mine = lambda y, *rest: buf.at[(links.core, y, *rest)]
        self.first = Ring(links.y, links.y_count, links.y_device,
                          lambda y, c: mine(y, pl.ds(0, early), pl.ds(c * half, half)),
                          e_s, e_r, reach, 2, None, lambda ref: self.hand(0, ref).start())
        self.last = Ring(links.y, links.y_count, links.y_device, lambda y, c: mine(y, pl.ds(early, self.zs - early)),
                         l_s, l_r, reach, 1, None, lambda ref: self.hand(1, ref).start())
        self.sends = lax.rem(links.z, 2) == links.core
        self.zz = lax.div(links.z, 2)

    def load(self):
        return pltpu.make_async_copy(self.source, self.buf.at[self.k.core, self.k.y, self.zz, self.k.x], self.load_s.at[0])

    def preload(self):
        pl.when(self.sends)(lambda: self.load().start())

    def z_copy(self, by):
        ref = self.buf.at[self.k.core, self.k.y, self.zz, self.k.x]
        return copy(ref, ref, self.z_s.at[0], self.z_r.at[0], self.k.z_device(by))

    def x_copy(self, by):
        ref = self.buf.at[self.k.core, self.k.y, :, self.k.x]
        return copy(ref, ref, self.x_s.at[0], self.x_r.at[0], self.k.x_device(by))

    def x_all(self):
        ref = self.buf.at[self.k.core, self.k.y, :, pl.ds(0, self.xs - 1)]
        return copy(ref, ref, self.x_s.at[0], self.x_r.at[0], self.k.x_device(1))

    def start(self):
        @pl.when(self.sends)
        def _():
            self.load().wait()
            for by in range(1, self.k.z_count):
                self.z_copy(by).start()

    def across(self):
        def got(count):
            ref = self.buf.at[self.k.core, self.k.y, pl.ds(0, count), self.k.x]
            copy(ref, ref, self.z_s.at[0], self.z_r.at[0], self.k.z_device(1)).wait_recv()

        pl.when(self.sends)(lambda: got(self.zs - 1))
        pl.when(jnp.logical_not(self.sends))(lambda: got(self.zs))
        for by in range(1, self.xs):
            self.x_copy(by).start()

    def collect(self):
        self.x_all().wait_recv()
        for chunk in range(2):
            self.first.start(1, chunk)
        for part in range(2):
            self.hand(part, self.part_of(part, self.k.core, self.k.y)).start()

    def up(self):
        for chunk in range(2):
            self.first.start(0, chunk)

    def rest(self):
        for way in BOTH:
            self.last.start(way, 0)

    def hand(self, part, ref):
        return copy(ref, ref, self.c_s.at[part], self.c_r.at[part], self.k.sibling())

    def part_of(self, part, core, y):
        zs = pl.ds(0, self.early) if part == 0 else pl.ds(self.early, self.zs - self.early)
        return self.buf.at[core, y, zs]

    def all_of(self, part, core):
        return self.hand(part, self.part_of(part, core, slice(None)))

    def wait(self, part):
        self.all_of(part, 1 - self.k.core).wait_recv()

    def finish(self):
        self.first.finish()
        self.last.finish()
        for part in range(2):
            self.all_of(part, self.k.core).wait_send()

        self.x_all().wait_send()

        @pl.when(self.sends)
        def _():
            ref = self.buf.at[self.k.core, pl.ds(0, self.k.z_count - 1), 0, self.k.x]
            copy(ref, ref, self.z_s.at[0], self.z_r.at[0], self.k.z_device(1)).wait_send()


def kernel(
    z_count, tm_count,
    features, gain, conv, proj, attn_gain, qkv, out_weight, out,
    feat, halo, conv_in, out_in, x_sums, z_sums, slab_sums, token_x, token_z,
    proj_all, qkv_all, act_hi, act_lo, residual, band_hi, band_lo, proj_hi, proj_lo, tokens, keys, queries, q_hi, q_lo, total, top, mass,
    partial, lse_mine, relay, relay_lse, joint, joint_lse, parts, parts_lse,
    load_s, halo_s, halo_r, sum_s, sum_r, *sems,
):
    proj_sems, qkv_sems, sems = sems[:10], sems[10:21], sems[21:]
    key_s, key_r, query_s, query_r, part_s, part_r = sems
    k = Links(z_count, X, tm_count)
    rows_count = z_count * X
    tm, z, x = k.tm, k.z, k.x
    frames, height, columns, channels = features.shape
    half_w = columns // 2
    count = (height // 2) * half_w
    width = tokens.shape[1]
    wide = proj_all.shape[5]
    per_half, narrow = qkv_all.shape[4:]
    steps = z_count // 2
    plan = Plan()

    loads = [
        pltpu.make_async_copy(features.at[:, :, :, pl.ds(128 * half, 128)], feat.at[half], load_s.at[half])
        for half in range(2)
    ]
    for load in loads:
        load.start()
    barrier = pltpu.get_barrier_semaphore()
    peers = (
        [k.x_device(by) for by in range(1, X)] + [k.z_device(by) for by in range(1, z_count)]
        + [k.tm_device(by) for by in range(1, tm_count)]
    )
    for peer in peers:
        pl.semaphore_signal(barrier, inc=1, device_id=peer, device_id_type=pl.DeviceIdType.MESH)

    quarters = [
        pltpu.make_async_copy(
            proj.at[:, pl.ds(pl.multiple_of((2 * k.core + part) * wide, wide), wide)],
            proj_all.at[k.core, part, z, x], load_s.at[2 + part],
        )
        for part in range(2)
    ]
    piece = qkv.at[
        pl.ds(pl.multiple_of(lax.div(k.y, 4) * per_half, 8), per_half),
        pl.ds(pl.multiple_of(lax.rem(k.y, 4) * narrow, narrow), narrow),
    ]
    proj_w = Proj(k, proj_all, proj_sems)
    qkv_w = Qkv(k, piece, qkv_all, qkv_sems)
    for one in quarters:
        one.start()
    qkv_w.preload()
    weight_loads = [
        pltpu.make_async_copy(conv, conv_in, load_s.at[4]), pltpu.make_async_copy(out_weight, out_in, load_s.at[5])
    ]
    for one in weight_loads:
        one.start()

    lane = iota((8, 128), 1)
    row = iota((8, 128), 0)
    sums = []
    for load in loads:
        load.wait()
    for frame in range(frames):
        values = jnp.concatenate([feat[half, frame].reshape(height * columns, 128) for half in range(2)], axis=1)
        sums += [jnp.sum(values, axis=0, keepdims=True), jnp.sum(values * values, axis=0, keepdims=True)]
    stacked = jnp.concatenate(sums + [jnp.zeros((4, channels), f32)], axis=0)
    per_group = channels // GROUPS
    fold = (iota((channels, 128), 1) % GROUPS == iota((channels, 128), 0) // per_group).astype(f32)

    def lanes_of(rows_of_sums, table):
        return jnp.sum(jnp.where(lane // GROUPS == row, exact(rows_of_sums, table), 0.0), axis=0, keepdims=True)

    slab_sums[tm] = lanes_of(stacked, fold)
    for one in quarters:
        one.wait()

    def exchange(slots, index, per, size, device, n):
        return Sums(slots, index, per, size, device, sum_s.at[n], sum_r.at[n])

    over_tm = exchange(slab_sums, tm, 1, tm_count, k.tm_device, 0)
    over_x = exchange(x_sums, x, 1, X, k.x_device, 1)
    over_z = exchange(z_sums, z, 1, z_count, k.z_device, 2)
    tokens_z = exchange(token_z, z, 1, z_count, k.z_device, 3)
    tokens_x = exchange(token_x, x, 1, X, k.x_device, 4)

    pl.semaphore_wait(barrier, len(peers))
    over_tm.start()
    pairs = height // 2

    def halo_copy(f, h):
        at = (slice(None), f, pl.ds(2 * h, 2))
        return copy(feat.at[at], halo.at[at], halo_s.at[f, h], halo_r.at[f, h], {"tm": mod(tm + 1, tm_count)})

    halo_copies = [halo_copy(f, h) for h in range(pairs) for f in range(frames)]
    for one in halo_copies:
        one.start()
    proj_w.start()
    qkv_w.start()
    plan.now = 4.0

    def summed_tm():
        over_tm.wait()
        x_sums[x] = jnp.concatenate([slab_sums[i] for i in range(tm_count)], axis=0)
        over_x.start()

    def summed_x():
        over_x.wait()
        z_sums[z] = jnp.sum(x_sums[...], axis=0)
        over_z.start()

    plan.expect(6.4, "tm", summed_tm)
    plan.expect(9.0, "x", summed_x)
    plan.expect(7.8, "qkv x", qkv_w.across)
    plan.expect(6.8, "b", proj_w.b_start)
    plan.expect(7.5, "a", functools.partial(proj_w.a_pass, 0))
    for n in range(1, steps + 1):
        plan.expect(4.0 + 2.7 * n, "a", functools.partial(proj_w.a_step, n))
        plan.expect(7.0 + 2.7 * n, "a", functools.partial(proj_w.a_pass, n))
        for chunk in range(2):
            plan.expect(8.8 + 1.8 * (2 * n - 1 + chunk), "b", functools.partial(proj_w.b_step, n, chunk))
    plan.expect(7.1 + 2.7 * steps, "a", proj_w.a_near)
    plan.expect(10.0 + 2.7 * steps, "a far", proj_w.a_far)
    plan.expect(10.6, "collect", qkv_w.collect)
    plan.expect(12.0, "z", over_z.wait)
    for h in range(pairs):
        for frame in range(frames):
            plan.expect(11.8 + 5.8 * h + 0.1 * frame, f"halo{h}", halo_copy(frame, h).wait_recv)
    plan.expect(6.1 + 5.8 * pairs, "up", qkv_w.up)
    qkv_done = 12.6
    for step, way, chunk in qkv_w.first.each():
        time = (12.6 if way else 8.1 + 5.8 * pairs) + 1.7 * (2 * step - 1 + chunk)
        qkv_done = max(qkv_done, time)
        plan.expect(time, "qkv", functools.partial(qkv_w.first.step, step, way, chunk))
    plan.expect(qkv_done + 0.1, "rest", qkv_w.rest)
    plan.expect(qkv_done + 3.6, "qkv", functools.partial(qkv_w.wait, 0))
    for step, way, chunk in qkv_w.last.each():
        plan.expect(qkv_done + 5.0 + 2.5 * step, "qkv last", functools.partial(qkv_w.last.step, step, way, chunk))
    plan.expect(qkv_done + 7.0 + 2.5 * max(qkv_w.last.reach), "qkv last", functools.partial(qkv_w.wait, 1))

    def split_taps():
        weight_loads[0].wait()
        return [split(conv_in[lag]) for lag in range(3)]

    taps = plan.run(0.4, split_taps)

    def statistics():
        everything = jnp.sum(z_sums[...], axis=0)
        slab = iota(everything.shape, 0)

        def of(these):
            return jnp.sum(jnp.where(these, everything, 0.0), axis=0, keepdims=True)

        earlier, previous, own = of(slab < tm - 1), of(slab == tm - 1), of(slab == tm)
        kind, upto = row % 2, row // 2
        lane_kind, lane_frame = lane // GROUPS % 2, lane // GROUPS // 2
        mine = lane_kind == kind
        running = (
            jnp.where(mine, earlier, 0.0)
            + jnp.where(mine & (lane_frame <= upto), previous, 0.0)
            + jnp.where(mine & (lane_frame <= upto - 2), own, 0.0)
        )
        unfold = (iota((128, channels), 0) % GROUPS == iota((128, channels), 1) // per_group).astype(f32)
        running = exact(running, unfold)
        means, scales = [], []
        for i in range(4):
            position = jnp.maximum(tm * frames + i - 1, 1).astype(f32)
            cells = position * float(rows_count * height * columns * per_group)
            mean = running[2 * i : 2 * i + 1] / cells
            variance = running[2 * i + 1 : 2 * i + 2] / cells - mean * mean
            means.append(mean)
            scales.append(rsqrt(variance))
        return means, scales

    means, scales = plan.run(0.6, statistics, "z")
    norm_gain = gain[...]

    def cells_of(src, frame, h, b, c):
        return jnp.concatenate([src[half, frame, 2 * h + b, pl.ds(c, half_w, stride=2), :] for half in range(2)], axis=1)

    def activate(src, frame, h, at):
        for b in range(2):
            for c in range(2):
                value = (cells_of(src, frame, h, b, c) - means[at]) * scales[at] * norm_gain
                value = value / (1.0 + jnp.exp(-value))
                if at < 2:
                    value = jnp.where(tm > 0, value, 0.0)
                high, low = split(value)
                place = pl.ds((2 * b + c) * half_w, half_w)
                act_hi[at, h, place] = high
                act_lo[at, h, place] = low

    def activated(at, h):
        return tuple(ref[at, h].reshape(-1, channels) for ref in (act_hi, act_lo))

    def convolve(frame, h, terms, first=False):
        value = functools.reduce(jnp.add, [dot3(activated(at, h), taps[lag]) for at, lag in terms])
        value = value.reshape((-1, 4 * half_w, channels))
        residual[frame, h] = value if first else residual[frame, h] + value

    every = pl.ds(0, pairs)
    for frame in range(frames):
        plan.run(0.7, lambda: [activate(feat, frame, h, 2 + frame) for h in range(pairs)])
    plan.run(0.5, lambda: convolve(0, every, [(2, 0)], True))
    plan.run(1.0, lambda: convolve(1, every, [(3, 0), (2, 1)], True))
    def split_quarter(half, part):
        at = 2 * half + part
        high, low = split(proj_all[half, part].reshape(width, wide))
        proj_hi[at] = high
        proj_lo[at] = low

    for h in range(pairs):
        for frame in range(frames):
            plan.run(0.35, lambda: activate(halo, frame, h, frame), f"halo{h}")
        plan.run(0.6, lambda: convolve(0, pl.ds(h, 1), [(1, 1), (0, 2)]))
        plan.run(0.3, lambda: convolve(1, pl.ds(h, 1), [(1, 2)]))

    def haar():
        bands = [
            jnp.concatenate([
                residual[a, h, pl.ds((2 * b + c) * half_w, half_w)] + cells_of(feat, a, h, b, c) for h in range(pairs)
            ], axis=0)
            for a in range(2) for b in range(2) for c in range(2)
        ]
        for bit in (4, 2, 1):
            bands = [
                bands[j] + bands[j | bit] if not j & bit else bands[j ^ bit] - bands[j] for j in range(8)
            ]
        bands = [split(band * (1.0 / math.sqrt(8.0))) for band in bands]
        per_quarter = wide // channels
        for quarter in range(4):
            ours = bands[quarter * per_quarter : (quarter + 1) * per_quarter]
            band_hi[quarter] = jnp.concatenate([band[0] for band in ours], axis=1)
            band_lo[quarter] = jnp.concatenate([band[1] for band in ours], axis=1)

    plan.run(0.7, haar)

    def quarter_of(half, part):
        at = 2 * half + part
        return dot3((band_hi[at], band_lo[at]), (proj_hi[at], proj_lo[at]), NT)

    other = 1 - k.core
    plan.run(0.3, lambda: split_quarter(k.core, 0), "a far")
    made = plan.run(0.5, lambda: quarter_of(k.core, 0))
    proj_w.wait(0)
    plan.run(0.3, lambda: split_quarter(other, 0))
    made = made + plan.run(0.5, lambda: quarter_of(other, 0))
    plan.run(0.3, lambda: split_quarter(k.core, 1), "b")
    made = made + plan.run(0.5, lambda: quarter_of(k.core, 1))
    proj_w.wait(1)
    plan.run(0.3, lambda: split_quarter(other, 1))
    made = made + plan.run(0.5, lambda: quarter_of(other, 1))
    tokens[...] = made
    keys[z] = made
    queries[x] = made

    part_rows = count // 2
    key_chunks = 4
    key_rows = count // key_chunks
    key_ring = Ring(z, z_count, k.z_device, lambda at, c: keys.at[at, pl.ds(c * key_rows, key_rows)],
                    key_s, key_r, (steps, steps), key_chunks)
    query_ring = Ring(x, X, k.x_device, lambda at, c: queries.at[at], query_s, query_r, (X // 2, X // 2), 1,
                      lambda ref, way: ref.at[pl.ds(way * part_rows, part_rows)])
    token_group = width // GROUPS
    sums = jnp.concatenate(
        [jnp.sum(made, axis=0, keepdims=True), jnp.sum(made * made, axis=0, keepdims=True), jnp.zeros((6, width), f32)],
        axis=0,
    )
    fold = (iota((width, 128), 1) % GROUPS == iota((width, 128), 0) // token_group).astype(f32)
    token_z[z] = lanes_of(sums, fold)
    tokens_z.start()
    for chunk in range(key_chunks):
        for way in BOTH:
            key_ring.start(way, chunk)
    begin = plan.now
    for step, way, chunk in key_ring.each():
        turn = chunk if step < steps else chunk % (key_chunks // 2)
        plan.expect(begin + 2.0 + 1.5 * (key_chunks * (step - 1) + turn + 1), f"key{step}",
                    functools.partial(key_ring.step, step, way, chunk))

    def token_summed_z():
        tokens_z.wait()
        token_x[x] = jnp.sum(token_z[...], axis=0)
        tokens_x.start()
        for way in BOTH:
            query_ring.start(way, 0)

    plan.expect(begin + 2.5, "tokens z", token_summed_z)
    plan.expect(begin + 5.0, "tokens x", tokens_x.wait)
    for step, way, chunk in query_ring.each():
        plan.expect(begin + 4.9 * step + 5.2, "queries", functools.partial(query_ring.step, step, way, chunk))

    def token_statistics():
        all_sums = jnp.sum(token_x[...], axis=0)
        unfold = (iota((128, width), 0) % GROUPS == iota((128, width), 1) // token_group).astype(f32)
        spread_sums = exact(jnp.where(lane // GROUPS == row, all_sums, 0.0), unfold)
        token_count = float(rows_count * count * token_group)
        mean = spread_sums[0:1] / token_count
        return mean, rsqrt(spread_sums[1:2] / token_count - mean * mean)

    token_mean, token_scale = plan.run(0.6, token_statistics, "tokens x")
    token_gain = attn_gain[...]

    def normed(value):
        return split((value - token_mean) * token_scale * token_gain)

    def columns_of(block):
        lanes = []
        for lane_at in range(4):
            chunks = []
            for at in range(block * width // per_half, (block + 1) * width // per_half + 1):
                owner, part = at // 2, at % 2
                if owner < rows_count:
                    own_z, own_x = owner // X, owner % X
                    chunks.append(qkv_all[own_z % 2, 4 * part + lane_at, own_z // 2, own_x])
            skip = block * width - block * width // per_half * per_half
            lanes.append(jnp.concatenate(chunks, axis=0)[skip : skip + width])
        return split(jnp.concatenate(lanes, axis=1))

    def query_key_weight():
        query_weight = tuple(jnp.transpose(part.astype(f32)).astype(bf16) for part in columns_of(0))
        return split(dot3(query_weight, columns_of(1)) * (1.0 / math.sqrt(float(width))))

    order = (2, 1, 3, 0)

    def ask():
        asking = jnp.concatenate([queries[mod(x + by, X)] for by in order], axis=0)
        high, low = split(dot3(normed(asking), query_key))
        q_hi[...], q_lo[...] = high.reshape(q_hi.shape), low.reshape(q_lo.shape)

    query_key = plan.run(2.0, query_key_weight, "qkv")
    plan.run(1.5, ask, "queries")

    sets = [(0, -1, 1)] + [(-step, step) for step in range(2, steps)] + [(steps,)]

    def key_block(at):
        return normed(jnp.concatenate([keys[mod(z + away, z_count)] for away in sets[at]], axis=0))

    def rows_of(ref, at):
        return ref[at].reshape(-1, ref.shape[-1])

    def scores_of(at, block):
        return dot3((rows_of(q_hi, at), rows_of(q_lo, at)), block, NT)

    def attend(first, at, block, scores):
        here = jnp.max(scores, axis=1, keepdims=True)
        if first:
            weights = jnp.exp(scores - here)
            return here, jnp.sum(weights, axis=1, keepdims=True), dot3(split(weights), block)
        new_top = jnp.maximum(rows_of(top, at), here)
        fade = jnp.exp(rows_of(top, at) - new_top)
        weights = jnp.exp(scores - new_top)
        new_mass = rows_of(mass, at) * fade + jnp.sum(weights, axis=1, keepdims=True)
        return new_top, new_mass, rows_of(total, at) * fade + dot3(split(weights), block)

    def attend_all(step, block, scores):
        for ref, value in zip((top, mass, total), attend(step == 0, slice(None), block, scores)):
            ref[...] = value.reshape(ref.shape)

    for step in range(len(sets) - 1):
        block = plan.run(0.2, lambda: key_block(step), f"key{step + 1}")
        scores = plan.run(1.2 if step == 0 else 0.9, lambda: scores_of(slice(None), block))
        plan.run(1.6 if step == 0 else 1.2, lambda: attend_all(step, block, scores))

    half_rows = [pl.ds(way * part_rows, part_rows) for way in BOTH]
    toward = (1, -1)

    def send(kind, way, src, dst):
        return copy(src, dst, part_s.at[kind, way], part_r.at[kind, way], k.x_device(toward[way]))

    def opposite(way):
        return (send(0, way, partial.at[0, half_rows[way]], relay.at[way]),
                send(1, way, lse_mine.at[0], relay_lse.at[way]))

    def plain(way):
        return (send(2, way, partial.at[1 + way, half_rows[1 - way]], parts.at[way, half_rows[1 - way]]),)

    def joined(way):
        return (send(3, way, joint.at[way], parts.at[way, half_rows[way]]), send(4, way, joint_lse.at[way], parts_lse.at[way]))

    def as_column(lanes):
        return jnp.transpose(jnp.broadcast_to(lanes, (count, 128)))

    def across(column):
        return jnp.concatenate([column] * (width // 128), axis=1)

    plan.need(f"key{steps}")
    block = key_block(-1)
    for first, last in ((0, 1), (1, X)):
        at = slice(first, last)
        last_top, last_mass, value = attend(False, at, block, scores_of(at, block))
        partial[at] = (value / last_mass).reshape(last - first, count, width)
        lse = last_top + jnp.log(last_mass)
        for i in range(first, last):
            column = lse[(i - first) * count : (i + 1 - first) * count]
            lse_mine[i] = jnp.transpose(jnp.broadcast_to(column, (count, 128)))[0:1]
        for way in BOTH:
            for one in opposite(way) if first == 0 else plain(way):
                one.start()
    plan.now += 1.5

    def value_to_out():
        weight_loads[1].wait()
        value_weight = tuple(jnp.transpose(part.astype(f32)).astype(bf16) for part in columns_of(2))
        return split(dot3(value_weight, split(out_in[...])))

    value_out = plan.run(2.0, value_to_out, "qkv last")
    plan.upto(1e9)
    lane_row = iota((1, 128), 1)
    for way in BOTH:
        for one in opposite(way):
            one.wait_recv()
        at = 1 + way
        own, theirs = lse_mine[at], relay_lse[way]
        both = jnp.maximum(own, theirs)
        both = both + jnp.log(jnp.exp(own - both) + jnp.exp(theirs - both))
        rows_of_way = slice(way * part_rows, (way + 1) * part_rows)
        joint[way] = (
            partial[at, half_rows[way]] * across(as_column(jnp.exp(own - both))[rows_of_way])
            + relay[way] * across(as_column(jnp.exp(theirs - both))[rows_of_way])
        )
        joint_lse[way] = jnp.where(lane_row // part_rows == way, both, own)
        for one in joined(way):
            one.start()

    proj_w.finish()
    qkv_w.finish()
    for one in halo_copies:
        one.wait_send()
    for one in (over_tm, over_x, over_z, tokens_x, tokens_z):
        one.finish()
    key_ring.finish()
    query_ring.finish()
    for way in BOTH:
        for one in (*plain(way), *joined(way)):
            one.wait_recv()
    given = [(lse_mine[3], partial[3])] + [(parts_lse[way], parts[way]) for way in BOTH]
    highest_lse = functools.reduce(jnp.maximum, [lse for lse, _ in given])
    shares = [jnp.exp(lse - highest_lse) for lse, _ in given]
    whole = functools.reduce(jnp.add, shares)
    merged = jnp.zeros((count, width), f32)
    for share, (_, value) in zip(shares, given):
        merged = merged + value * across(as_column(share / whole))
    encoded = tokens[...] + dot3(split(merged), value_out)
    out[...] = encoded.reshape(out.shape)

    for way in BOTH:
        for one in (*opposite(way), *plain(way), *joined(way)):
            one.wait_send()


def shards(z_count, tm_count, features, norm_gain, conv_weight, proj_weight, attn_gain, qkv_weight, out_weight):
    frames, height, columns, channels = features.shape
    width = out_weight.shape[0]
    half_h, half_w = height // 2, columns // 2
    count = half_h * half_w
    steps = z_count // 2
    rows_count = z_count * X
    proj_rows, qkv_rows = proj_weight.shape[1], qkv_weight.shape[1] // 2
    wide, narrow = proj_weight.shape[0] // 4, qkv_weight.shape[0] // 4
    y_count = tm_count // 2
    far = y_count - 1 - (y_count - 1) // 3
    vmem = pltpu.VMEM
    dma = pltpu.SemaphoreType.DMA
    proj_sems = [dma((2, steps)), dma((2, steps)), dma((3, z_count)), dma((3, z_count)), dma((X,)), dma((X,)), dma((4, steps)),
                 dma((4, steps)), dma((2,)), dma((2,))]
    qkv_sems = [dma((1,)), dma((1,)), dma((1,)), dma((1,)), dma((1,)), dma((4, far)), dma((4, far)), dma((2, far)),
                dma((2, far)), dma((2,)), dma((2,))]
    scratch = [
        vmem((2, frames, height, columns, 128), f32), vmem((2, frames, height, columns, 128), f32),
        vmem(conv_weight.shape, f32), vmem(out_weight.shape, f32),
        vmem((X, tm_count, 128), f32), vmem((z_count, tm_count, 128), f32), vmem((tm_count, 1, 128), f32),
        vmem((X, 1, 128), f32), vmem((z_count, 1, 128), f32),
        vmem((2, 2, z_count, X, proj_rows, wide), f32),
        vmem((2, y_count, z_count // 2, X, qkv_rows, narrow), f32),
        vmem((4, half_h, 4 * half_w, channels), bf16), vmem((4, half_h, 4 * half_w, channels), bf16),
        vmem((frames, half_h, 4 * half_w, channels), f32),
        vmem((4, count, wide), bf16), vmem((4, count, wide), bf16),
        vmem((4, width, wide), bf16), vmem((4, width, wide), bf16),
        vmem((count, width), f32),
        vmem((z_count, count, width), f32),
        vmem((X, count, width), f32),
        vmem((X, count, width), bf16), vmem((X, count, width), bf16),
        vmem((X, count, width), f32), vmem((X, count, 1), f32), vmem((X, count, 1), f32),
        vmem((X, count, width), f32), vmem((X, 1, 128), f32),
        vmem((2, count // 2, width), f32), vmem((2, 1, 128), f32),
        vmem((2, count // 2, width), f32), vmem((2, 1, 128), f32),
        vmem((2, count, width), f32), vmem((2, 1, 128), f32),
        dma((6,)), dma((frames, half_h)), dma((frames, half_h)), dma((6,)), dma((6,)),
        *proj_sems, *qkv_sems,
        dma((8, steps)), dma((8, steps)), dma((2, X // 2)), dma((2, X // 2)), dma((5, 2)), dma((5, 2)),
    ]
    whole = pl.BlockSpec(memory_space=vmem)
    anywhere = pl.BlockSpec(memory_space=pl.ANY)
    return pl.pallas_call(
        functools.partial(kernel, z_count, tm_count),
        out_shape=jax.ShapeDtypeStruct((frames // 2, half_h, half_w, width), f32),
        in_specs=[anywhere, whole, anywhere, anywhere, whole, anywhere, anywhere],
        out_specs=whole,
        scratch_shapes=scratch,
        compiler_params=pltpu.CompilerParams(collective_id=0, has_side_effects=True, vmem_limit_bytes=56 * 2**20),
    )(features, norm_gain[None], conv_weight, proj_weight.T, attn_gain[None], qkv_weight.T, out_weight)


def solution(mesh):
    in_specs = (P("tm", "rows", None, None), P(), P(), P(None, "rows"), P(), P(None, "rows"), P())
    out_specs = P("tm", "rows", None, None)
    body = functools.partial(shards, mesh.shape["rows"] // X, mesh.shape["tm"])
    return jax.shard_map(body, mesh=mesh, in_specs=in_specs, out_specs=out_specs, check_vma=False)
```

```python
import functools
import math

import jax
import jax.numpy as jnp
from jax import lax
from jax.experimental import pallas as pl
from jax.experimental.pallas import tpu as pltpu
from jax.sharding import PartitionSpec as P

GROUPS = 32
X = 4
epsilon = 1e-06
f32, bf16 = jnp.float32, jnp.bfloat16
NN = (((1,), (0,)), ((), ()))
NT = (((1,), (1,)), ((), ()))
BOTH = (0, 1)


def split(value):
    high = value.astype(bf16)
    return high, (value - high.astype(f32)).astype(bf16)


def dot(a, b, dims):
    return lax.dot_general(a, b, dims, preferred_element_type=f32)


def dot3(a, b, dims=NN):
    rows = a[0].shape[0]
    if rows > 256:
        deep = (b[0], b[0], b[1])
        return dot(jnp.concatenate((a[0], a[1], a[0]), axis=1), jnp.concatenate(deep, axis=dims[0][1][0]), dims)
    by_high = dot(jnp.concatenate(a, axis=0), b[0], dims)
    return by_high[:rows] + (by_high[rows:] + dot(a[0], b[1], dims))


def exact(a, table):
    high = a.astype(bf16)
    rest = a - high.astype(f32)
    middle = rest.astype(bf16)
    low = (rest - middle.astype(f32)).astype(bf16)
    rows = a.shape[0]
    parts = jnp.concatenate([part.astype(f32) for part in (high, middle, low)] + [jnp.zeros_like(a)], axis=0).astype(bf16)
    by_part = dot(parts, table.astype(bf16), NN)
    return by_part[:rows] + (by_part[rows : 2 * rows] + by_part[2 * rows : 3 * rows])


def iota(shape, axis):
    return lax.broadcasted_iota(jnp.int32, shape, axis)


def rsqrt(value):
    return lax.rsqrt(value + epsilon)


def mod(value, size):
    return lax.rem(value + size, size)


class Plan:
    def __init__(self):
        self.now, self.waits = 0.0, []

    def expect(self, time, name, action):
        self.waits.append((time, len(self.waits), name, action))

    def upto(self, time):
        while True:
            due = [wait for wait in self.waits if wait[0] <= time]
            if not due:
                return
            first = min(due, key=lambda wait: wait[:2])
            self.waits.remove(first)
            first[3]()

    def need(self, name):
        times = [wait[0] for wait in self.waits if wait[2] == name]
        if times:
            self.now = max(self.now, max(times))
            self.upto(max(times))

    def run(self, duration, action, *needs):
        for name in needs:
            self.need(name)
        self.upto(self.now)
        result = action()
        self.now += duration
        return result


class Links:
    def __init__(self, z_count, x_count, tm_count):
        self.rows, self.tm = lax.axis_index("rows"), lax.axis_index("tm")
        self.z, self.x = lax.div(self.rows, x_count), lax.rem(self.rows, x_count)
        self.y, self.core = lax.div(self.tm, 2), lax.rem(self.tm, 2)
        self.z_count, self.x_count, self.y_count = z_count, x_count, tm_count // 2

    def z_device(self, by):
        return {"rows": mod(self.z + by, self.z_count) * self.x_count + self.x}

    def x_device(self, by):
        return {"rows": self.z * self.x_count + mod(self.x + by, self.x_count)}

    def y_device(self, by):
        return {"tm": mod(self.y + by, self.y_count) * 2 + self.core}

    def tm_device(self, by):
        return {"tm": mod(self.tm + by, 2 * self.y_count)}

    def sibling(self):
        return {"tm": self.tm + 1 - 2 * self.core}


def copy(src, dst, send, recv, device):
    return pltpu.make_async_remote_copy(
        src_ref=src, dst_ref=dst, send_sem=send, recv_sem=recv, device_id=device,
        device_id_type=pl.DeviceIdType.MESH,
    )


class Ring:
    def __init__(self, place, count, device, at, send, recv, reach, chunks=1, half=None, arrived=None):
        self.place, self.count, self.device, self.at, self.half = place, count, device, at, half
        self.send, self.recv, self.reach, self.chunks, self.arrived = send, recv, reach, chunks, arrived

    def moves(self, step, way, chunk):
        if step > self.reach[way]:
            return False
        shared = step == self.reach[0] == self.reach[1] and 2 * step == self.count
        return not shared or self.chunks == 1 or chunk // (self.chunks // 2) == way

    def ref(self, away, step, way, chunk):
        ref = self.at(mod(self.place + away, self.count), chunk)
        return self.half(ref, way) if self.half and 2 * step == self.count else ref

    def copy(self, step, way, chunk, away):
        ref = self.ref(away, step, way, chunk)
        at = (way * self.chunks + chunk, step - 1)
        return copy(ref, ref, self.send.at[at], self.recv.at[at], self.device(1 if way == 0 else -1))

    def outgoing(self, step, way, chunk):
        return self.copy(step, way, chunk, 1 - step if way == 0 else step - 1)

    def start(self, way, chunk):
        self.outgoing(1, way, chunk).start()

    def step(self, step, way, chunk):
        if not self.moves(step, way, chunk):
            return
        away = -step if way == 0 else step
        self.copy(step, way, chunk, away).wait_recv()
        if self.moves(step + 1, way, chunk):
            self.outgoing(step + 1, way, chunk).start()
        if self.arrived:
            self.arrived(self.ref(away, step, way, chunk))

    def each(self):
        for step in range(1, max(self.reach) + 1):
            for chunk in range(self.chunks):
                for way in BOTH:
                    if self.moves(step, way, chunk):
                        yield step, way, chunk

    def finish(self):
        for step, way, chunk in self.each():
            self.outgoing(step, way, chunk).wait_send()


class Sums:
    def __init__(self, slots, index, per, size, device, send, recv):
        self.slots, self.index, self.per, self.size, self.device = slots, index, per, size, device
        self.send, self.recv = send, recv

    def copies(self, by):
        ref = self.slots.at[pl.ds(self.index * self.per, self.per)]
        return copy(ref, ref, self.send, self.recv, self.device(by))

    def everything(self):
        ref = self.slots.at[pl.ds(0, (self.size - 1) * self.per)]
        return copy(ref, ref, self.send, self.recv, self.device(1))

    def start(self):
        for by in range(1, self.size):
            self.copies(by).start()

    def wait(self):
        self.everything().wait_recv()

    def finish(self):
        self.everything().wait_send()


class Proj:
    def __init__(self, links, buf, sems):
        self.k, self.buf = links, buf
        az_s, az_r, self.ax_s, self.ax_r, self.bx_s, self.bx_r, bz_s, bz_r, self.c_s, self.c_r = sems
        self.core = links.core
        rows, xs, steps = buf.shape[4] // 2, links.x_count // 2, links.z_count // 2
        self.first = Ring(links.z, links.z_count, links.z_device, lambda z, chunk: buf.at[self.core, 0, z, links.x],
                          az_s, az_r, (steps, steps), 1, lambda ref, way: ref.at[pl.ds(way * rows, rows)])
        self.second = Ring(links.z, links.z_count, links.z_device,
                           lambda z, chunk: buf.at[self.core, 1, z, pl.ds(chunk * xs, xs)],
                           bz_s, bz_r, (steps, steps), 2, None, self.hand_second)
        self.steps = steps

    def block(self, away, x_away):
        return self.buf.at[self.core, 0, mod(self.k.z + away, self.k.z_count), mod(self.k.x + x_away, self.k.x_count)]

    def ax(self, kind, away, x_away):
        ref = self.block(away, x_away)
        up = self.goes_up(away) if kind == 2 else kind == 0
        at = (kind, away % self.k.z_count)
        return copy(ref, ref, self.ax_s.at[at], self.ax_r.at[at], self.k.x_device(1 if up else -1))

    def goes_up(self, away):
        return away % self.k.z_count < self.steps

    def a_out(self, away):
        for kind in range(2):
            self.ax(kind, away, 0).start()

    def a_on(self, away):
        for kind, x_away in enumerate((-1, 1)):
            self.ax(kind, away, x_away).wait_recv()
        self.ax(2, away, -1 if self.goes_up(away) else 1).start()

    def aways(self, n):
        return (0,) if n == 0 else (-n, n) if n < self.steps else (n,)

    def bx(self, by, away):
        ref = self.buf.at[self.core, 1, self.k.z, mod(self.k.x + away, self.k.x_count)]
        return copy(ref, ref, self.bx_s.at[by], self.bx_r.at[by], self.k.x_device(by))

    def hand(self, part, ref):
        return copy(ref, ref, self.c_s.at[part], self.c_r.at[part], self.k.sibling())

    def hand_second(self, ref):
        self.hand(1, ref).start()

    def start(self):
        for by in range(1, self.k.x_count):
            self.bx(by, 0).start()
        for way in BOTH:
            self.first.start(way, 0)
        self.a_out(0)

    def a_step(self, n):
        for way in BOTH:
            self.first.step(n, way, 0)
        for away in self.aways(n):
            self.a_out(away)

    def a_pass(self, n):
        for away in self.aways(n):
            self.a_on(away)

    def b_start(self):
        for by in range(1, self.k.x_count):
            self.bx(by, -by).wait_recv()
        for chunk in range(2):
            for way in BOTH:
                self.second.start(way, chunk)
        self.hand(1, self.buf.at[self.core, 1, self.k.z]).start()

    def b_step(self, n, chunk):
        for way in BOTH:
            self.second.step(n, way, chunk)

    def a_hand(self, by):
        self.hand(0, self.buf.at[self.core, 0, :, mod(self.k.x + by, self.k.x_count)]).start()

    def a_near(self):
        for by in (0, -1, 1):
            self.a_hand(by)

    def a_far(self):
        for away in range(self.k.z_count):
            self.ax(2, away, 2).wait_recv()
        self.a_hand(2)

    def wait(self, part):
        self.hand(part, self.buf.at[1 - self.core, part]).wait_recv()

    def finish(self):
        self.first.finish()
        self.second.finish()
        for by in range(1, self.k.x_count):
            self.bx(by, 0).wait_send()
        for away in range(self.k.z_count):
            for kind in range(3):
                self.ax(kind, away, 0).wait_send()
        for part in range(2):
            self.hand(part, self.buf.at[self.core, part]).wait_send()


class Qkv:
    def __init__(self, links, piece, buf, sems):
        self.k, self.buf, self.source = links, buf, piece
        self.load_s, self.x_s, self.x_r, self.z_s, self.z_r, e_s, e_r, l_s, l_r, self.c_s, self.c_r = sems
        self.zs, self.xs = buf.shape[2], buf.shape[3]
        self.early = early = self.zs * 3 // 4
        up = (links.y_count - 1) // 3
        reach = (up, links.y_count - 1 - up)
        half = self.xs // 2
        mine = lambda y, *rest: buf.at[(links.core, y, *rest)]
        self.first = Ring(links.y, links.y_count, links.y_device,
                          lambda y, c: mine(y, pl.ds(0, early), pl.ds(c * half, half)),
                          e_s, e_r, reach, 2, None, lambda ref: self.hand(0, ref).start())
        self.last = Ring(links.y, links.y_count, links.y_device, lambda y, c: mine(y, pl.ds(early, self.zs - early)),
                         l_s, l_r, reach, 1, None, lambda ref: self.hand(1, ref).start())
        self.sends = lax.rem(links.z, 2) == links.core
        self.zz = lax.div(links.z, 2)

    def load(self):
        return pltpu.make_async_copy(self.source, self.buf.at[self.k.core, self.k.y, self.zz, self.k.x], self.load_s.at[0])

    def preload(self):
        pl.when(self.sends)(lambda: self.load().start())

    def z_copy(self, by):
        ref = self.buf.at[self.k.core, self.k.y, self.zz, self.k.x]
        return copy(ref, ref, self.z_s.at[0], self.z_r.at[0], self.k.z_device(by))

    def x_copy(self, by):
        ref = self.buf.at[self.k.core, self.k.y, :, self.k.x]
        return copy(ref, ref, self.x_s.at[0], self.x_r.at[0], self.k.x_device(by))

    def x_all(self):
        ref = self.buf.at[self.k.core, self.k.y, :, pl.ds(0, self.xs - 1)]
        return copy(ref, ref, self.x_s.at[0], self.x_r.at[0], self.k.x_device(1))

    def start(self):
        @pl.when(self.sends)
        def _():
            self.load().wait()
            for by in range(1, self.k.z_count):
                self.z_copy(by).start()

    def across(self):
        def got(count):
            ref = self.buf.at[self.k.core, self.k.y, pl.ds(0, count), self.k.x]
            copy(ref, ref, self.z_s.at[0], self.z_r.at[0], self.k.z_device(1)).wait_recv()

        pl.when(self.sends)(lambda: got(self.zs - 1))
        pl.when(jnp.logical_not(self.sends))(lambda: got(self.zs))
        for by in range(1, self.xs):
            self.x_copy(by).start()

    def collect(self):
        self.x_all().wait_recv()
        for chunk in range(2):
            self.first.start(1, chunk)
        for part in range(2):
            self.hand(part, self.part_of(part, self.k.core, self.k.y)).start()

    def up(self):
        for chunk in range(2):
            self.first.start(0, chunk)

    def rest(self):
        for way in BOTH:
            self.last.start(way, 0)

    def hand(self, part, ref):
        return copy(ref, ref, self.c_s.at[part], self.c_r.at[part], self.k.sibling())

    def part_of(self, part, core, y):
        zs = pl.ds(0, self.early) if part == 0 else pl.ds(self.early, self.zs - self.early)
        return self.buf.at[core, y, zs]

    def all_of(self, part, core):
        return self.hand(part, self.part_of(part, core, slice(None)))

    def wait(self, part):
        self.all_of(part, 1 - self.k.core).wait_recv()

    def finish(self):
        self.first.finish()
        self.last.finish()
        for part in range(2):
            self.all_of(part, self.k.core).wait_send()

        self.x_all().wait_send()

        @pl.when(self.sends)
        def _():
            ref = self.buf.at[self.k.core, pl.ds(0, self.k.z_count - 1), 0, self.k.x]
            copy(ref, ref, self.z_s.at[0], self.z_r.at[0], self.k.z_device(1)).wait_send()


def kernel(
    z_count, tm_count,
    features, gain, conv, proj, attn_gain, qkv, out_weight, tokens_out, out,
    feat, halo, conv_in, out_in, x_sums, z_sums, slab_sums, token_x, token_z,
    proj_all, qkv_all, act_hi, act_lo, residual, band_hi, band_lo, proj_hi, proj_lo, keys, queries, q_hi, q_lo, total, top, mass,
    partial, lse_mine, relay, relay_lse, joint, joint_lse, parts, parts_lse,
    load_s, halo_s, halo_r, sum_s, sum_r, *sems,
):
    proj_sems, qkv_sems, sems = sems[:10], sems[10:21], sems[21:]
    key_s, key_r, query_s, query_r, part_s, part_r = sems
    k = Links(z_count, X, tm_count)
    rows_count = z_count * X
    tm, z, x = k.tm, k.z, k.x
    frames, height, columns, channels = features.shape
    half_w = columns // 2
    count = (height // 2) * half_w
    width = keys.shape[2]
    wide = proj_all.shape[5]
    per_half, narrow = qkv_all.shape[4:]
    steps = z_count // 2
    plan = Plan()

    loads = [
        pltpu.make_async_copy(features.at[:, :, :, pl.ds(128 * half, 128)], feat.at[half], load_s.at[half])
        for half in range(2)
    ]
    for load in loads:
        load.start()
    barrier = pltpu.get_barrier_semaphore()
    peers = (
        [k.x_device(by) for by in range(1, X)] + [k.z_device(by) for by in range(1, z_count)]
        + [k.tm_device(by) for by in range(1, tm_count)]
    )
    for peer in peers:
        pl.semaphore_signal(barrier, inc=1, device_id=peer, device_id_type=pl.DeviceIdType.MESH)

    quarters = [
        pltpu.make_async_copy(
            proj.at[:, pl.ds(pl.multiple_of((2 * k.core + part) * wide, wide), wide)],
            proj_all.at[k.core, part, z, x], load_s.at[2 + part],
        )
        for part in range(2)
    ]
    piece = qkv.at[
        pl.ds(pl.multiple_of(lax.div(k.y, 4) * per_half, 8), per_half),
        pl.ds(pl.multiple_of(lax.rem(k.y, 4) * narrow, narrow), narrow),
    ]
    proj_w = Proj(k, proj_all, proj_sems)
    qkv_w = Qkv(k, piece, qkv_all, qkv_sems)
    for one in quarters:
        one.start()
    qkv_w.preload()
    weight_loads = [
        pltpu.make_async_copy(conv, conv_in, load_s.at[4]), pltpu.make_async_copy(out_weight, out_in, load_s.at[5])
    ]
    for one in weight_loads:
        one.start()

    lane = iota((8, 128), 1)
    row = iota((8, 128), 0)
    sums = []
    for load in loads:
        load.wait()
    for frame in range(frames):
        values = jnp.concatenate([feat[half, frame].reshape(height * columns, 128) for half in range(2)], axis=1)
        sums += [jnp.sum(values, axis=0, keepdims=True), jnp.sum(values * values, axis=0, keepdims=True)]
    stacked = jnp.concatenate(sums + [jnp.zeros((4, channels), f32)], axis=0)
    per_group = channels // GROUPS
    fold = (iota((channels, 128), 1) % GROUPS == iota((channels, 128), 0) // per_group).astype(f32)

    def lanes_of(rows_of_sums, table):
        return jnp.sum(jnp.where(lane // GROUPS == row, exact(rows_of_sums, table), 0.0), axis=0, keepdims=True)

    slab_sums[tm] = lanes_of(stacked, fold)
    for one in quarters:
        one.wait()

    def exchange(slots, index, per, size, device, n):
        return Sums(slots, index, per, size, device, sum_s.at[n], sum_r.at[n])

    over_tm = exchange(slab_sums, tm, 1, tm_count, k.tm_device, 0)
    over_x = exchange(x_sums, x, 1, X, k.x_device, 1)
    over_z = exchange(z_sums, z, 1, z_count, k.z_device, 2)
    tokens_z = exchange(token_z, z, 1, z_count, k.z_device, 3)
    tokens_x = exchange(token_x, x, 1, X, k.x_device, 4)

    pl.semaphore_wait(barrier, len(peers))
    over_tm.start()
    pairs = height // 2

    def halo_copy(f, h):
        at = (slice(None), f, pl.ds(2 * h, 2))
        return copy(feat.at[at], halo.at[at], halo_s.at[f, h], halo_r.at[f, h], {"tm": mod(tm + 1, tm_count)})

    halo_copies = [halo_copy(f, h) for h in range(pairs) for f in range(frames)]
    for one in halo_copies:
        one.start()
    proj_w.start()
    qkv_w.start()
    plan.now = 4.0

    def summed_tm():
        over_tm.wait()
        x_sums[x] = jnp.concatenate([slab_sums[i] for i in range(tm_count)], axis=0)
        over_x.start()

    def summed_x():
        over_x.wait()
        z_sums[z] = jnp.sum(x_sums[...], axis=0)
        over_z.start()

    plan.expect(6.4, "tm", summed_tm)
    plan.expect(9.0, "x", summed_x)
    plan.expect(7.8, "qkv x", qkv_w.across)
    plan.expect(6.8, "b", proj_w.b_start)
    plan.expect(7.5, "a", functools.partial(proj_w.a_pass, 0))
    for n in range(1, steps + 1):
        plan.expect(4.0 + 2.7 * n, "a", functools.partial(proj_w.a_step, n))
        plan.expect(7.0 + 2.7 * n, "a", functools.partial(proj_w.a_pass, n))
        for chunk in range(2):
            plan.expect(8.8 + 1.8 * (2 * n - 1 + chunk), "b", functools.partial(proj_w.b_step, n, chunk))
    plan.expect(7.1 + 2.7 * steps, "a", proj_w.a_near)
    plan.expect(10.0 + 2.7 * steps, "a far", proj_w.a_far)
    plan.expect(10.6, "collect", qkv_w.collect)
    plan.expect(12.0, "z", over_z.wait)
    for h in range(pairs):
        for frame in range(frames):
            plan.expect(13.0 + 7.0 * h + 0.1 * frame, f"halo{h}", halo_copy(frame, h).wait_recv)
    plan.expect(6.2 + 7.0 * pairs, "up", qkv_w.up)
    qkv_done = 12.6
    for step, way, chunk in qkv_w.first.each():
        time = (12.6 if way else 8.2 + 7.0 * pairs) + 1.7 * (2 * step - 1 + chunk)
        qkv_done = max(qkv_done, time)
        plan.expect(time, "qkv", functools.partial(qkv_w.first.step, step, way, chunk))
    plan.expect(qkv_done + 0.1, "rest", qkv_w.rest)
    plan.expect(qkv_done + 3.6, "qkv", functools.partial(qkv_w.wait, 0))
    for step, way, chunk in qkv_w.last.each():
        plan.expect(qkv_done + 5.0 + 2.5 * step, "qkv last", functools.partial(qkv_w.last.step, step, way, chunk))
    plan.expect(qkv_done + 7.0 + 2.5 * max(qkv_w.last.reach), "qkv last", functools.partial(qkv_w.wait, 1))

    def split_taps():
        weight_loads[0].wait()
        return [split(conv_in[lag]) for lag in range(3)]

    taps = plan.run(0.4, split_taps)

    def statistics():
        everything = jnp.sum(z_sums[...], axis=0)
        slab = iota(everything.shape, 0)

        def of(these):
            return jnp.sum(jnp.where(these, everything, 0.0), axis=0, keepdims=True)

        earlier, previous, own = of(slab < tm - 1), of(slab == tm - 1), of(slab == tm)
        kind, upto = row % 2, row // 2
        lane_kind, lane_frame = lane // GROUPS % 2, lane // GROUPS // 2
        mine = lane_kind == kind
        running = (
            jnp.where(mine, earlier, 0.0)
            + jnp.where(mine & (lane_frame <= upto), previous, 0.0)
            + jnp.where(mine & (lane_frame <= upto - 2), own, 0.0)
        )
        unfold = (iota((128, channels), 0) % GROUPS == iota((128, channels), 1) // per_group).astype(f32)
        running = exact(running, unfold)
        means, scales = [], []
        for i in range(4):
            position = jnp.maximum(tm * frames + i - 1, 1).astype(f32)
            cells = position * float(rows_count * height * columns * per_group)
            mean = running[2 * i : 2 * i + 1] / cells
            variance = running[2 * i + 1 : 2 * i + 2] / cells - mean * mean
            means.append(mean)
            scales.append(rsqrt(variance))
        return means, scales

    means, scales = plan.run(0.6, statistics, "z")
    norm_gain = gain[...]

    def cells_of(src, frame, h, b, c):
        return jnp.concatenate([src[half, frame, 2 * h + b, pl.ds(c, half_w, stride=2), :] for half in range(2)], axis=1)

    def activate(src, frame, h, at):
        for b in range(2):
            for c in range(2):
                value = (cells_of(src, frame, h, b, c) - means[at]) * scales[at] * norm_gain
                value = value / (1.0 + jnp.exp(-value))
                if at < 2:
                    value = jnp.where(tm > 0, value, 0.0)
                high, low = split(value)
                place = pl.ds((2 * b + c) * half_w, half_w)
                act_hi[at, h, place] = high
                act_lo[at, h, place] = low

    def activated(at, h):
        return tuple(ref[at, h].reshape(-1, channels) for ref in (act_hi, act_lo))

    def convolve(frame, h, terms, first=False):
        value = functools.reduce(jnp.add, [dot3(activated(at, h), taps[lag]) for at, lag in terms])
        value = value.reshape((-1, 4 * half_w, channels))
        residual[frame, h] = value if first else residual[frame, h] + value

    every = pl.ds(0, pairs)
    for frame in range(frames):
        plan.run(0.7, lambda: [activate(feat, frame, h, 2 + frame) for h in range(pairs)])
    plan.run(0.5, lambda: convolve(0, every, [(2, 0)], True))
    plan.run(1.0, lambda: convolve(1, every, [(3, 0), (2, 1)], True))
    def split_quarter(half, part):
        at = 2 * half + part
        high, low = split(proj_all[half, part].reshape(width, wide))
        proj_hi[at] = high
        proj_lo[at] = low

    for h in range(pairs):
        for frame in range(frames):
            plan.run(0.35, lambda: activate(halo, frame, h, frame), f"halo{h}")
        plan.run(0.6, lambda: convolve(0, pl.ds(h, 1), [(1, 1), (0, 2)]))
        plan.run(0.3, lambda: convolve(1, pl.ds(h, 1), [(1, 2)]))

    def haar():
        bands = [
            jnp.concatenate([
                residual[a, h, pl.ds((2 * b + c) * half_w, half_w)] + cells_of(feat, a, h, b, c) for h in range(pairs)
            ], axis=0)
            for a in range(2) for b in range(2) for c in range(2)
        ]
        for bit in (4, 2, 1):
            bands = [
                bands[j] + bands[j | bit] if not j & bit else bands[j ^ bit] - bands[j] for j in range(8)
            ]
        bands = [split(band * (1.0 / math.sqrt(8.0))) for band in bands]
        per_quarter = wide // channels
        for quarter in range(4):
            ours = bands[quarter * per_quarter : (quarter + 1) * per_quarter]
            band_hi[quarter] = jnp.concatenate([band[0] for band in ours], axis=1)
            band_lo[quarter] = jnp.concatenate([band[1] for band in ours], axis=1)

    plan.run(0.7, haar)

    def quarter_of(half, part):
        at = 2 * half + part
        return dot3((band_hi[at], band_lo[at]), (proj_hi[at], proj_lo[at]), NT)

    other = 1 - k.core
    plan.run(0.3, lambda: split_quarter(k.core, 0), "a far")
    made = plan.run(0.5, lambda: quarter_of(k.core, 0))
    proj_w.wait(0)
    plan.run(0.3, lambda: split_quarter(other, 0))
    made = made + plan.run(0.5, lambda: quarter_of(other, 0))
    plan.run(0.3, lambda: split_quarter(k.core, 1), "b")
    made = made + plan.run(0.5, lambda: quarter_of(k.core, 1))
    proj_w.wait(1)
    plan.run(0.3, lambda: split_quarter(other, 1))
    made = made + plan.run(0.5, lambda: quarter_of(other, 1))
    tokens_out[...] = made.reshape(tokens_out.shape)
    keys[z] = made
    queries[x] = made

    part_rows = count // 2
    key_chunks = 4
    key_rows = count // key_chunks
    key_ring = Ring(z, z_count, k.z_device, lambda at, c: keys.at[at, pl.ds(c * key_rows, key_rows)],
                    key_s, key_r, (steps, steps), key_chunks)
    query_ring = Ring(x, X, k.x_device, lambda at, c: queries.at[at], query_s, query_r, (X // 2, X // 2), 1,
                      lambda ref, way: ref.at[pl.ds(way * part_rows, part_rows)])
    token_group = width // GROUPS
    sums = jnp.concatenate(
        [jnp.sum(made, axis=0, keepdims=True), jnp.sum(made * made, axis=0, keepdims=True), jnp.zeros((6, width), f32)],
        axis=0,
    )
    fold = (iota((width, 128), 1) % GROUPS == iota((width, 128), 0) // token_group).astype(f32)
    token_z[z] = lanes_of(sums, fold)
    tokens_z.start()
    for way in BOTH:
        query_ring.start(way, 0)
    for chunk in range(key_chunks):
        for way in BOTH:
            key_ring.start(way, chunk)
    begin = plan.now
    for step, way, chunk in key_ring.each():
        turn = chunk if step < steps else chunk % (key_chunks // 2)
        plan.expect(begin + 2.0 + 1.5 * (key_chunks * (step - 1) + turn + 1), f"key{step}",
                    functools.partial(key_ring.step, step, way, chunk))

    def token_summed_z():
        tokens_z.wait()
        token_x[x] = jnp.sum(token_z[...], axis=0)
        tokens_x.start()

    plan.expect(begin + 2.5, "tokens z", token_summed_z)
    plan.expect(begin + 9.5, "tokens x", tokens_x.wait)
    for step, way, chunk in query_ring.each():
        plan.expect(begin + 4.9 * step + 2.9, "queries", functools.partial(query_ring.step, step, way, chunk))

    def token_statistics():
        all_sums = jnp.sum(token_x[...], axis=0)
        unfold = (iota((128, width), 0) % GROUPS == iota((128, width), 1) // token_group).astype(f32)
        spread_sums = exact(jnp.where(lane // GROUPS == row, all_sums, 0.0), unfold)
        token_count = float(rows_count * count * token_group)
        mean = spread_sums[0:1] / token_count
        return mean, rsqrt(spread_sums[1:2] / token_count - mean * mean)

    token_gain = attn_gain[...]

    def normed(value):
        return split((value - token_mean) * token_scale * token_gain)

    def columns_of(block):
        lanes = []
        for lane_at in range(4):
            chunks = []
            for at in range(block * width // per_half, (block + 1) * width // per_half + 1):
                owner, part = at // 2, at % 2
                if owner < rows_count:
                    own_z, own_x = owner // X, owner % X
                    chunks.append(qkv_all[own_z % 2, 4 * part + lane_at, own_z // 2, own_x])
            skip = block * width - block * width // per_half * per_half
            lanes.append(jnp.concatenate(chunks, axis=0)[skip : skip + width])
        return split(jnp.concatenate(lanes, axis=1))

    def query_key_weight():
        query_weight = tuple(jnp.transpose(part.astype(f32)).astype(bf16) for part in columns_of(0))
        return split(dot3(query_weight, columns_of(1)) * (1.0 / math.sqrt(float(width))))

    order = (2, 1, 3, 0)

    def ask():
        asking = jnp.concatenate([queries[mod(x + by, X)] for by in order], axis=0)
        high, low = split(dot3(normed(asking), query_key))
        q_hi[...], q_lo[...] = high.reshape(q_hi.shape), low.reshape(q_lo.shape)

    query_key = plan.run(2.0, query_key_weight, "qkv")
    token_mean, token_scale = plan.run(0.6, token_statistics, "tokens x")
    plan.run(1.5, ask, "queries")

    sets = [(0, -1, 1)] + [(-step, step) for step in range(2, steps)] + [(steps,)]

    def key_block(at):
        return normed(jnp.concatenate([keys[mod(z + away, z_count)] for away in sets[at]], axis=0))

    def rows_of(ref, at):
        return ref[at].reshape(-1, ref.shape[-1])

    def scores_of(at, block):
        return dot3((rows_of(q_hi, at), rows_of(q_lo, at)), block, NT)

    def attend(first, at, block, scores):
        here = jnp.max(scores, axis=1, keepdims=True)
        if first:
            weights = jnp.exp(scores - here)
            return here, jnp.sum(weights, axis=1, keepdims=True), dot3(split(weights), block)
        new_top = jnp.maximum(rows_of(top, at), here)
        fade = jnp.exp(rows_of(top, at) - new_top)
        weights = jnp.exp(scores - new_top)
        new_mass = rows_of(mass, at) * fade + jnp.sum(weights, axis=1, keepdims=True)
        return new_top, new_mass, rows_of(total, at) * fade + dot3(split(weights), block)

    def attend_all(step, block, scores):
        for ref, value in zip((top, mass, total), attend(step == 0, slice(None), block, scores)):
            ref[...] = value.reshape(ref.shape)

    for step in range(len(sets) - 1):
        block = plan.run(0.2, lambda: key_block(step), f"key{step + 1}")
        scores = plan.run(1.2 if step == 0 else 0.9, lambda: scores_of(slice(None), block))
        plan.run(1.6 if step == 0 else 1.2, lambda: attend_all(step, block, scores))

    half_rows = [pl.ds(way * part_rows, part_rows) for way in BOTH]
    toward = (1, -1)

    def send(kind, way, src, dst):
        return copy(src, dst, part_s.at[kind, way], part_r.at[kind, way], k.x_device(toward[way]))

    def opposite(way):
        return (send(0, way, partial.at[0, half_rows[way]], relay.at[way]),
                send(1, way, lse_mine.at[0], relay_lse.at[way]))

    def plain(way):
        return (send(2, way, partial.at[1 + way, half_rows[1 - way]], parts.at[way, half_rows[1 - way]]),)

    def joined(way):
        return (send(3, way, joint.at[way], parts.at[way, half_rows[way]]), send(4, way, joint_lse.at[way], parts_lse.at[way]))

    def as_column(lanes):
        return jnp.transpose(jnp.broadcast_to(lanes, (count, 128)))

    def across(column):
        return jnp.concatenate([column] * (width // 128), axis=1)

    plan.need(f"key{steps}")
    block = key_block(-1)
    for first, last in ((0, 1), (1, X)):
        at = slice(first, last)
        last_top, last_mass, value = attend(False, at, block, scores_of(at, block))
        partial[at] = (value / last_mass).reshape(last - first, count, width)
        lse = last_top + jnp.log(last_mass)
        for i in range(first, last):
            column = lse[(i - first) * count : (i + 1 - first) * count]
            lse_mine[i] = jnp.transpose(jnp.broadcast_to(column, (count, 128)))[0:1]
        for way in BOTH:
            for one in opposite(way) if first == 0 else plain(way):
                one.start()
    plan.now += 1.5

    def value_to_out():
        weight_loads[1].wait()
        value_weight = tuple(jnp.transpose(part.astype(f32)).astype(bf16) for part in columns_of(2))
        return split(dot3(value_weight, split(out_in[...])))

    value_out = plan.run(2.0, value_to_out, "qkv last")
    plan.upto(1e9)
    lane_row = iota((1, 128), 1)
    for way in BOTH:
        for one in opposite(way):
            one.wait_recv()
        at = 1 + way
        own, theirs = lse_mine[at], relay_lse[way]
        both = jnp.maximum(own, theirs)
        both = both + jnp.log(jnp.exp(own - both) + jnp.exp(theirs - both))
        rows_of_way = slice(way * part_rows, (way + 1) * part_rows)
        joint[way] = (
            partial[at, half_rows[way]] * across(as_column(jnp.exp(own - both))[rows_of_way])
            + relay[way] * across(as_column(jnp.exp(theirs - both))[rows_of_way])
        )
        joint_lse[way] = jnp.where(lane_row // part_rows == way, both, own)
        for one in joined(way):
            one.start()

    proj_w.finish()
    qkv_w.finish()
    for one in halo_copies:
        one.wait_send()
    for one in (over_tm, over_x, over_z, tokens_x, tokens_z):
        one.finish()
    key_ring.finish()
    query_ring.finish()
    for way in BOTH:
        for one in (*plain(way), *joined(way)):
            one.wait_recv()
    given = [(lse_mine[3], partial[3])] + [(parts_lse[way], parts[way]) for way in BOTH]
    highest_lse = functools.reduce(jnp.maximum, [lse for lse, _ in given])
    shares = [jnp.exp(lse - highest_lse) for lse, _ in given]
    whole = functools.reduce(jnp.add, shares)
    merged = jnp.zeros((count, width), f32)
    for share, (_, value) in zip(shares, given):
        merged = merged + value * across(as_column(share / whole))
    out[...] = dot3(split(merged), value_out).reshape(out.shape)

    for way in BOTH:
        for one in (*opposite(way), *plain(way), *joined(way)):
            one.wait_send()


def shards(z_count, tm_count, features, norm_gain, conv_weight, proj_weight, attn_gain, qkv_weight, out_weight):
    frames, height, columns, channels = features.shape
    width = out_weight.shape[0]
    half_h, half_w = height // 2, columns // 2
    count = half_h * half_w
    steps = z_count // 2
    rows_count = z_count * X
    proj_rows, qkv_rows = proj_weight.shape[1], qkv_weight.shape[1] // 2
    wide, narrow = proj_weight.shape[0] // 4, qkv_weight.shape[0] // 4
    y_count = tm_count // 2
    far = y_count - 1 - (y_count - 1) // 3
    vmem = pltpu.VMEM
    dma = pltpu.SemaphoreType.DMA
    proj_sems = [dma((2, steps)), dma((2, steps)), dma((3, z_count)), dma((3, z_count)), dma((X,)), dma((X,)), dma((4, steps)),
                 dma((4, steps)), dma((2,)), dma((2,))]
    qkv_sems = [dma((1,)), dma((1,)), dma((1,)), dma((1,)), dma((1,)), dma((4, far)), dma((4, far)), dma((2, far)),
                dma((2, far)), dma((2,)), dma((2,))]
    scratch = [
        vmem((2, frames, height, columns, 128), f32), vmem((2, frames, height, columns, 128), f32),
        vmem(conv_weight.shape, f32), vmem(out_weight.shape, f32),
        vmem((X, tm_count, 128), f32), vmem((z_count, tm_count, 128), f32), vmem((tm_count, 1, 128), f32),
        vmem((X, 1, 128), f32), vmem((z_count, 1, 128), f32),
        vmem((2, 2, z_count, X, proj_rows, wide), f32),
        vmem((2, y_count, z_count // 2, X, qkv_rows, narrow), f32),
        vmem((4, half_h, 4 * half_w, channels), bf16), vmem((4, half_h, 4 * half_w, channels), bf16),
        vmem((frames, half_h, 4 * half_w, channels), f32),
        vmem((4, count, wide), bf16), vmem((4, count, wide), bf16),
        vmem((4, width, wide), bf16), vmem((4, width, wide), bf16),
        vmem((z_count, count, width), f32),
        vmem((X, count, width), f32),
        vmem((X, count, width), bf16), vmem((X, count, width), bf16),
        vmem((X, count, width), f32), vmem((X, count, 1), f32), vmem((X, count, 1), f32),
        vmem((X, count, width), f32), vmem((X, 1, 128), f32),
        vmem((2, count // 2, width), f32), vmem((2, 1, 128), f32),
        vmem((2, count // 2, width), f32), vmem((2, 1, 128), f32),
        vmem((2, count, width), f32), vmem((2, 1, 128), f32),
        dma((6,)), dma((frames, half_h)), dma((frames, half_h)), dma((6,)), dma((6,)),
        *proj_sems, *qkv_sems,
        dma((8, steps)), dma((8, steps)), dma((2, X // 2)), dma((2, X // 2)), dma((5, 2)), dma((5, 2)),
    ]
    whole = pl.BlockSpec(memory_space=vmem)
    anywhere = pl.BlockSpec(memory_space=pl.ANY)
    given = jax.ShapeDtypeStruct((frames // 2, half_h, half_w, width), f32)
    tokens, attended = pl.pallas_call(
        functools.partial(kernel, z_count, tm_count),
        out_shape=(given, given),
        in_specs=[anywhere, whole, anywhere, anywhere, whole, anywhere, anywhere],
        out_specs=(whole, whole),
        scratch_shapes=scratch,
        compiler_params=pltpu.CompilerParams(collective_id=0, has_side_effects=True, vmem_limit_bytes=56 * 2**20),
    )(features, norm_gain[None], conv_weight, proj_weight.T, attn_gain[None], qkv_weight.T, out_weight)
    return tokens + attended


def solution(mesh):
    in_specs = (P("tm", "rows", None, None), P(), P(), P(None, "rows"), P(), P(None, "rows"), P())
    out_specs = P("tm", "rows", None, None)
    body = functools.partial(shards, mesh.shape["rows"] // X, mesh.shape["tm"])
    return jax.shard_map(body, mesh=mesh, in_specs=in_specs, out_specs=out_specs, check_vma=False)
```

```python
import functools
import math

import jax
import jax.numpy as jnp
from jax import lax
from jax.experimental import pallas as pl
from jax.experimental.pallas import tpu as pltpu
from jax.sharding import PartitionSpec as P

GROUPS = 32
X = 4
epsilon = 1e-06
f32, bf16 = jnp.float32, jnp.bfloat16
NN = (((1,), (0,)), ((), ()))
NT = (((1,), (1,)), ((), ()))
BOTH = (0, 1)


def split(value):
    high = value.astype(bf16)
    return high, (value - high.astype(f32)).astype(bf16)


def dot(a, b, dims):
    return lax.dot_general(a, b, dims, preferred_element_type=f32)


def dot3(a, b, dims=NN):
    rows = a[0].shape[0]
    if rows > 256:
        deep = (b[0], b[0], b[1])
        return dot(jnp.concatenate((a[0], a[1], a[0]), axis=1), jnp.concatenate(deep, axis=dims[0][1][0]), dims)
    by_high = dot(jnp.concatenate(a, axis=0), b[0], dims)
    return by_high[:rows] + (by_high[rows:] + dot(a[0], b[1], dims))


def exact(a, table):
    high = a.astype(bf16)
    rest = a - high.astype(f32)
    middle = rest.astype(bf16)
    low = (rest - middle.astype(f32)).astype(bf16)
    rows = a.shape[0]
    parts = jnp.concatenate([part.astype(f32) for part in (high, middle, low)] + [jnp.zeros_like(a)], axis=0).astype(bf16)
    by_part = dot(parts, table.astype(bf16), NN)
    return by_part[:rows] + (by_part[rows : 2 * rows] + by_part[2 * rows : 3 * rows])


def iota(shape, axis):
    return lax.broadcasted_iota(jnp.int32, shape, axis)


def rsqrt(value):
    return lax.rsqrt(value + epsilon)


def mod(value, size):
    return lax.rem(value + size, size)


class Plan:
    def __init__(self):
        self.now, self.waits = 0.0, []

    def expect(self, time, name, action):
        self.waits.append((time, len(self.waits), name, action))

    def upto(self, time):
        while True:
            due = [wait for wait in self.waits if wait[0] <= time]
            if not due:
                return
            first = min(due, key=lambda wait: wait[:2])
            self.waits.remove(first)
            first[3]()

    def need(self, name):
        times = [wait[0] for wait in self.waits if wait[2] == name]
        if times:
            self.now = max(self.now, max(times))
            self.upto(max(times))

    def run(self, duration, action, *needs):
        for name in needs:
            self.need(name)
        self.upto(self.now)
        result = action()
        self.now += duration
        return result


class Links:
    def __init__(self, z_count, x_count, tm_count):
        self.rows, self.tm = lax.axis_index("rows"), lax.axis_index("tm")
        self.z, self.x = lax.div(self.rows, x_count), lax.rem(self.rows, x_count)
        self.y, self.core = lax.div(self.tm, 2), lax.rem(self.tm, 2)
        self.z_count, self.x_count, self.y_count = z_count, x_count, tm_count // 2

    def z_device(self, by):
        return {"rows": mod(self.z + by, self.z_count) * self.x_count + self.x}

    def x_device(self, by):
        return {"rows": self.z * self.x_count + mod(self.x + by, self.x_count)}

    def y_device(self, by):
        return {"tm": mod(self.y + by, self.y_count) * 2 + self.core}

    def tm_device(self, by):
        return {"tm": mod(self.tm + by, 2 * self.y_count)}

    def sibling(self):
        return {"tm": self.tm + 1 - 2 * self.core}


def copy(src, dst, send, recv, device):
    return pltpu.make_async_remote_copy(
        src_ref=src, dst_ref=dst, send_sem=send, recv_sem=recv, device_id=device,
        device_id_type=pl.DeviceIdType.MESH,
    )


class Ring:
    def __init__(self, place, count, device, at, send, recv, reach, chunks=1, half=None, arrived=None):
        self.place, self.count, self.device, self.at, self.half = place, count, device, at, half
        self.send, self.recv, self.reach, self.chunks, self.arrived = send, recv, reach, chunks, arrived

    def moves(self, step, way, chunk):
        if step > self.reach[way]:
            return False
        shared = step == self.reach[0] == self.reach[1] and 2 * step == self.count
        return not shared or self.chunks == 1 or chunk // (self.chunks // 2) == way

    def ref(self, away, step, way, chunk):
        ref = self.at(mod(self.place + away, self.count), chunk)
        return self.half(ref, way) if self.half and 2 * step == self.count else ref

    def copy(self, step, way, chunk, away):
        ref = self.ref(away, step, way, chunk)
        at = (way * self.chunks + chunk, step - 1)
        return copy(ref, ref, self.send.at[at], self.recv.at[at], self.device(1 if way == 0 else -1))

    def outgoing(self, step, way, chunk):
        return self.copy(step, way, chunk, 1 - step if way == 0 else step - 1)

    def start(self, way, chunk):
        self.outgoing(1, way, chunk).start()

    def step(self, step, way, chunk):
        if not self.moves(step, way, chunk):
            return
        away = -step if way == 0 else step
        self.copy(step, way, chunk, away).wait_recv()
        if self.moves(step + 1, way, chunk):
            self.outgoing(step + 1, way, chunk).start()
        if self.arrived:
            self.arrived(self.ref(away, step, way, chunk))

    def each(self):
        for step in range(1, max(self.reach) + 1):
            for chunk in range(self.chunks):
                for way in BOTH:
                    if self.moves(step, way, chunk):
                        yield step, way, chunk

    def finish(self):
        for step, way, chunk in self.each():
            self.outgoing(step, way, chunk).wait_send()


class Sums:
    def __init__(self, slots, index, per, size, device, send, recv):
        self.slots, self.index, self.per, self.size, self.device = slots, index, per, size, device
        self.send, self.recv = send, recv

    def copies(self, by):
        ref = self.slots.at[pl.ds(self.index * self.per, self.per)]
        return copy(ref, ref, self.send, self.recv, self.device(by))

    def everything(self):
        ref = self.slots.at[pl.ds(0, (self.size - 1) * self.per)]
        return copy(ref, ref, self.send, self.recv, self.device(1))

    def start(self):
        for by in range(1, self.size):
            self.copies(by).start()

    def wait(self):
        self.everything().wait_recv()

    def finish(self):
        self.everything().wait_send()


class Proj:
    def __init__(self, links, buf, sems):
        self.k, self.buf = links, buf
        az_s, az_r, self.ax_s, self.ax_r, self.bx_s, self.bx_r, bz_s, bz_r, self.c_s, self.c_r = sems
        self.core = links.core
        rows, xs, steps = buf.shape[4] // 2, links.x_count // 2, links.z_count // 2
        self.first = Ring(links.z, links.z_count, links.z_device, lambda z, chunk: buf.at[self.core, 0, z, links.x],
                          az_s, az_r, (steps, steps), 1, lambda ref, way: ref.at[pl.ds(way * rows, rows)])
        self.second = Ring(links.z, links.z_count, links.z_device,
                           lambda z, chunk: buf.at[self.core, 1, z, pl.ds(chunk * xs, xs)],
                           bz_s, bz_r, (steps, steps), 2, None, self.hand_second)
        self.steps = steps

    def block(self, away, x_away):
        return self.buf.at[self.core, 0, mod(self.k.z + away, self.k.z_count), mod(self.k.x + x_away, self.k.x_count)]

    def ax(self, kind, away, x_away):
        ref = self.block(away, x_away)
        up = self.goes_up(away) if kind == 2 else kind == 0
        at = (kind, away % self.k.z_count)
        return copy(ref, ref, self.ax_s.at[at], self.ax_r.at[at], self.k.x_device(1 if up else -1))

    def goes_up(self, away):
        return away % self.k.z_count < self.steps

    def a_out(self, away):
        for kind in range(2):
            self.ax(kind, away, 0).start()

    def a_on(self, away):
        for kind, x_away in enumerate((-1, 1)):
            self.ax(kind, away, x_away).wait_recv()
        self.ax(2, away, -1 if self.goes_up(away) else 1).start()

    def aways(self, n):
        return (0,) if n == 0 else (-n, n) if n < self.steps else (n,)

    def bx(self, by, away):
        ref = self.buf.at[self.core, 1, self.k.z, mod(self.k.x + away, self.k.x_count)]
        return copy(ref, ref, self.bx_s.at[by], self.bx_r.at[by], self.k.x_device(by))

    def hand(self, part, ref):
        return copy(ref, ref, self.c_s.at[part], self.c_r.at[part], self.k.sibling())

    def hand_second(self, ref):
        self.hand(1, ref).start()

    def start(self):
        for by in range(1, self.k.x_count):
            self.bx(by, 0).start()
        for way in BOTH:
            self.first.start(way, 0)
        self.a_out(0)

    def a_step(self, n):
        for way in BOTH:
            self.first.step(n, way, 0)
        for away in self.aways(n):
            self.a_out(away)

    def a_pass(self, n):
        for away in self.aways(n):
            self.a_on(away)

    def b_start(self):
        for by in range(1, self.k.x_count):
            self.bx(by, -by).wait_recv()
        for chunk in range(2):
            for way in BOTH:
                self.second.start(way, chunk)
        self.hand(1, self.buf.at[self.core, 1, self.k.z]).start()

    def b_step(self, n, chunk):
        for way in BOTH:
            self.second.step(n, way, chunk)

    def a_hand(self, by):
        self.hand(0, self.buf.at[self.core, 0, :, mod(self.k.x + by, self.k.x_count)]).start()

    def a_near(self):
        for by in (0, -1, 1):
            self.a_hand(by)

    def a_far(self):
        for away in range(self.k.z_count):
            self.ax(2, away, 2).wait_recv()
        self.a_hand(2)

    def wait(self, part):
        self.hand(part, self.buf.at[1 - self.core, part]).wait_recv()

    def finish(self):
        self.first.finish()
        self.second.finish()
        for by in range(1, self.k.x_count):
            self.bx(by, 0).wait_send()
        for away in range(self.k.z_count):
            for kind in range(3):
                self.ax(kind, away, 0).wait_send()
        for part in range(2):
            self.hand(part, self.buf.at[self.core, part]).wait_send()


class Qkv:
    def __init__(self, links, piece, buf, sems):
        self.k, self.buf, self.source = links, buf, piece
        self.load_s, self.x_s, self.x_r, self.z_s, self.z_r, e_s, e_r, l_s, l_r, self.c_s, self.c_r = sems
        self.zs, self.xs = buf.shape[2], buf.shape[3]
        self.early = early = self.zs * 3 // 4
        up = (links.y_count - 1) // 3
        reach = (up, links.y_count - 1 - up)
        half = self.xs // 2
        mine = lambda y, *rest: buf.at[(links.core, y, *rest)]
        self.first = Ring(links.y, links.y_count, links.y_device,
                          lambda y, c: mine(y, pl.ds(0, early), pl.ds(c * half, half)),
                          e_s, e_r, reach, 2, None, lambda ref: self.hand(0, ref).start())
        self.last = Ring(links.y, links.y_count, links.y_device, lambda y, c: mine(y, pl.ds(early, self.zs - early)),
                         l_s, l_r, reach, 1, None, lambda ref: self.hand(1, ref).start())
        self.sends = lax.rem(links.z, 2) == links.core
        self.zz = lax.div(links.z, 2)

    def load(self):
        return pltpu.make_async_copy(self.source, self.buf.at[self.k.core, self.k.y, self.zz, self.k.x], self.load_s.at[0])

    def preload(self):
        pl.when(self.sends)(lambda: self.load().start())

    def z_copy(self, by):
        ref = self.buf.at[self.k.core, self.k.y, self.zz, self.k.x]
        return copy(ref, ref, self.z_s.at[0], self.z_r.at[0], self.k.z_device(by))

    def x_copy(self, by):
        ref = self.buf.at[self.k.core, self.k.y, :, self.k.x]
        return copy(ref, ref, self.x_s.at[0], self.x_r.at[0], self.k.x_device(by))

    def x_all(self):
        ref = self.buf.at[self.k.core, self.k.y, :, pl.ds(0, self.xs - 1)]
        return copy(ref, ref, self.x_s.at[0], self.x_r.at[0], self.k.x_device(1))

    def start(self):
        @pl.when(self.sends)
        def _():
            self.load().wait()
            for by in range(1, self.k.z_count):
                self.z_copy(by).start()

    def across(self):
        def got(count):
            ref = self.buf.at[self.k.core, self.k.y, pl.ds(0, count), self.k.x]
            copy(ref, ref, self.z_s.at[0], self.z_r.at[0], self.k.z_device(1)).wait_recv()

        pl.when(self.sends)(lambda: got(self.zs - 1))
        pl.when(jnp.logical_not(self.sends))(lambda: got(self.zs))
        for by in range(1, self.xs):
            self.x_copy(by).start()

    def collect(self):
        self.x_all().wait_recv()
        for chunk in range(2):
            self.first.start(1, chunk)
        for part in range(2):
            self.hand(part, self.part_of(part, self.k.core, self.k.y)).start()

    def up(self):
        for chunk in range(2):
            self.first.start(0, chunk)

    def rest(self):
        for way in BOTH:
            self.last.start(way, 0)

    def hand(self, part, ref):
        return copy(ref, ref, self.c_s.at[part], self.c_r.at[part], self.k.sibling())

    def part_of(self, part, core, y):
        zs = pl.ds(0, self.early) if part == 0 else pl.ds(self.early, self.zs - self.early)
        return self.buf.at[core, y, zs]

    def all_of(self, part, core):
        return self.hand(part, self.part_of(part, core, slice(None)))

    def wait(self, part):
        self.all_of(part, 1 - self.k.core).wait_recv()

    def finish(self):
        self.first.finish()
        self.last.finish()
        for part in range(2):
            self.all_of(part, self.k.core).wait_send()

        self.x_all().wait_send()

        @pl.when(self.sends)
        def _():
            ref = self.buf.at[self.k.core, pl.ds(0, self.k.z_count - 1), 0, self.k.x]
            copy(ref, ref, self.z_s.at[0], self.z_r.at[0], self.k.z_device(1)).wait_send()


def kernel(
    z_count, tm_count,
    features, gain, conv, proj, attn_gain, qkv, out_weight, tokens_out, out,
    feat, halo, conv_in, out_in, x_sums, z_sums, slab_sums, token_x, token_z,
    proj_all, qkv_all, act_hi, act_lo, residual, band_hi, band_lo, proj_hi, proj_lo, keys, queries, q_hi, q_lo, total, top, mass,
    partial, lse_mine, relay, relay_lse, joint, joint_lse, parts, parts_lse,
    load_s, halo_s, halo_r, sum_s, sum_r, *sems,
):
    proj_sems, qkv_sems, sems = sems[:10], sems[10:21], sems[21:]
    key_s, key_r, query_s, query_r, part_s, part_r = sems
    k = Links(z_count, X, tm_count)
    rows_count = z_count * X
    tm, z, x = k.tm, k.z, k.x
    frames, height, columns, channels = features.shape
    half_w = columns // 2
    count = (height // 2) * half_w
    width = keys.shape[2]
    wide = proj_all.shape[5]
    per_half, narrow = qkv_all.shape[4:]
    steps = z_count // 2
    plan = Plan()

    loads = [
        pltpu.make_async_copy(features.at[:, :, :, pl.ds(128 * half, 128)], feat.at[half], load_s.at[half])
        for half in range(2)
    ]
    for load in loads:
        load.start()
    barrier = pltpu.get_barrier_semaphore()
    peers = (
        [k.x_device(by) for by in range(1, X)] + [k.z_device(by) for by in range(1, z_count)]
        + [k.tm_device(by) for by in range(1, tm_count)]
    )
    for peer in peers:
        pl.semaphore_signal(barrier, inc=1, device_id=peer, device_id_type=pl.DeviceIdType.MESH)

    quarters = [
        pltpu.make_async_copy(
            proj.at[:, pl.ds(pl.multiple_of((2 * k.core + part) * wide, wide), wide)],
            proj_all.at[k.core, part, z, x], load_s.at[2 + part],
        )
        for part in range(2)
    ]
    piece = qkv.at[
        pl.ds(pl.multiple_of(lax.div(k.y, 4) * per_half, 8), per_half),
        pl.ds(pl.multiple_of(lax.rem(k.y, 4) * narrow, narrow), narrow),
    ]
    proj_w = Proj(k, proj_all, proj_sems)
    qkv_w = Qkv(k, piece, qkv_all, qkv_sems)
    for one in quarters:
        one.start()
    qkv_w.preload()
    weight_loads = [
        pltpu.make_async_copy(conv, conv_in, load_s.at[4]), pltpu.make_async_copy(out_weight, out_in, load_s.at[5])
    ]
    for one in weight_loads:
        one.start()

    lane = iota((8, 128), 1)
    row = iota((8, 128), 0)
    sums = []
    for load in loads:
        load.wait()
    for frame in range(frames):
        values = jnp.concatenate([feat[half, frame].reshape(height * columns, 128) for half in range(2)], axis=1)
        sums += [jnp.sum(values, axis=0, keepdims=True), jnp.sum(values * values, axis=0, keepdims=True)]
    stacked = jnp.concatenate(sums + [jnp.zeros((4, channels), f32)], axis=0)
    per_group = channels // GROUPS
    fold = (iota((channels, 128), 1) % GROUPS == iota((channels, 128), 0) // per_group).astype(f32)

    def lanes_of(rows_of_sums, table):
        return jnp.sum(jnp.where(lane // GROUPS == row, exact(rows_of_sums, table), 0.0), axis=0, keepdims=True)

    slab_sums[tm] = lanes_of(stacked, fold)
    for one in quarters:
        one.wait()

    def exchange(slots, index, per, size, device, n):
        return Sums(slots, index, per, size, device, sum_s.at[n], sum_r.at[n])

    over_tm = exchange(slab_sums, tm, 1, tm_count, k.tm_device, 0)
    over_x = exchange(x_sums, x, 1, X, k.x_device, 1)
    over_z = exchange(z_sums, z, 1, z_count, k.z_device, 2)
    tokens_z = exchange(token_z, z, 1, z_count, k.z_device, 3)
    tokens_x = exchange(token_x, x, 1, X, k.x_device, 4)

    pl.semaphore_wait(barrier, len(peers))
    over_tm.start()
    groups = 2 * (height // 2)
    group = count // groups

    def halo_copy(f, g):
        at = (slice(None), f, pl.ds(2 * (g // 2), 2), pl.ds(g % 2 * 2 * group, 2 * group))
        return copy(feat.at[at], halo.at[at], halo_s.at[f, g], halo_r.at[f, g], {"tm": mod(tm + 1, tm_count)})

    halo_copies = [halo_copy(f, g) for g in range(groups) for f in range(frames)]
    for one in halo_copies:
        one.start()
    proj_w.start()
    qkv_w.start()
    plan.now = 4.0

    def summed_tm():
        over_tm.wait()
        x_sums[x] = jnp.concatenate([slab_sums[i] for i in range(tm_count)], axis=0)
        over_x.start()

    def summed_x():
        over_x.wait()
        z_sums[z] = jnp.sum(x_sums[...], axis=0)
        over_z.start()

    plan.expect(6.4, "tm", summed_tm)
    plan.expect(9.0, "x", summed_x)
    plan.expect(7.8, "qkv x", qkv_w.across)
    plan.expect(6.8, "b", proj_w.b_start)
    plan.expect(7.5, "a", functools.partial(proj_w.a_pass, 0))
    for n in range(1, steps + 1):
        plan.expect(4.0 + 2.7 * n, "a", functools.partial(proj_w.a_step, n))
        plan.expect(7.0 + 2.7 * n, "a", functools.partial(proj_w.a_pass, n))
        for chunk in range(2):
            plan.expect(8.8 + 1.8 * (2 * n - 1 + chunk), "b", functools.partial(proj_w.b_step, n, chunk))
    plan.expect(7.1 + 2.7 * steps, "a", proj_w.a_near)
    plan.expect(10.0 + 2.7 * steps, "a far", proj_w.a_far)
    plan.expect(10.6, "collect", qkv_w.collect)
    plan.expect(12.0, "z", over_z.wait)
    for g in range(groups):
        for frame in range(frames):
            plan.expect(10.0 + 3.65 * g + 0.05 * frame, f"halo{g}", halo_copy(frame, g).wait_recv)
    plan.expect(10.2 + 3.65 * (groups - 1), "up", qkv_w.up)
    qkv_done = 12.6
    for step, way, chunk in qkv_w.first.each():
        time = (12.6 if way else 12.2 + 3.65 * (groups - 1)) + 1.7 * (2 * step - 1 + chunk)
        qkv_done = max(qkv_done, time)
        plan.expect(time, "qkv", functools.partial(qkv_w.first.step, step, way, chunk))
    plan.expect(qkv_done + 0.1, "rest", qkv_w.rest)
    plan.expect(qkv_done + 3.6, "qkv", functools.partial(qkv_w.wait, 0))
    for step, way, chunk in qkv_w.last.each():
        plan.expect(qkv_done + 5.0 + 2.5 * step, "qkv last", functools.partial(qkv_w.last.step, step, way, chunk))
    plan.expect(qkv_done + 7.0 + 2.5 * max(qkv_w.last.reach), "qkv last", functools.partial(qkv_w.wait, 1))

    def split_taps():
        weight_loads[0].wait()
        return [split(conv_in[lag]) for lag in range(3)]

    taps = plan.run(0.4, split_taps)

    def statistics():
        everything = jnp.sum(z_sums[...], axis=0)
        slab = iota(everything.shape, 0)

        def of(these):
            return jnp.sum(jnp.where(these, everything, 0.0), axis=0, keepdims=True)

        earlier, previous, own = of(slab < tm - 1), of(slab == tm - 1), of(slab == tm)
        kind, upto = row % 2, row // 2
        lane_kind, lane_frame = lane // GROUPS % 2, lane // GROUPS // 2
        mine = lane_kind == kind
        running = (
            jnp.where(mine, earlier, 0.0)
            + jnp.where(mine & (lane_frame <= upto), previous, 0.0)
            + jnp.where(mine & (lane_frame <= upto - 2), own, 0.0)
        )
        unfold = (iota((128, channels), 0) % GROUPS == iota((128, channels), 1) // per_group).astype(f32)
        running = exact(running, unfold)
        means, scales = [], []
        for i in range(4):
            position = jnp.maximum(tm * frames + i - 1, 1).astype(f32)
            cells = position * float(rows_count * height * columns * per_group)
            mean = running[2 * i : 2 * i + 1] / cells
            variance = running[2 * i + 1 : 2 * i + 2] / cells - mean * mean
            means.append(mean)
            scales.append(rsqrt(variance))
        return means, scales

    means, scales = plan.run(0.6, statistics, "z")
    norm_gain = gain[...]

    def cells_of(src, frame, g, b, c):
        place = pl.ds(g % 2 * 2 * group + c, group, stride=2)
        return jnp.concatenate([src[half, frame, 2 * (g // 2) + b, place, :] for half in range(2)], axis=1)

    def activate(src, frame, g, at):
        for b in range(2):
            for c in range(2):
                value = (cells_of(src, frame, g, b, c) - means[at]) * scales[at] * norm_gain
                value = value / (1.0 + jnp.exp(-value))
                if at < 2:
                    value = jnp.where(tm > 0, value, 0.0)
                high, low = split(value)
                place = pl.ds((2 * b + c) * group, group)
                act_hi[at, g, place] = high
                act_lo[at, g, place] = low

    def activated(at, these):
        return tuple(ref[at, these].reshape(-1, channels) for ref in (act_hi, act_lo))

    def convolve(frame, these, terms, first=False):
        value = functools.reduce(jnp.add, [dot3(activated(at, these), taps[lag]) for at, lag in terms])
        value = value.reshape((-1, 4 * group, channels))
        residual[frame, these] = value if first else residual[frame, these] + value

    def haar(g):
        bands = [
            residual[a, g, pl.ds((2 * b + c) * group, group)] + cells_of(feat, a, g, b, c)
            for a in range(2) for b in range(2) for c in range(2)
        ]
        for bit in (4, 2, 1):
            bands = [
                bands[j] + bands[j | bit] if not j & bit else bands[j ^ bit] - bands[j] for j in range(8)
            ]
        bands = [split(band * (1.0 / math.sqrt(8.0))) for band in bands]
        per_quarter = wide // channels
        place = pl.ds(g * group, group)
        for quarter in range(4):
            ours = bands[quarter * per_quarter : (quarter + 1) * per_quarter]
            band_hi[quarter, place] = jnp.concatenate([band[0] for band in ours], axis=1)
            band_lo[quarter, place] = jnp.concatenate([band[1] for band in ours], axis=1)

    wide = proj_all.shape[5]

    def split_quarter(half, part):
        at = 2 * half + part
        high, low = split(proj_all[half, part].reshape(width, wide))
        proj_hi[at] = high
        proj_lo[at] = low

    def quarter_of(half, part):
        at = 2 * half + part
        return dot3((band_hi[at], band_lo[at]), (proj_hi[at], proj_lo[at]), NT)

    every = pl.ds(0, groups)
    for frame in range(frames):
        plan.run(0.7, lambda: [activate(feat, frame, g, 2 + frame) for g in range(groups)])
    plan.run(0.5, lambda: convolve(0, every, [(2, 0)], True))
    plan.run(1.0, lambda: convolve(1, every, [(3, 0), (2, 1)], True))

    def join(g):
        for frame in range(frames):
            activate(halo, frame, g, frame)
        convolve(0, pl.ds(g, 1), [(1, 1), (0, 2)])
        convolve(1, pl.ds(g, 1), [(1, 2)])
        haar(g)

    other = 1 - k.core
    for g in range(groups - 1):
        plan.run(1.2, lambda: join(g), f"halo{g}")
    plan.run(0.3, lambda: split_quarter(k.core, 0), "a far")
    plan.run(1.2, lambda: join(groups - 1), f"halo{groups - 1}")
    made = plan.run(0.5, lambda: quarter_of(k.core, 0))
    proj_w.wait(0)
    plan.run(0.3, lambda: split_quarter(other, 0))
    made = made + plan.run(0.5, lambda: quarter_of(other, 0))
    plan.run(0.3, lambda: split_quarter(k.core, 1), "b")
    made = made + plan.run(0.5, lambda: quarter_of(k.core, 1))
    proj_w.wait(1)
    plan.run(0.3, lambda: split_quarter(other, 1))
    made = made + plan.run(0.5, lambda: quarter_of(other, 1))
    tokens_out[...] = made.reshape(tokens_out.shape)
    keys[z] = made
    queries[x] = made

    part_rows = count // 2
    key_chunks = 4
    key_rows = count // key_chunks
    key_ring = Ring(z, z_count, k.z_device, lambda at, c: keys.at[at, pl.ds(c * key_rows, key_rows)],
                    key_s, key_r, (steps, steps), key_chunks)
    query_ring = Ring(x, X, k.x_device, lambda at, c: queries.at[at], query_s, query_r, (X // 2, X // 2), 1,
                      lambda ref, way: ref.at[pl.ds(way * part_rows, part_rows)])
    token_group = width // GROUPS
    sums = jnp.concatenate(
        [jnp.sum(made, axis=0, keepdims=True), jnp.sum(made * made, axis=0, keepdims=True), jnp.zeros((6, width), f32)],
        axis=0,
    )
    fold = (iota((width, 128), 1) % GROUPS == iota((width, 128), 0) // token_group).astype(f32)
    token_z[z] = lanes_of(sums, fold)
    tokens_z.start()
    for way in BOTH:
        query_ring.start(way, 0)
    for chunk in range(key_chunks):
        for way in BOTH:
            key_ring.start(way, chunk)
    begin = plan.now
    for step, way, chunk in key_ring.each():
        turn = chunk if step < steps else chunk % (key_chunks // 2)
        plan.expect(begin + 2.0 + 1.5 * (key_chunks * (step - 1) + turn + 1), f"key{step}",
                    functools.partial(key_ring.step, step, way, chunk))

    def token_summed_z():
        tokens_z.wait()
        token_x[x] = jnp.sum(token_z[...], axis=0)
        tokens_x.start()

    plan.expect(begin + 2.5, "tokens z", token_summed_z)
    plan.expect(begin + 7.7, "tokens x", tokens_x.wait)
    for step, way, chunk in query_ring.each():
        plan.expect(begin + 4.9 * step + 2.9, ("near", "far")[step - 1], functools.partial(query_ring.step, step, way, chunk))

    def token_statistics():
        all_sums = jnp.sum(token_x[...], axis=0)
        unfold = (iota((128, width), 0) % GROUPS == iota((128, width), 1) // token_group).astype(f32)
        spread_sums = exact(jnp.where(lane // GROUPS == row, all_sums, 0.0), unfold)
        token_count = float(rows_count * count * token_group)
        mean = spread_sums[0:1] / token_count
        return mean, rsqrt(spread_sums[1:2] / token_count - mean * mean)

    def columns_of(block):
        lanes = []
        for lane_at in range(4):
            chunks = []
            for at in range(block * width // per_half, (block + 1) * width // per_half + 1):
                owner, part = at // 2, at % 2
                if owner < rows_count:
                    own_z, own_x = owner // X, owner % X
                    chunks.append(qkv_all[own_z % 2, 4 * part + lane_at, own_z // 2, own_x])
            skip = block * width - block * width // per_half * per_half
            lanes.append(jnp.concatenate(chunks, axis=0)[skip : skip + width])
        return split(jnp.concatenate(lanes, axis=1))

    def query_key_weight():
        query_weight = tuple(jnp.transpose(part.astype(f32)).astype(bf16) for part in columns_of(0))
        return split(dot3(query_weight, columns_of(1)) * (1.0 / math.sqrt(float(width))))

    order = (2, 1, 3, 0)

    def ask(first, last):
        asking = jnp.concatenate([queries[mod(x + by, X)] for by in (2, 1, 3, 0)[first:last]], axis=0)
        for ref, value in zip((q_hi, q_lo), split(dot3(normed(asking), query_key))):
            ref[first:last] = value.reshape((last - first, count, width))

    query_key = plan.run(2.0, query_key_weight, "qkv")
    token_mean, token_scale = plan.run(0.6, token_statistics, "tokens x")
    token_gain = attn_gain[...]

    def normed(value):
        return split((value - token_mean) * token_scale * token_gain)

    plan.run(1.3, lambda: ask(1, X), "near")

    sets = [(0, -1, 1)] + [(-step, step) for step in range(2, steps)] + [(steps,)]

    def key_block(at):
        return normed(jnp.concatenate([keys[mod(z + away, z_count)] for away in sets[at]], axis=0))

    def rows_of(ref, at):
        return ref[at].reshape(-1, ref.shape[-1])

    def scores_of(at, block):
        return dot3((rows_of(q_hi, at), rows_of(q_lo, at)), block, NT)

    def attend(first, at, block, scores):
        here = jnp.max(scores, axis=1, keepdims=True)
        if first:
            weights = jnp.exp(scores - here)
            return here, jnp.sum(weights, axis=1, keepdims=True), dot3(split(weights), block)
        new_top = jnp.maximum(rows_of(top, at), here)
        fade = jnp.exp(rows_of(top, at) - new_top)
        weights = jnp.exp(scores - new_top)
        new_mass = rows_of(mass, at) * fade + jnp.sum(weights, axis=1, keepdims=True)
        return new_top, new_mass, rows_of(total, at) * fade + dot3(split(weights), block)

    def attend_all(first, at, block, scores):
        for ref, value in zip((top, mass, total), attend(first, at, block, scores)):
            ref[at] = value.reshape(-1, count, value.shape[-1])

    near, far, both = slice(1, X), slice(0, 1), slice(0, X)
    block = plan.run(0.2, lambda: key_block(0), "key1")
    scores = plan.run(1.0, lambda: scores_of(near, block))
    plan.run(1.4, lambda: attend_all(True, near, block, scores))
    plan.run(0.6, lambda: ask(0, 1), "far")
    scores = plan.run(0.5, lambda: scores_of(far, block))
    plan.run(0.6, lambda: attend_all(True, far, block, scores))
    for step in range(1, len(sets) - 1):
        block = plan.run(0.2, lambda: key_block(step), f"key{step + 1}")
        scores = plan.run(0.9, lambda: scores_of(both, block))
        plan.run(1.2, lambda: attend_all(False, both, block, scores))

    half_rows = [pl.ds(way * part_rows, part_rows) for way in BOTH]
    toward = (1, -1)

    def send(kind, way, src, dst):
        return copy(src, dst, part_s.at[kind, way], part_r.at[kind, way], k.x_device(toward[way]))

    def opposite(way):
        return (send(0, way, partial.at[0, half_rows[way]], relay.at[way]),
                send(1, way, lse_mine.at[0], relay_lse.at[way]))

    def plain(way):
        return (send(2, way, partial.at[1 + way, half_rows[1 - way]], parts.at[way, half_rows[1 - way]]),)

    def joined(way):
        return (send(3, way, joint.at[way], parts.at[way, half_rows[way]]), send(4, way, joint_lse.at[way], parts_lse.at[way]))

    def as_column(lanes):
        return jnp.transpose(jnp.broadcast_to(lanes, (count, 128)))

    def across(column):
        return jnp.concatenate([column] * (width // 128), axis=1)

    plan.need(f"key{steps}")
    block = key_block(-1)
    for first, last in ((0, 1), (1, X)):
        at = slice(first, last)
        last_top, last_mass, value = attend(False, at, block, scores_of(at, block))
        partial[at] = (value / last_mass).reshape(last - first, count, width)
        lse = last_top + jnp.log(last_mass)
        for i in range(first, last):
            column = lse[(i - first) * count : (i + 1 - first) * count]
            lse_mine[i] = jnp.transpose(jnp.broadcast_to(column, (count, 128)))[0:1]
        for way in BOTH:
            for one in opposite(way) if first == 0 else plain(way):
                one.start()
    plan.now += 1.5

    def value_to_out():
        weight_loads[1].wait()
        value_weight = tuple(jnp.transpose(part.astype(f32)).astype(bf16) for part in columns_of(2))
        return split(dot3(value_weight, split(out_in[...])))

    value_out = plan.run(2.0, value_to_out, "qkv last")
    plan.upto(1e9)
    lane_row = iota((1, 128), 1)
    for way in BOTH:
        for one in opposite(way):
            one.wait_recv()
        at = 1 + way
        own, theirs = lse_mine[at], relay_lse[way]
        both = jnp.maximum(own, theirs)
        both = both + jnp.log(jnp.exp(own - both) + jnp.exp(theirs - both))
        rows_of_way = slice(way * part_rows, (way + 1) * part_rows)
        joint[way] = (
            partial[at, half_rows[way]] * across(as_column(jnp.exp(own - both))[rows_of_way])
            + relay[way] * across(as_column(jnp.exp(theirs - both))[rows_of_way])
        )
        joint_lse[way] = jnp.where(lane_row // part_rows == way, both, own)
        for one in joined(way):
            one.start()

    proj_w.finish()
    qkv_w.finish()
    for one in halo_copies:
        one.wait_send()
    for one in (over_tm, over_x, over_z, tokens_x, tokens_z):
        one.finish()
    key_ring.finish()
    query_ring.finish()
    for way in BOTH:
        for one in (*plain(way), *joined(way)):
            one.wait_recv()
    given = [(lse_mine[3], partial[3])] + [(parts_lse[way], parts[way]) for way in BOTH]
    highest_lse = functools.reduce(jnp.maximum, [lse for lse, _ in given])
    shares = [jnp.exp(lse - highest_lse) for lse, _ in given]
    whole = functools.reduce(jnp.add, shares)
    merged = jnp.zeros((count, width), f32)
    for share, (_, value) in zip(shares, given):
        merged = merged + value * across(as_column(share / whole))
    out[...] = dot3(split(merged), value_out).reshape(out.shape)

    for way in BOTH:
        for one in (*opposite(way), *plain(way), *joined(way)):
            one.wait_send()


def shards(z_count, tm_count, features, norm_gain, conv_weight, proj_weight, attn_gain, qkv_weight, out_weight):
    frames, height, columns, channels = features.shape
    width = out_weight.shape[0]
    half_h, half_w = height // 2, columns // 2
    count = half_h * half_w
    steps = z_count // 2
    rows_count = z_count * X
    proj_rows, qkv_rows = proj_weight.shape[1], qkv_weight.shape[1] // 2
    wide, narrow = proj_weight.shape[0] // 4, qkv_weight.shape[0] // 4
    y_count = tm_count // 2
    far = y_count - 1 - (y_count - 1) // 3
    vmem = pltpu.VMEM
    dma = pltpu.SemaphoreType.DMA
    proj_sems = [dma((2, steps)), dma((2, steps)), dma((3, z_count)), dma((3, z_count)), dma((X,)), dma((X,)), dma((4, steps)),
                 dma((4, steps)), dma((2,)), dma((2,))]
    qkv_sems = [dma((1,)), dma((1,)), dma((1,)), dma((1,)), dma((1,)), dma((4, far)), dma((4, far)), dma((2, far)),
                dma((2, far)), dma((2,)), dma((2,))]
    scratch = [
        vmem((2, frames, height, columns, 128), f32), vmem((2, frames, height, columns, 128), f32),
        vmem(conv_weight.shape, f32), vmem(out_weight.shape, f32),
        vmem((X, tm_count, 128), f32), vmem((z_count, tm_count, 128), f32), vmem((tm_count, 1, 128), f32),
        vmem((X, 1, 128), f32), vmem((z_count, 1, 128), f32),
        vmem((2, 2, z_count, X, proj_rows, wide), f32),
        vmem((2, y_count, z_count // 2, X, qkv_rows, narrow), f32),
        vmem((4, 2 * half_h, 2 * half_w, channels), bf16), vmem((4, 2 * half_h, 2 * half_w, channels), bf16),
        vmem((frames, 2 * half_h, 2 * half_w, channels), f32),
        vmem((4, count, wide), bf16), vmem((4, count, wide), bf16),
        vmem((4, width, wide), bf16), vmem((4, width, wide), bf16),
        vmem((z_count, count, width), f32),
        vmem((X, count, width), f32),
        vmem((X, count, width), bf16), vmem((X, count, width), bf16),
        vmem((X, count, width), f32), vmem((X, count, 1), f32), vmem((X, count, 1), f32),
        vmem((X, count, width), f32), vmem((X, 1, 128), f32),
        vmem((2, count // 2, width), f32), vmem((2, 1, 128), f32),
        vmem((2, count // 2, width), f32), vmem((2, 1, 128), f32),
        vmem((2, count, width), f32), vmem((2, 1, 128), f32),
        dma((6,)), dma((frames, 2 * half_h)), dma((frames, 2 * half_h)), dma((6,)), dma((6,)),
        *proj_sems, *qkv_sems,
        dma((8, steps)), dma((8, steps)), dma((2, X // 2)), dma((2, X // 2)), dma((5, 2)), dma((5, 2)),
    ]
    whole = pl.BlockSpec(memory_space=vmem)
    anywhere = pl.BlockSpec(memory_space=pl.ANY)
    given = jax.ShapeDtypeStruct((frames // 2, half_h, half_w, width), f32)
    tokens, attended = pl.pallas_call(
        functools.partial(kernel, z_count, tm_count),
        out_shape=(given, given),
        in_specs=[anywhere, whole, anywhere, anywhere, whole, anywhere, anywhere],
        out_specs=(whole, whole),
        scratch_shapes=scratch,
        compiler_params=pltpu.CompilerParams(collective_id=0, has_side_effects=True, vmem_limit_bytes=56 * 2**20),
    )(features, norm_gain[None], conv_weight, proj_weight.T, attn_gain[None], qkv_weight.T, out_weight)
    return tokens + attended


def solution(mesh):
    in_specs = (P("tm", "rows", None, None), P(), P(), P(None, "rows"), P(), P(None, "rows"), P())
    out_specs = P("tm", "rows", None, None)
    body = functools.partial(shards, mesh.shape["rows"] // X, mesh.shape["tm"])
    return jax.shard_map(body, mesh=mesh, in_specs=in_specs, out_specs=out_specs, check_vma=False)
```

```python
import functools
import math

import jax
import jax.numpy as jnp
from jax import lax
from jax.experimental import pallas as pl
from jax.experimental.pallas import tpu as pltpu
from jax.sharding import PartitionSpec as P

GROUPS = 32
X = 4
epsilon = 1e-06
f32, bf16 = jnp.float32, jnp.bfloat16
NN = (((1,), (0,)), ((), ()))
NT = (((1,), (1,)), ((), ()))
BOTH = (0, 1)


def split(value):
    high = value.astype(bf16)
    return high, (value - high.astype(f32)).astype(bf16)


def dot(a, b, dims):
    return lax.dot_general(a, b, dims, preferred_element_type=f32)


def dot3(a, b, dims=NN):
    rows = a[0].shape[0]
    if rows > 256:
        deep = (b[0], b[0], b[1])
        return dot(jnp.concatenate((a[0], a[1], a[0]), axis=1), jnp.concatenate(deep, axis=dims[0][1][0]), dims)
    by_high = dot(jnp.concatenate(a, axis=0), b[0], dims)
    return by_high[:rows] + (by_high[rows:] + dot(a[0], b[1], dims))


def exact(a, table):
    high = a.astype(bf16)
    rest = a - high.astype(f32)
    middle = rest.astype(bf16)
    low = (rest - middle.astype(f32)).astype(bf16)
    rows = a.shape[0]
    parts = jnp.concatenate([part.astype(f32) for part in (high, middle, low)] + [jnp.zeros_like(a)], axis=0).astype(bf16)
    by_part = dot(parts, table.astype(bf16), NN)
    return by_part[:rows] + (by_part[rows : 2 * rows] + by_part[2 * rows : 3 * rows])


def iota(shape, axis):
    return lax.broadcasted_iota(jnp.int32, shape, axis)


def rsqrt(value):
    return lax.rsqrt(value + epsilon)


def mod(value, size):
    return lax.rem(value + size, size)


class Plan:
    def __init__(self):
        self.now, self.waits = 0.0, []

    def expect(self, time, name, action):
        self.waits.append((time, len(self.waits), name, action))

    def upto(self, time):
        while True:
            due = [wait for wait in self.waits if wait[0] <= time]
            if not due:
                return
            first = min(due, key=lambda wait: wait[:2])
            self.waits.remove(first)
            first[3]()

    def need(self, name):
        times = [wait[0] for wait in self.waits if wait[2] == name]
        if times:
            self.now = max(self.now, max(times))
            self.upto(max(times))

    def run(self, duration, action, *needs):
        for name in needs:
            self.need(name)
        self.upto(self.now)
        result = action()
        self.now += duration
        return result


class Links:
    def __init__(self, z_count, x_count, tm_count):
        self.rows, self.tm = lax.axis_index("rows"), lax.axis_index("tm")
        self.z, self.x = lax.div(self.rows, x_count), lax.rem(self.rows, x_count)
        self.y, self.core = lax.div(self.tm, 2), lax.rem(self.tm, 2)
        self.z_count, self.x_count, self.y_count = z_count, x_count, tm_count // 2

    def z_device(self, by):
        return {"rows": mod(self.z + by, self.z_count) * self.x_count + self.x}

    def x_device(self, by):
        return {"rows": self.z * self.x_count + mod(self.x + by, self.x_count)}

    def y_device(self, by):
        return {"tm": mod(self.y + by, self.y_count) * 2 + self.core}

    def tm_device(self, by):
        return {"tm": mod(self.tm + by, 2 * self.y_count)}

    def sibling(self):
        return {"tm": self.tm + 1 - 2 * self.core}


def copy(src, dst, send, recv, device):
    return pltpu.make_async_remote_copy(
        src_ref=src, dst_ref=dst, send_sem=send, recv_sem=recv, device_id=device,
        device_id_type=pl.DeviceIdType.MESH,
    )


class Ring:
    def __init__(self, place, count, device, at, send, recv, reach, chunks=1, half=None, arrived=None):
        self.place, self.count, self.device, self.at, self.half = place, count, device, at, half
        self.send, self.recv, self.reach, self.chunks, self.arrived = send, recv, reach, chunks, arrived

    def moves(self, step, way, chunk):
        if step > self.reach[way]:
            return False
        shared = step == self.reach[0] == self.reach[1] and 2 * step == self.count
        return not shared or self.chunks == 1 or chunk // (self.chunks // 2) == way

    def ref(self, away, step, way, chunk):
        ref = self.at(mod(self.place + away, self.count), chunk)
        return self.half(ref, way) if self.half and 2 * step == self.count else ref

    def copy(self, step, way, chunk, away):
        ref = self.ref(away, step, way, chunk)
        at = (way * self.chunks + chunk, step - 1)
        return copy(ref, ref, self.send.at[at], self.recv.at[at], self.device(1 if way == 0 else -1))

    def outgoing(self, step, way, chunk):
        return self.copy(step, way, chunk, 1 - step if way == 0 else step - 1)

    def start(self, way, chunk):
        self.outgoing(1, way, chunk).start()

    def step(self, step, way, chunk):
        if not self.moves(step, way, chunk):
            return
        away = -step if way == 0 else step
        self.copy(step, way, chunk, away).wait_recv()
        if self.moves(step + 1, way, chunk):
            self.outgoing(step + 1, way, chunk).start()
        if self.arrived:
            self.arrived(self.ref(away, step, way, chunk))

    def each(self):
        for step in range(1, max(self.reach) + 1):
            for chunk in range(self.chunks):
                for way in BOTH:
                    if self.moves(step, way, chunk):
                        yield step, way, chunk

    def finish(self):
        for step, way, chunk in self.each():
            self.outgoing(step, way, chunk).wait_send()


class Sums:
    def __init__(self, slots, index, per, size, device, send, recv):
        self.slots, self.index, self.per, self.size, self.device = slots, index, per, size, device
        self.send, self.recv = send, recv

    def copies(self, by):
        ref = self.slots.at[pl.ds(self.index * self.per, self.per)]
        return copy(ref, ref, self.send, self.recv, self.device(by))

    def everything(self):
        ref = self.slots.at[pl.ds(0, (self.size - 1) * self.per)]
        return copy(ref, ref, self.send, self.recv, self.device(1))

    def start(self):
        for by in range(1, self.size):
            self.copies(by).start()

    def wait(self):
        self.everything().wait_recv()

    def finish(self):
        self.everything().wait_send()


class Proj:
    def __init__(self, links, buf, sems):
        self.k, self.buf = links, buf
        az_s, az_r, self.ax_s, self.ax_r, self.bx_s, self.bx_r, bz_s, bz_r, self.c_s, self.c_r = sems
        self.core = links.core
        rows, xs, steps = buf.shape[4] // 2, links.x_count // 2, links.z_count // 2
        self.first = Ring(links.z, links.z_count, links.z_device, lambda z, chunk: buf.at[self.core, 0, z, links.x],
                          az_s, az_r, (steps, steps), 1, lambda ref, way: ref.at[pl.ds(way * rows, rows)])
        self.second = Ring(links.z, links.z_count, links.z_device,
                           lambda z, chunk: buf.at[self.core, 1, z, pl.ds(chunk * xs, xs)],
                           bz_s, bz_r, (steps, steps), 2, None, self.hand_second)
        self.steps = steps

    def block(self, away, x_away):
        return self.buf.at[self.core, 0, mod(self.k.z + away, self.k.z_count), mod(self.k.x + x_away, self.k.x_count)]

    def ax(self, kind, away, x_away):
        ref = self.block(away, x_away)
        up = self.goes_up(away) if kind == 2 else kind == 0
        at = (kind, away % self.k.z_count)
        return copy(ref, ref, self.ax_s.at[at], self.ax_r.at[at], self.k.x_device(1 if up else -1))

    def goes_up(self, away):
        return away % self.k.z_count < self.steps

    def a_out(self, away):
        for kind in range(2):
            self.ax(kind, away, 0).start()

    def a_on(self, away):
        for kind, x_away in enumerate((-1, 1)):
            self.ax(kind, away, x_away).wait_recv()
        self.ax(2, away, -1 if self.goes_up(away) else 1).start()

    def aways(self, n):
        return (0,) if n == 0 else (-n, n) if n < self.steps else (n,)

    def bx(self, by, away):
        ref = self.buf.at[self.core, 1, self.k.z, mod(self.k.x + away, self.k.x_count)]
        return copy(ref, ref, self.bx_s.at[by], self.bx_r.at[by], self.k.x_device(by))

    def hand(self, part, ref):
        return copy(ref, ref, self.c_s.at[part], self.c_r.at[part], self.k.sibling())

    def hand_second(self, ref):
        self.hand(1, ref).start()

    def start(self):
        for by in range(1, self.k.x_count):
            self.bx(by, 0).start()
        for way in BOTH:
            self.first.start(way, 0)
        self.a_out(0)

    def a_step(self, n):
        for way in BOTH:
            self.first.step(n, way, 0)
        for away in self.aways(n):
            self.a_out(away)

    def a_pass(self, n):
        for away in self.aways(n):
            self.a_on(away)

    def b_start(self):
        for by in range(1, self.k.x_count):
            self.bx(by, -by).wait_recv()
        for chunk in range(2):
            for way in BOTH:
                self.second.start(way, chunk)
        self.hand(1, self.buf.at[self.core, 1, self.k.z]).start()

    def b_step(self, n, chunk):
        for way in BOTH:
            self.second.step(n, way, chunk)

    def a_hand(self, by):
        self.hand(0, self.buf.at[self.core, 0, :, mod(self.k.x + by, self.k.x_count)]).start()

    def a_near(self):
        for by in (0, -1, 1):
            self.a_hand(by)

    def a_far(self):
        for away in range(self.k.z_count):
            self.ax(2, away, 2).wait_recv()
        self.a_hand(2)

    def wait(self, part):
        self.hand(part, self.buf.at[1 - self.core, part]).wait_recv()

    def finish(self):
        self.first.finish()
        self.second.finish()
        for by in range(1, self.k.x_count):
            self.bx(by, 0).wait_send()
        for away in range(self.k.z_count):
            for kind in range(3):
                self.ax(kind, away, 0).wait_send()
        for part in range(2):
            self.hand(part, self.buf.at[self.core, part]).wait_send()


class Qkv:
    def __init__(self, links, piece, buf, sems):
        self.k, self.buf, self.source = links, buf, piece
        self.load_s, x_s, x_r, self.z_s, self.z_r, e_s, e_r, l_s, l_r, self.c_s, self.c_r = sems
        self.zs, self.xs = buf.shape[2], buf.shape[3]
        self.early = early = self.zs * 3 // 4
        places, self.quarter = 4, lax.rem(links.y, 4)
        reach = (1, 2)
        half = self.xs // 2
        mine = lambda y, *rest: buf.at[(links.core, y, *rest)]
        self.first = Ring(self.quarter, places, links.y_device,
                          lambda y, c: mine(y, pl.ds(0, early), pl.ds(c * half, half)),
                          e_s, e_r, reach, 2, None, lambda ref: self.hand(0, ref).start())
        self.last = Ring(self.quarter, places, links.y_device, lambda y, c: mine(y, pl.ds(early, self.zs - early)),
                         l_s, l_r, reach, 1, None, lambda ref: self.hand(1, ref).start())
        halves = self.zs // 2
        self.over_x = Ring(links.x, links.x_count, links.x_device, lambda x, c: mine(self.quarter, slice(None), x), x_s, x_r,
                           (links.x_count // 2,) * 2, 1, lambda ref, way: ref.at[pl.ds(way * halves, halves)])
        self.sends = lax.rem(links.z, 2) == links.core
        self.zz = lax.div(links.z, 2)

    def load(self):
        return pltpu.make_async_copy(self.source, self.buf.at[self.k.core, self.quarter, self.zz, self.k.x], self.load_s.at[0])

    def preload(self):
        pl.when(self.sends)(lambda: self.load().start())

    def z_copy(self, by):
        ref = self.buf.at[self.k.core, self.quarter, self.zz, self.k.x]
        return copy(ref, ref, self.z_s.at[by], self.z_r.at[0], self.k.z_device(by))

    def start(self):
        @pl.when(self.sends)
        def _():
            self.load().wait()
            for by in range(1, self.k.z_count):
                self.z_copy(by).start()

    def across(self):
        def got(count):
            ref = self.buf.at[self.k.core, self.quarter, pl.ds(0, count), self.k.x]
            copy(ref, ref, self.z_s.at[0], self.z_r.at[0], self.k.z_device(1)).wait_recv()

        pl.when(self.sends)(lambda: got(self.zs - 1))
        pl.when(jnp.logical_not(self.sends))(lambda: got(self.zs))
        for way in BOTH:
            self.over_x.start(way, 0)

    def pass_x(self):
        for way in BOTH:
            self.over_x.step(1, way, 0)

    def collect(self):
        for way in BOTH:
            self.over_x.step(2, way, 0)
        for chunk in range(2):
            self.first.start(1, chunk)
        for part in range(2):
            self.hand(part, self.part_of(part, self.k.core, self.quarter)).start()

    def up(self):
        for chunk in range(2):
            self.first.start(0, chunk)

    def rest(self):
        for way in BOTH:
            self.last.start(way, 0)

    def hand(self, part, ref):
        return copy(ref, ref, self.c_s.at[part], self.c_r.at[part], self.k.sibling())

    def part_of(self, part, core, y):
        zs = pl.ds(0, self.early) if part == 0 else pl.ds(self.early, self.zs - self.early)
        return self.buf.at[core, y, zs]

    def all_of(self, part, core):
        return self.hand(part, self.part_of(part, core, slice(None)))

    def wait(self, part):
        self.all_of(part, 1 - self.k.core).wait_recv()

    def finish(self):
        self.first.finish()
        self.last.finish()
        for part in range(2):
            self.all_of(part, self.k.core).wait_send()

        self.over_x.finish()

        @pl.when(self.sends)
        def _():
            for by in range(1, self.k.z_count):
                self.z_copy(by).wait_send()


def kernel(
    z_count, tm_count,
    features, gain, conv, proj, attn_gain, qkv, out_weight, tokens_out, out,
    feat, halo, conv_in, out_in, x_sums, z_sums, slab_sums, token_x, token_z,
    proj_all, qkv_all, act_hi, act_lo, residual, band_hi, band_lo, proj_hi, proj_lo, keys, queries, q_hi, q_lo, total, top, mass,
    partial, lse_mine, relay, relay_lse, joint, joint_lse, parts, parts_lse,
    load_s, halo_s, halo_r, sum_s, sum_r, *sems,
):
    proj_sems, qkv_sems, sems = sems[:10], sems[10:21], sems[21:]
    key_s, key_r, query_s, query_r, part_s, part_r = sems
    k = Links(z_count, X, tm_count)
    rows_count = z_count * X
    tm, z, x = k.tm, k.z, k.x
    frames, height, columns, channels = features.shape
    half_w = columns // 2
    count = (height // 2) * half_w
    width = keys.shape[2]
    wide = proj_all.shape[5]
    per_block, narrow = qkv_all.shape[4:]
    steps = z_count // 2
    plan = Plan()

    loads = [
        pltpu.make_async_copy(features.at[:, :, :, pl.ds(128 * half, 128)], feat.at[half], load_s.at[half])
        for half in range(2)
    ]
    for load in loads:
        load.start()
    barrier = pltpu.get_barrier_semaphore()
    peers = (
        [k.x_device(by) for by in range(1, X)] + [k.z_device(by) for by in range(1, z_count)]
        + [k.tm_device(by) for by in range(1, tm_count)]
    )
    for peer in peers:
        pl.semaphore_signal(barrier, inc=1, device_id=peer, device_id_type=pl.DeviceIdType.MESH)

    quarters = [
        pltpu.make_async_copy(
            proj.at[:, pl.ds(pl.multiple_of((2 * k.core + part) * wide, wide), wide)],
            proj_all.at[k.core, part, z, x], load_s.at[2 + part],
        )
        for part in range(2)
    ]
    piece = qkv.at[:, pl.ds(pl.multiple_of(lax.rem(k.y, 4) * narrow, narrow), narrow)]
    proj_w = Proj(k, proj_all, proj_sems)
    qkv_w = Qkv(k, piece, qkv_all, qkv_sems)
    for one in quarters:
        one.start()
    qkv_w.preload()
    weight_loads = [
        pltpu.make_async_copy(conv, conv_in, load_s.at[4]), pltpu.make_async_copy(out_weight, out_in, load_s.at[5])
    ]
    for one in weight_loads:
        one.start()

    lane = iota((8, 128), 1)
    row = iota((8, 128), 0)
    sums = []
    for load in loads:
        load.wait()
    for frame in range(frames):
        values = jnp.concatenate([feat[half, frame].reshape(height * columns, 128) for half in range(2)], axis=1)
        sums += [jnp.sum(values, axis=0, keepdims=True), jnp.sum(values * values, axis=0, keepdims=True)]
    stacked = jnp.concatenate(sums + [jnp.zeros((4, channels), f32)], axis=0)
    per_group = channels // GROUPS
    fold = (iota((channels, 128), 1) % GROUPS == iota((channels, 128), 0) // per_group).astype(f32)

    def lanes_of(rows_of_sums, table):
        return jnp.sum(jnp.where(lane // GROUPS == row, exact(rows_of_sums, table), 0.0), axis=0, keepdims=True)

    slab_sums[tm] = lanes_of(stacked, fold)
    for one in quarters:
        one.wait()

    def exchange(slots, index, per, size, device, n):
        return Sums(slots, index, per, size, device, sum_s.at[n], sum_r.at[n])

    over_tm = exchange(slab_sums, tm, 1, tm_count, k.tm_device, 0)
    over_x = exchange(x_sums, x, 1, X, k.x_device, 1)
    over_z = exchange(z_sums, z, 1, z_count, k.z_device, 2)
    tokens_z = exchange(token_z, z, 1, z_count, k.z_device, 3)
    tokens_x = exchange(token_x, x, 1, X, k.x_device, 4)

    pl.semaphore_wait(barrier, len(peers))
    over_tm.start()
    groups = 2 * (height // 2)
    group = count // groups

    def halo_copy(f, g):
        at = (slice(None), f, pl.ds(2 * (g // 2), 2), pl.ds(g % 2 * 2 * group, 2 * group))
        return copy(feat.at[at], halo.at[at], halo_s.at[f, g], halo_r.at[f, g], {"tm": mod(tm + 1, tm_count)})

    halo_copies = [halo_copy(f, g) for g in range(groups) for f in range(frames)]
    for one in halo_copies:
        one.start()
    proj_w.start()
    qkv_w.start()
    plan.now = 4.0

    def summed_tm():
        over_tm.wait()
        x_sums[x] = jnp.concatenate([slab_sums[i] for i in range(tm_count)], axis=0)
        over_x.start()

    def summed_x():
        over_x.wait()
        z_sums[z] = jnp.sum(x_sums[...], axis=0)
        over_z.start()

    plan.expect(6.4, "tm", summed_tm)
    plan.expect(9.0, "x", summed_x)
    plan.expect(7.8, "qkv x", qkv_w.across)
    plan.expect(6.8, "b", proj_w.b_start)
    plan.expect(7.5, "a", functools.partial(proj_w.a_pass, 0))
    for n in range(1, steps + 1):
        plan.expect(4.0 + 2.7 * n, "a", functools.partial(proj_w.a_step, n))
        plan.expect(7.0 + 2.7 * n, "a", functools.partial(proj_w.a_pass, n))
        for chunk in range(2):
            plan.expect(8.8 + 1.8 * (2 * n - 1 + chunk), "b", functools.partial(proj_w.b_step, n, chunk))
    plan.expect(7.1 + 2.7 * steps, "a", proj_w.a_near)
    plan.expect(10.0 + 2.7 * steps, "a far", proj_w.a_far)
    plan.expect(10.3, "qkv x", qkv_w.pass_x)
    plan.expect(13.0, "collect", qkv_w.collect)
    plan.expect(12.0, "z", over_z.wait)
    for g in range(groups):
        for frame in range(frames):
            plan.expect(10.0 + 3.65 * g + 0.05 * frame, f"halo{g}", halo_copy(frame, g).wait_recv)
    plan.expect(16.5, "up", qkv_w.up)
    qkv_done = 0.0
    for step, way, chunk in qkv_w.first.each():
        time = (15.0 if way else 18.5) + 3.2 * (2 * step - 1 + chunk)
        qkv_done = max(qkv_done, time)
        plan.expect(time, "qkv", functools.partial(qkv_w.first.step, step, way, chunk))
    plan.expect(qkv_done + 0.1, "rest", qkv_w.rest)
    plan.expect(qkv_done + 1.7, "qkv", functools.partial(qkv_w.wait, 0))
    for step, way, chunk in qkv_w.last.each():
        plan.expect(qkv_done + 5.0 + 2.5 * step, "qkv last", functools.partial(qkv_w.last.step, step, way, chunk))
    plan.expect(qkv_done + 7.0 + 2.5 * max(qkv_w.last.reach), "qkv last", functools.partial(qkv_w.wait, 1))

    def split_taps():
        weight_loads[0].wait()
        return [split(conv_in[lag]) for lag in range(3)]

    taps = plan.run(0.4, split_taps)

    def statistics():
        everything = jnp.sum(z_sums[...], axis=0)
        slab = iota(everything.shape, 0)

        def of(these):
            return jnp.sum(jnp.where(these, everything, 0.0), axis=0, keepdims=True)

        earlier, previous, own = of(slab < tm - 1), of(slab == tm - 1), of(slab == tm)
        kind, upto = row % 2, row // 2
        lane_kind, lane_frame = lane // GROUPS % 2, lane // GROUPS // 2
        mine = lane_kind == kind
        running = (
            jnp.where(mine, earlier, 0.0)
            + jnp.where(mine & (lane_frame <= upto), previous, 0.0)
            + jnp.where(mine & (lane_frame <= upto - 2), own, 0.0)
        )
        unfold = (iota((128, channels), 0) % GROUPS == iota((128, channels), 1) // per_group).astype(f32)
        running = exact(running, unfold)
        means, scales = [], []
        for i in range(4):
            position = jnp.maximum(tm * frames + i - 1, 1).astype(f32)
            cells = position * float(rows_count * height * columns * per_group)
            mean = running[2 * i : 2 * i + 1] / cells
            variance = running[2 * i + 1 : 2 * i + 2] / cells - mean * mean
            means.append(mean)
            scales.append(rsqrt(variance))
        return means, scales

    means, scales = plan.run(0.6, statistics, "z")
    norm_gain = gain[...]

    def cells_of(src, frame, g, b, c):
        place = pl.ds(g % 2 * 2 * group + c, group, stride=2)
        return jnp.concatenate([src[half, frame, 2 * (g // 2) + b, place, :] for half in range(2)], axis=1)

    def activate(src, frame, g, at):
        for b in range(2):
            for c in range(2):
                value = (cells_of(src, frame, g, b, c) - means[at]) * scales[at] * norm_gain
                value = value / (1.0 + jnp.exp(-value))
                if at < 2:
                    value = jnp.where(tm > 0, value, 0.0)
                high, low = split(value)
                place = pl.ds((2 * b + c) * group, group)
                act_hi[at, g, place] = high
                act_lo[at, g, place] = low

    def activated(at, these):
        return tuple(ref[at, these].reshape(-1, channels) for ref in (act_hi, act_lo))

    def convolve(frame, these, terms, first=False):
        value = functools.reduce(jnp.add, [dot3(activated(at, these), taps[lag]) for at, lag in terms])
        value = value.reshape((-1, 4 * group, channels))
        residual[frame, these] = value if first else residual[frame, these] + value

    def haar(g):
        bands = [
            residual[a, g, pl.ds((2 * b + c) * group, group)] + cells_of(feat, a, g, b, c)
            for a in range(2) for b in range(2) for c in range(2)
        ]
        for bit in (4, 2, 1):
            bands = [
                bands[j] + bands[j | bit] if not j & bit else bands[j ^ bit] - bands[j] for j in range(8)
            ]
        bands = [split(band * (1.0 / math.sqrt(8.0))) for band in bands]
        per_quarter = wide // channels
        place = pl.ds(g * group, group)
        for quarter in range(4):
            ours = bands[quarter * per_quarter : (quarter + 1) * per_quarter]
            band_hi[quarter, place] = jnp.concatenate([band[0] for band in ours], axis=1)
            band_lo[quarter, place] = jnp.concatenate([band[1] for band in ours], axis=1)

    wide = proj_all.shape[5]

    def split_quarter(half, part):
        at = 2 * half + part
        high, low = split(proj_all[half, part].reshape(width, wide))
        proj_hi[at] = high
        proj_lo[at] = low

    def quarter_of(half, part):
        at = 2 * half + part
        return dot3((band_hi[at], band_lo[at]), (proj_hi[at], proj_lo[at]), NT)

    every = pl.ds(0, groups)
    for frame in range(frames):
        plan.run(0.7, lambda: [activate(feat, frame, g, 2 + frame) for g in range(groups)])
    plan.run(0.5, lambda: convolve(0, every, [(2, 0)], True))
    plan.run(1.0, lambda: convolve(1, every, [(3, 0), (2, 1)], True))

    def join(g):
        for frame in range(frames):
            activate(halo, frame, g, frame)
        convolve(0, pl.ds(g, 1), [(1, 1), (0, 2)])
        convolve(1, pl.ds(g, 1), [(1, 2)])
        haar(g)

    other = 1 - k.core
    for g in range(groups - 1):
        plan.run(1.2, lambda: join(g), f"halo{g}")
    plan.run(0.3, lambda: split_quarter(k.core, 0), "a far")
    plan.run(1.2, lambda: join(groups - 1), f"halo{groups - 1}")
    made = plan.run(0.5, lambda: quarter_of(k.core, 0))
    proj_w.wait(0)
    plan.run(0.3, lambda: split_quarter(other, 0))
    made = made + plan.run(0.5, lambda: quarter_of(other, 0))
    plan.run(0.3, lambda: split_quarter(k.core, 1), "b")
    made = made + plan.run(0.5, lambda: quarter_of(k.core, 1))
    proj_w.wait(1)
    plan.run(0.3, lambda: split_quarter(other, 1))
    made = made + plan.run(0.5, lambda: quarter_of(other, 1))
    tokens_out[...] = made.reshape(tokens_out.shape)
    keys[z] = made
    queries[x] = made

    part_rows = count // 2
    key_chunks = 4
    key_rows = count // key_chunks
    key_ring = Ring(z, z_count, k.z_device, lambda at, c: keys.at[at, pl.ds(c * key_rows, key_rows)],
                    key_s, key_r, (steps, steps), key_chunks)
    query_ring = Ring(x, X, k.x_device, lambda at, c: queries.at[at], query_s, query_r, (X // 2, X // 2), 1,
                      lambda ref, way: ref.at[pl.ds(way * part_rows, part_rows)])
    token_group = width // GROUPS
    sums = jnp.concatenate(
        [jnp.sum(made, axis=0, keepdims=True), jnp.sum(made * made, axis=0, keepdims=True), jnp.zeros((6, width), f32)],
        axis=0,
    )
    fold = (iota((width, 128), 1) % GROUPS == iota((width, 128), 0) // token_group).astype(f32)
    token_z[z] = lanes_of(sums, fold)
    tokens_z.start()
    for way in BOTH:
        query_ring.start(way, 0)
    for chunk in range(key_chunks):
        for way in BOTH:
            key_ring.start(way, chunk)
    begin = plan.now
    for step, way, chunk in key_ring.each():
        turn = chunk if step < steps else chunk % (key_chunks // 2)
        plan.expect(begin + 2.0 + 1.5 * (key_chunks * (step - 1) + turn + 1), f"key{step}",
                    functools.partial(key_ring.step, step, way, chunk))

    def token_summed_z():
        tokens_z.wait()
        token_x[x] = jnp.sum(token_z[...], axis=0)
        tokens_x.start()

    plan.expect(begin + 2.5, "tokens z", token_summed_z)
    plan.expect(begin + 7.7, "tokens x", tokens_x.wait)
    for step, way, chunk in query_ring.each():
        plan.expect(begin + 4.9 * step + 2.9, ("near", "far")[step - 1], functools.partial(query_ring.step, step, way, chunk))

    def token_statistics():
        all_sums = jnp.sum(token_x[...], axis=0)
        unfold = (iota((128, width), 0) % GROUPS == iota((128, width), 1) // token_group).astype(f32)
        spread_sums = exact(jnp.where(lane // GROUPS == row, all_sums, 0.0), unfold)
        token_count = float(rows_count * count * token_group)
        mean = spread_sums[0:1] / token_count
        return mean, rsqrt(spread_sums[1:2] / token_count - mean * mean)

    def columns_of(block):
        first = block * width // per_block
        owners = range(first, min(rows_count, (block + 1) * width // per_block + 1))
        skip = block * width - first * per_block
        lanes = [
            jnp.concatenate([qkv_all[at // X % 2, quarter, at // X // 2, at % X] for at in owners], axis=0)[skip : skip + width]
            for quarter in range(4)
        ]
        return split(jnp.concatenate(lanes, axis=1))

    def query_key_weight():
        query_weight = tuple(jnp.transpose(part.astype(f32)).astype(bf16) for part in columns_of(0))
        return split(dot3(query_weight, columns_of(1)) * (1.0 / math.sqrt(float(width))))

    order = (2, 1, 3, 0)

    def ask(first, last):
        asking = jnp.concatenate([queries[mod(x + by, X)] for by in (2, 1, 3, 0)[first:last]], axis=0)
        for ref, value in zip((q_hi, q_lo), split(dot3(normed(asking), query_key))):
            ref[first:last] = value.reshape((last - first, count, width))

    query_key = plan.run(2.0, query_key_weight, "qkv")
    token_mean, token_scale = plan.run(0.6, token_statistics, "tokens x")
    token_gain = attn_gain[...]

    def normed(value):
        return split((value - token_mean) * token_scale * token_gain)

    plan.run(1.3, lambda: ask(1, X), "near")

    sets = [(0, -1, 1)] + [(-step, step) for step in range(2, steps)] + [(steps,)]

    def key_block(at):
        return normed(jnp.concatenate([keys[mod(z + away, z_count)] for away in sets[at]], axis=0))

    def rows_of(ref, at):
        return ref[at].reshape(-1, ref.shape[-1])

    def scores_of(at, block):
        return dot3((rows_of(q_hi, at), rows_of(q_lo, at)), block, NT)

    def attend(first, at, block, scores):
        here = jnp.max(scores, axis=1, keepdims=True)
        if first:
            weights = jnp.exp(scores - here)
            return here, jnp.sum(weights, axis=1, keepdims=True), dot3(split(weights), block)
        new_top = jnp.maximum(rows_of(top, at), here)
        fade = jnp.exp(rows_of(top, at) - new_top)
        weights = jnp.exp(scores - new_top)
        new_mass = rows_of(mass, at) * fade + jnp.sum(weights, axis=1, keepdims=True)
        return new_top, new_mass, rows_of(total, at) * fade + dot3(split(weights), block)

    def attend_all(first, at, block, scores):
        for ref, value in zip((top, mass, total), attend(first, at, block, scores)):
            ref[at] = value.reshape(-1, count, value.shape[-1])

    near, far, both = slice(1, X), slice(0, 1), slice(0, X)
    block = plan.run(0.2, lambda: key_block(0), "key1")
    scores = plan.run(1.0, lambda: scores_of(near, block))
    plan.run(1.4, lambda: attend_all(True, near, block, scores))
    plan.run(0.6, lambda: ask(0, 1), "far")
    scores = plan.run(0.5, lambda: scores_of(far, block))
    plan.run(0.6, lambda: attend_all(True, far, block, scores))
    for step in range(1, len(sets) - 1):
        block = plan.run(0.2, lambda: key_block(step), f"key{step + 1}")
        scores = plan.run(0.9, lambda: scores_of(both, block))
        plan.run(1.2, lambda: attend_all(False, both, block, scores))

    half_rows = [pl.ds(way * part_rows, part_rows) for way in BOTH]
    toward = (1, -1)

    def send(kind, way, src, dst):
        return copy(src, dst, part_s.at[kind, way], part_r.at[kind, way], k.x_device(toward[way]))

    def opposite(way):
        return (send(0, way, partial.at[0, half_rows[way]], relay.at[way]),
                send(1, way, lse_mine.at[0], relay_lse.at[way]))

    def plain(way):
        return (send(2, way, partial.at[1 + way, half_rows[1 - way]], parts.at[way, half_rows[1 - way]]),)

    def joined(way):
        return (send(3, way, joint.at[way], parts.at[way, half_rows[way]]), send(4, way, joint_lse.at[way], parts_lse.at[way]))

    def as_column(lanes):
        return jnp.transpose(jnp.broadcast_to(lanes, (count, 128)))

    def across(column):
        return jnp.concatenate([column] * (width // 128), axis=1)

    plan.need(f"key{steps}")
    block = key_block(-1)
    for first, last in ((0, 1), (1, X)):
        at = slice(first, last)
        last_top, last_mass, value = attend(False, at, block, scores_of(at, block))
        partial[at] = (value / last_mass).reshape(last - first, count, width)
        lse = last_top + jnp.log(last_mass)
        for i in range(first, last):
            column = lse[(i - first) * count : (i + 1 - first) * count]
            lse_mine[i] = jnp.transpose(jnp.broadcast_to(column, (count, 128)))[0:1]
        for way in BOTH:
            for one in opposite(way) if first == 0 else plain(way):
                one.start()
    plan.now += 1.5

    def value_to_out():
        weight_loads[1].wait()
        value_weight = tuple(jnp.transpose(part.astype(f32)).astype(bf16) for part in columns_of(2))
        return split(dot3(value_weight, split(out_in[...])))

    value_out = plan.run(2.0, value_to_out, "qkv last")
    plan.upto(1e9)
    lane_row = iota((1, 128), 1)
    for way in BOTH:
        for one in opposite(way):
            one.wait_recv()
        at = 1 + way
        own, theirs = lse_mine[at], relay_lse[way]
        both = jnp.maximum(own, theirs)
        both = both + jnp.log(jnp.exp(own - both) + jnp.exp(theirs - both))
        rows_of_way = slice(way * part_rows, (way + 1) * part_rows)
        joint[way] = (
            partial[at, half_rows[way]] * across(as_column(jnp.exp(own - both))[rows_of_way])
            + relay[way] * across(as_column(jnp.exp(theirs - both))[rows_of_way])
        )
        joint_lse[way] = jnp.where(lane_row // part_rows == way, both, own)
        for one in joined(way):
            one.start()

    proj_w.finish()
    qkv_w.finish()
    for one in halo_copies:
        one.wait_send()
    for one in (over_tm, over_x, over_z, tokens_x, tokens_z):
        one.finish()
    key_ring.finish()
    query_ring.finish()
    for way in BOTH:
        for one in (*plain(way), *joined(way)):
            one.wait_recv()
    given = [(lse_mine[3], partial[3])] + [(parts_lse[way], parts[way]) for way in BOTH]
    highest_lse = functools.reduce(jnp.maximum, [lse for lse, _ in given])
    shares = [jnp.exp(lse - highest_lse) for lse, _ in given]
    whole = functools.reduce(jnp.add, shares)
    merged = jnp.zeros((count, width), f32)
    for share, (_, value) in zip(shares, given):
        merged = merged + value * across(as_column(share / whole))
    out[...] = dot3(split(merged), value_out).reshape(out.shape)

    for way in BOTH:
        for one in (*opposite(way), *plain(way), *joined(way)):
            one.wait_send()


def shards(z_count, tm_count, features, norm_gain, conv_weight, proj_weight, attn_gain, qkv_weight, out_weight):
    frames, height, columns, channels = features.shape
    width = out_weight.shape[0]
    half_h, half_w = height // 2, columns // 2
    count = half_h * half_w
    steps = z_count // 2
    rows_count = z_count * X
    proj_rows, qkv_rows = proj_weight.shape[1], qkv_weight.shape[1]
    wide, narrow = proj_weight.shape[0] // 4, qkv_weight.shape[0] // 4
    far = 2
    vmem = pltpu.VMEM
    dma = pltpu.SemaphoreType.DMA
    proj_sems = [dma((2, steps)), dma((2, steps)), dma((3, z_count)), dma((3, z_count)), dma((X,)), dma((X,)), dma((4, steps)),
                 dma((4, steps)), dma((2,)), dma((2,))]
    qkv_sems = [dma((1,)), dma((2, X // 2)), dma((2, X // 2)), dma((z_count,)), dma((1,)), dma((4, far)), dma((4, far)), dma((2, far)),
                dma((2, far)), dma((2,)), dma((2,))]
    scratch = [
        vmem((2, frames, height, columns, 128), f32), vmem((2, frames, height, columns, 128), f32),
        vmem(conv_weight.shape, f32), vmem(out_weight.shape, f32),
        vmem((X, tm_count, 128), f32), vmem((z_count, tm_count, 128), f32), vmem((tm_count, 1, 128), f32),
        vmem((X, 1, 128), f32), vmem((z_count, 1, 128), f32),
        vmem((2, 2, z_count, X, proj_rows, wide), f32),
        vmem((2, 4, z_count // 2, X, qkv_rows, narrow), f32),
        vmem((4, 2 * half_h, 2 * half_w, channels), bf16), vmem((4, 2 * half_h, 2 * half_w, channels), bf16),
        vmem((frames, 2 * half_h, 2 * half_w, channels), f32),
        vmem((4, count, wide), bf16), vmem((4, count, wide), bf16),
        vmem((4, width, wide), bf16), vmem((4, width, wide), bf16),
        vmem((z_count, count, width), f32),
        vmem((X, count, width), f32),
        vmem((X, count, width), bf16), vmem((X, count, width), bf16),
        vmem((X, count, width), f32), vmem((X, count, 1), f32), vmem((X, count, 1), f32),
        vmem((X, count, width), f32), vmem((X, 1, 128), f32),
        vmem((2, count // 2, width), f32), vmem((2, 1, 128), f32),
        vmem((2, count // 2, width), f32), vmem((2, 1, 128), f32),
        vmem((2, count, width), f32), vmem((2, 1, 128), f32),
        dma((6,)), dma((frames, 2 * half_h)), dma((frames, 2 * half_h)), dma((6,)), dma((6,)),
        *proj_sems, *qkv_sems,
        dma((8, steps)), dma((8, steps)), dma((2, X // 2)), dma((2, X // 2)), dma((5, 2)), dma((5, 2)),
    ]
    whole = pl.BlockSpec(memory_space=vmem)
    anywhere = pl.BlockSpec(memory_space=pl.ANY)
    given = jax.ShapeDtypeStruct((frames // 2, half_h, half_w, width), f32)
    tokens, attended = pl.pallas_call(
        functools.partial(kernel, z_count, tm_count),
        out_shape=(given, given),
        in_specs=[anywhere, whole, anywhere, anywhere, whole, anywhere, anywhere],
        out_specs=(whole, whole),
        scratch_shapes=scratch,
        compiler_params=pltpu.CompilerParams(collective_id=0, has_side_effects=True, vmem_limit_bytes=56 * 2**20),
    )(features, norm_gain[None], conv_weight, proj_weight.T, attn_gain[None], qkv_weight.T, out_weight)
    return tokens + attended


def solution(mesh):
    in_specs = (P("tm", "rows", None, None), P(), P(), P(None, "rows"), P(), P(None, "rows"), P())
    out_specs = P("tm", "rows", None, None)
    body = functools.partial(shards, mesh.shape["rows"] // X, mesh.shape["tm"])
    return jax.shard_map(body, mesh=mesh, in_specs=in_specs, out_specs=out_specs, check_vma=False)
```

```python
import functools
import math

import jax
import jax.numpy as jnp
from jax import lax
from jax.experimental import pallas as pl
from jax.experimental.pallas import tpu as pltpu
from jax.sharding import PartitionSpec as P

GROUPS = 32
X = 4
epsilon = 1e-06
f32, bf16 = jnp.float32, jnp.bfloat16
NN = (((1,), (0,)), ((), ()))
NT = (((1,), (1,)), ((), ()))
BOTH = (0, 1)
SLOWER = 1.4


def split(value):
    high = value.astype(bf16)
    return high, (value - high.astype(f32)).astype(bf16)


def dot(a, b, dims):
    return lax.dot_general(a, b, dims, preferred_element_type=f32)


def dot3(a, b, dims=NN):
    rows = a[0].shape[0]
    if rows > 256:
        deep = (b[0], b[0], b[1])
        return dot(jnp.concatenate((a[0], a[1], a[0]), axis=1), jnp.concatenate(deep, axis=dims[0][1][0]), dims)
    by_high = dot(jnp.concatenate(a, axis=0), b[0], dims)
    return by_high[:rows] + (by_high[rows:] + dot(a[0], b[1], dims))


def exact(a, table):
    high = a.astype(bf16)
    rest = a - high.astype(f32)
    middle = rest.astype(bf16)
    low = (rest - middle.astype(f32)).astype(bf16)
    rows = a.shape[0]
    parts = jnp.concatenate([part.astype(f32) for part in (high, middle, low)] + [jnp.zeros_like(a)], axis=0).astype(bf16)
    by_part = dot(parts, table.astype(bf16), NN)
    return by_part[:rows] + (by_part[rows : 2 * rows] + by_part[2 * rows : 3 * rows])


def iota(shape, axis):
    return lax.broadcasted_iota(jnp.int32, shape, axis)


def rsqrt(value):
    return lax.rsqrt(value + epsilon)


def mod(value, size):
    return lax.rem(value + size, size)


class Plan:
    def __init__(self):
        self.now, self.waits = 0.0, []

    def expect(self, time, name, action):
        self.waits.append((time, len(self.waits), name, action))

    def upto(self, time):
        while True:
            due = [wait for wait in self.waits if wait[0] <= time]
            if not due:
                return
            first = min(due, key=lambda wait: wait[:2])
            self.waits.remove(first)
            first[3]()

    def need(self, name):
        times = [wait[0] for wait in self.waits if wait[2] == name]
        if times:
            self.now = max(self.now, max(times))
            self.upto(max(times))

    def run(self, duration, action, *needs):
        for name in needs:
            self.need(name)
        self.upto(self.now)
        result = action()
        self.now += SLOWER * duration
        return result


class Links:
    def __init__(self, z_count, x_count, tm_count):
        self.rows, self.tm = lax.axis_index("rows"), lax.axis_index("tm")
        self.z, self.x = lax.div(self.rows, x_count), lax.rem(self.rows, x_count)
        self.y, self.core = lax.div(self.tm, 2), lax.rem(self.tm, 2)
        self.z_count, self.x_count, self.y_count = z_count, x_count, tm_count // 2

    def z_device(self, by):
        return {"rows": mod(self.z + by, self.z_count) * self.x_count + self.x}

    def x_device(self, by):
        return {"rows": self.z * self.x_count + mod(self.x + by, self.x_count)}

    def y_device(self, by):
        return {"tm": mod(self.y + by, self.y_count) * 2 + self.core}

    def tm_device(self, by):
        return {"tm": mod(self.tm + by, 2 * self.y_count)}

    def sibling(self):
        return {"tm": self.tm + 1 - 2 * self.core}


def copy(src, dst, send, recv, device):
    return pltpu.make_async_remote_copy(
        src_ref=src, dst_ref=dst, send_sem=send, recv_sem=recv, device_id=device,
        device_id_type=pl.DeviceIdType.MESH,
    )


class Ring:
    def __init__(self, place, count, device, at, send, recv, reach, chunks=1, half=None, arrived=None):
        self.place, self.count, self.device, self.at, self.half = place, count, device, at, half
        self.send, self.recv, self.reach, self.chunks, self.arrived = send, recv, reach, chunks, arrived

    def moves(self, step, way, chunk):
        if step > self.reach[way]:
            return False
        shared = step == self.reach[0] == self.reach[1] and 2 * step == self.count
        return not shared or self.chunks == 1 or chunk // (self.chunks // 2) == way

    def ref(self, away, step, way, chunk):
        ref = self.at(mod(self.place + away, self.count), chunk)
        return self.half(ref, way) if self.half and 2 * step == self.count else ref

    def copy(self, step, way, chunk, away):
        ref = self.ref(away, step, way, chunk)
        at = (way * self.chunks + chunk, step - 1)
        return copy(ref, ref, self.send.at[at], self.recv.at[at], self.device(1 if way == 0 else -1))

    def outgoing(self, step, way, chunk):
        return self.copy(step, way, chunk, 1 - step if way == 0 else step - 1)

    def start(self, way, chunk):
        self.outgoing(1, way, chunk).start()

    def step(self, step, way, chunk):
        if not self.moves(step, way, chunk):
            return
        away = -step if way == 0 else step
        self.copy(step, way, chunk, away).wait_recv()
        if self.moves(step + 1, way, chunk):
            self.outgoing(step + 1, way, chunk).start()
        if self.arrived:
            self.arrived(self.ref(away, step, way, chunk))

    def each(self):
        for step in range(1, max(self.reach) + 1):
            for chunk in range(self.chunks):
                for way in BOTH:
                    if self.moves(step, way, chunk):
                        yield step, way, chunk

    def finish(self):
        for step, way, chunk in self.each():
            self.outgoing(step, way, chunk).wait_send()


class Sums:
    def __init__(self, slots, index, per, size, device, send, recv):
        self.slots, self.index, self.per, self.size, self.device = slots, index, per, size, device
        self.send, self.recv = send, recv

    def copies(self, by):
        ref = self.slots.at[pl.ds(self.index * self.per, self.per)]
        return copy(ref, ref, self.send, self.recv, self.device(by))

    def everything(self):
        ref = self.slots.at[pl.ds(0, (self.size - 1) * self.per)]
        return copy(ref, ref, self.send, self.recv, self.device(1))

    def start(self):
        for by in range(1, self.size):
            self.copies(by).start()

    def wait(self):
        self.everything().wait_recv()

    def finish(self):
        self.everything().wait_send()


class Proj:
    def __init__(self, links, buf, sems):
        self.k, self.buf = links, buf
        az_s, az_r, self.ax_s, self.ax_r, self.bx_s, self.bx_r, bz_s, bz_r, self.c_s, self.c_r = sems
        self.core = links.core
        rows, xs, steps = buf.shape[4] // 2, links.x_count // 2, links.z_count // 2
        self.first = Ring(links.z, links.z_count, links.z_device, lambda z, chunk: buf.at[self.core, 0, z, links.x],
                          az_s, az_r, (steps, steps), 1, lambda ref, way: ref.at[pl.ds(way * rows, rows)])
        self.second = Ring(links.z, links.z_count, links.z_device,
                           lambda z, chunk: buf.at[self.core, 1, z, pl.ds(chunk * xs, xs)],
                           bz_s, bz_r, (steps, steps), 2, None, self.hand_second)
        self.steps = steps

    def block(self, away, x_away):
        return self.buf.at[self.core, 0, mod(self.k.z + away, self.k.z_count), mod(self.k.x + x_away, self.k.x_count)]

    def ax(self, kind, away, x_away):
        ref = self.block(away, x_away)
        up = self.goes_up(away) if kind == 2 else kind == 0
        at = (kind, away % self.k.z_count)
        return copy(ref, ref, self.ax_s.at[at], self.ax_r.at[at], self.k.x_device(1 if up else -1))

    def goes_up(self, away):
        return away % self.k.z_count < self.steps

    def a_out(self, away):
        for kind in range(2):
            self.ax(kind, away, 0).start()

    def a_on(self, away):
        for kind, x_away in enumerate((-1, 1)):
            self.ax(kind, away, x_away).wait_recv()
        self.ax(2, away, -1 if self.goes_up(away) else 1).start()

    def aways(self, n):
        return (0,) if n == 0 else (-n, n) if n < self.steps else (n,)

    def bx(self, by, away):
        ref = self.buf.at[self.core, 1, self.k.z, mod(self.k.x + away, self.k.x_count)]
        return copy(ref, ref, self.bx_s.at[by], self.bx_r.at[by], self.k.x_device(by))

    def hand(self, part, ref):
        return copy(ref, ref, self.c_s.at[part], self.c_r.at[part], self.k.sibling())

    def hand_second(self, ref):
        self.hand(1, ref).start()

    def start(self):
        for by in range(1, self.k.x_count):
            self.bx(by, 0).start()
        for way in BOTH:
            self.first.start(way, 0)
        self.a_out(0)

    def a_step(self, n):
        for way in BOTH:
            self.first.step(n, way, 0)
        for away in self.aways(n):
            self.a_out(away)

    def a_pass(self, n):
        for away in self.aways(n):
            self.a_on(away)

    def b_start(self):
        for by in range(1, self.k.x_count):
            self.bx(by, -by).wait_recv()
        for chunk in range(2):
            for way in BOTH:
                self.second.start(way, chunk)
        self.hand(1, self.buf.at[self.core, 1, self.k.z]).start()

    def b_step(self, n, chunk):
        for way in BOTH:
            self.second.step(n, way, chunk)

    def a_hand(self, by):
        self.hand(0, self.buf.at[self.core, 0, :, mod(self.k.x + by, self.k.x_count)]).start()

    def a_near(self):
        for by in (0, -1, 1):
            self.a_hand(by)

    def a_far(self):
        for away in range(self.k.z_count):
            self.ax(2, away, 2).wait_recv()
        self.a_hand(2)

    def wait(self, part):
        self.hand(part, self.buf.at[1 - self.core, part]).wait_recv()

    def finish(self):
        self.first.finish()
        self.second.finish()
        for by in range(1, self.k.x_count):
            self.bx(by, 0).wait_send()
        for away in range(self.k.z_count):
            for kind in range(3):
                self.ax(kind, away, 0).wait_send()
        for part in range(2):
            self.hand(part, self.buf.at[self.core, part]).wait_send()


class Qkv:
    def __init__(self, links, piece, buf, sems):
        self.k, self.buf, self.source = links, buf, piece
        self.load_s, x_s, x_r, self.z_s, self.z_r, e_s, e_r, l_s, l_r, self.c_s, self.c_r = sems
        self.zs, self.xs = buf.shape[2], buf.shape[3]
        self.early = early = self.zs * 3 // 4
        places, self.quarter = 4, lax.rem(links.y, 4)
        reach = (1, 2)
        half = self.xs // 2
        mine = lambda y, *rest: buf.at[(links.core, y, *rest)]
        self.first = Ring(self.quarter, places, links.y_device,
                          lambda y, c: mine(y, pl.ds(0, early), pl.ds(c * half, half)),
                          e_s, e_r, reach, 2, None, lambda ref: self.hand(0, ref).start())
        self.last = Ring(self.quarter, places, links.y_device, lambda y, c: mine(y, pl.ds(early, self.zs - early)),
                         l_s, l_r, reach, 1, None, lambda ref: self.hand(1, ref).start())
        halves = self.zs // 2
        self.over_x = Ring(links.x, links.x_count, links.x_device, lambda x, c: mine(self.quarter, slice(None), x), x_s, x_r,
                           (links.x_count // 2,) * 2, 1, lambda ref, way: ref.at[pl.ds(way * halves, halves)])
        self.sends = lax.rem(links.z, 2) == links.core
        self.zz = lax.div(links.z, 2)

    def load(self):
        return pltpu.make_async_copy(self.source, self.buf.at[self.k.core, self.quarter, self.zz, self.k.x], self.load_s.at[0])

    def preload(self):
        pl.when(self.sends)(lambda: self.load().start())

    def z_copy(self, by):
        ref = self.buf.at[self.k.core, self.quarter, self.zz, self.k.x]
        return copy(ref, ref, self.z_s.at[by], self.z_r.at[0], self.k.z_device(by))

    def start(self):
        @pl.when(self.sends)
        def _():
            self.load().wait()
            for by in range(1, self.k.z_count):
                self.z_copy(by).start()

    def across(self):
        def got(count):
            ref = self.buf.at[self.k.core, self.quarter, pl.ds(0, count), self.k.x]
            copy(ref, ref, self.z_s.at[0], self.z_r.at[0], self.k.z_device(1)).wait_recv()

        pl.when(self.sends)(lambda: got(self.zs - 1))
        pl.when(jnp.logical_not(self.sends))(lambda: got(self.zs))
        for way in BOTH:
            self.over_x.start(way, 0)

    def pass_x(self):
        for way in BOTH:
            self.over_x.step(1, way, 0)

    def collect(self):
        for way in BOTH:
            self.over_x.step(2, way, 0)
        for chunk in range(2):
            self.first.start(1, chunk)
        for part in range(2):
            self.hand(part, self.part_of(part, self.k.core, self.quarter)).start()

    def up(self):
        for chunk in range(2):
            self.first.start(0, chunk)

    def rest(self):
        for way in BOTH:
            self.last.start(way, 0)

    def hand(self, part, ref):
        return copy(ref, ref, self.c_s.at[part], self.c_r.at[part], self.k.sibling())

    def part_of(self, part, core, y):
        zs = pl.ds(0, self.early) if part == 0 else pl.ds(self.early, self.zs - self.early)
        return self.buf.at[core, y, zs]

    def all_of(self, part, core):
        return self.hand(part, self.part_of(part, core, slice(None)))

    def wait(self, part):
        self.all_of(part, 1 - self.k.core).wait_recv()

    def finish(self):
        self.first.finish()
        self.last.finish()
        for part in range(2):
            self.all_of(part, self.k.core).wait_send()

        self.over_x.finish()

        @pl.when(self.sends)
        def _():
            for by in range(1, self.k.z_count):
                self.z_copy(by).wait_send()


def kernel(
    z_count, tm_count,
    features, gain, conv, proj, attn_gain, qkv, out_weight, tokens_out, out,
    feat, halo, conv_in, out_in, x_sums, z_sums, slab_sums, token_x, token_z,
    proj_all, qkv_all, act_hi, act_lo, residual, band_hi, band_lo, proj_hi, proj_lo, keys, queries, q_hi, q_lo, total, top, mass,
    partial, lse_mine, relay, relay_lse, joint, joint_lse, parts, parts_lse,
    load_s, halo_s, halo_r, sum_s, sum_r, *sems,
):
    proj_sems, qkv_sems, sems = sems[:10], sems[10:21], sems[21:]
    key_s, key_r, query_s, query_r, part_s, part_r = sems
    k = Links(z_count, X, tm_count)
    rows_count = z_count * X
    tm, z, x = k.tm, k.z, k.x
    frames, height, columns, channels = features.shape
    half_w = columns // 2
    count = (height // 2) * half_w
    width = keys.shape[2]
    wide = proj_all.shape[5]
    per_block, narrow = qkv_all.shape[4:]
    steps = z_count // 2
    plan = Plan()

    loads = [
        pltpu.make_async_copy(features.at[:, :, :, pl.ds(128 * half, 128)], feat.at[half], load_s.at[half])
        for half in range(2)
    ]
    for load in loads:
        load.start()
    barrier = pltpu.get_barrier_semaphore()
    peers = (
        [k.x_device(by) for by in range(1, X)] + [k.z_device(by) for by in range(1, z_count)]
        + [k.tm_device(by) for by in range(1, tm_count)]
    )
    for peer in peers:
        pl.semaphore_signal(barrier, inc=1, device_id=peer, device_id_type=pl.DeviceIdType.MESH)

    quarters = [
        pltpu.make_async_copy(
            proj.at[:, pl.ds(pl.multiple_of((2 * k.core + part) * wide, wide), wide)],
            proj_all.at[k.core, part, z, x], load_s.at[2 + part],
        )
        for part in range(2)
    ]
    piece = qkv.at[:, pl.ds(pl.multiple_of(lax.rem(k.y, 4) * narrow, narrow), narrow)]
    proj_w = Proj(k, proj_all, proj_sems)
    qkv_w = Qkv(k, piece, qkv_all, qkv_sems)
    for one in quarters:
        one.start()
    qkv_w.preload()
    weight_loads = [
        pltpu.make_async_copy(conv, conv_in, load_s.at[4]), pltpu.make_async_copy(out_weight, out_in, load_s.at[5])
    ]
    for one in weight_loads:
        one.start()

    lane = iota((8, 128), 1)
    row = iota((8, 128), 0)
    sums = []
    for load in loads:
        load.wait()
    for frame in range(frames):
        values = jnp.concatenate([feat[half, frame].reshape(height * columns, 128) for half in range(2)], axis=1)
        sums += [jnp.sum(values, axis=0, keepdims=True), jnp.sum(values * values, axis=0, keepdims=True)]
    stacked = jnp.concatenate(sums + [jnp.zeros((4, channels), f32)], axis=0)
    per_group = channels // GROUPS
    fold = (iota((channels, 128), 1) % GROUPS == iota((channels, 128), 0) // per_group).astype(f32)

    def lanes_of(rows_of_sums, table):
        return jnp.sum(jnp.where(lane // GROUPS == row, exact(rows_of_sums, table), 0.0), axis=0, keepdims=True)

    slab_sums[tm] = lanes_of(stacked, fold)
    for one in quarters:
        one.wait()

    def exchange(slots, index, per, size, device, n):
        return Sums(slots, index, per, size, device, sum_s.at[n], sum_r.at[n])

    over_tm = exchange(slab_sums, tm, 1, tm_count, k.tm_device, 0)
    over_x = exchange(x_sums, x, 1, X, k.x_device, 1)
    over_z = exchange(z_sums, z, 1, z_count, k.z_device, 2)
    tokens_z = exchange(token_z, z, 1, z_count, k.z_device, 3)
    tokens_x = exchange(token_x, x, 1, X, k.x_device, 4)

    pl.semaphore_wait(barrier, len(peers))
    over_tm.start()
    groups = 2 * (height // 2)
    group = count // groups

    def halo_copy(f, g):
        at = (slice(None), f, pl.ds(2 * (g // 2), 2), pl.ds(g % 2 * 2 * group, 2 * group))
        return copy(feat.at[at], halo.at[at], halo_s.at[f, g], halo_r.at[f, g], {"tm": mod(tm + 1, tm_count)})

    halo_copies = [halo_copy(f, g) for g in range(groups) for f in range(frames)]
    for one in halo_copies:
        one.start()
    proj_w.start()
    qkv_w.start()
    plan.now = 4.0

    def summed_tm():
        over_tm.wait()
        x_sums[x] = jnp.concatenate([slab_sums[i] for i in range(tm_count)], axis=0)
        over_x.start()

    def summed_x():
        over_x.wait()
        z_sums[z] = jnp.sum(x_sums[...], axis=0)
        over_z.start()

    plan.expect(6.4, "tm", summed_tm)
    plan.expect(9.0, "x", summed_x)
    plan.expect(7.8, "qkv x", qkv_w.across)
    plan.expect(6.8, "b", proj_w.b_start)
    plan.expect(7.5, "a", functools.partial(proj_w.a_pass, 0))
    for n in range(1, steps + 1):
        plan.expect(4.0 + 2.7 * n, "a", functools.partial(proj_w.a_step, n))
        plan.expect(7.0 + 2.7 * n, "a", functools.partial(proj_w.a_pass, n))
        for chunk in range(2):
            plan.expect(8.8 + 1.8 * (2 * n - 1 + chunk), "b", functools.partial(proj_w.b_step, n, chunk))
    plan.expect(7.1 + 2.7 * steps, "a", proj_w.a_near)
    plan.expect(10.0 + 2.7 * steps, "a far", proj_w.a_far)
    plan.expect(10.3, "qkv x", qkv_w.pass_x)
    plan.expect(13.0, "collect", qkv_w.collect)
    plan.expect(12.0, "z", over_z.wait)
    for g in range(groups):
        for frame in range(frames):
            plan.expect(10.0 + 3.65 * g + 0.05 * frame, f"halo{g}", halo_copy(frame, g).wait_recv)
    plan.expect(16.5, "up", qkv_w.up)
    qkv_done = 0.0
    for step, way, chunk in qkv_w.first.each():
        time = (15.0 if way else 18.5) + 3.2 * (2 * step - 1 + chunk)
        qkv_done = max(qkv_done, time)
        plan.expect(time, "qkv", functools.partial(qkv_w.first.step, step, way, chunk))
    plan.expect(qkv_done + 0.1, "rest", qkv_w.rest)
    plan.expect(qkv_done + 1.7, "qkv", functools.partial(qkv_w.wait, 0))
    for step, way, chunk in qkv_w.last.each():
        plan.expect(qkv_done + 5.0 + 2.5 * step, "qkv last", functools.partial(qkv_w.last.step, step, way, chunk))
    plan.expect(qkv_done + 7.0 + 2.5 * max(qkv_w.last.reach), "qkv last", functools.partial(qkv_w.wait, 1))

    def split_taps():
        weight_loads[0].wait()
        return [split(conv_in[lag]) for lag in range(3)]

    taps = plan.run(0.4, split_taps)

    def statistics():
        everything = jnp.sum(z_sums[...], axis=0)
        slab = iota(everything.shape, 0)

        def of(these):
            return jnp.sum(jnp.where(these, everything, 0.0), axis=0, keepdims=True)

        earlier, previous, own = of(slab < tm - 1), of(slab == tm - 1), of(slab == tm)
        kind, upto = row % 2, row // 2
        lane_kind, lane_frame = lane // GROUPS % 2, lane // GROUPS // 2
        mine = lane_kind == kind
        running = (
            jnp.where(mine, earlier, 0.0)
            + jnp.where(mine & (lane_frame <= upto), previous, 0.0)
            + jnp.where(mine & (lane_frame <= upto - 2), own, 0.0)
        )
        unfold = (iota((128, channels), 0) % GROUPS == iota((128, channels), 1) // per_group).astype(f32)
        running = exact(running, unfold)
        means, scales = [], []
        for i in range(4):
            position = jnp.maximum(tm * frames + i - 1, 1).astype(f32)
            cells = position * float(rows_count * height * columns * per_group)
            mean = running[2 * i : 2 * i + 1] / cells
            variance = running[2 * i + 1 : 2 * i + 2] / cells - mean * mean
            means.append(mean)
            scales.append(rsqrt(variance))
        return means, scales

    means, scales = plan.run(0.6, statistics, "z")
    norm_gain = gain[...]

    def cells_of(src, frame, g, b, c):
        place = pl.ds(g % 2 * 2 * group + c, group, stride=2)
        return jnp.concatenate([src[half, frame, 2 * (g // 2) + b, place, :] for half in range(2)], axis=1)

    def activate(src, frame, g, at):
        for b in range(2):
            for c in range(2):
                value = (cells_of(src, frame, g, b, c) - means[at]) * scales[at] * norm_gain
                value = value / (1.0 + jnp.exp(-value))
                if at < 2:
                    value = jnp.where(tm > 0, value, 0.0)
                high, low = split(value)
                place = pl.ds((2 * b + c) * group, group)
                act_hi[at, g, place] = high
                act_lo[at, g, place] = low

    def activated(at, these):
        return tuple(ref[at, these].reshape(-1, channels) for ref in (act_hi, act_lo))

    def convolve(frame, these, terms, first=False):
        value = functools.reduce(jnp.add, [dot3(activated(at, these), taps[lag]) for at, lag in terms])
        value = value.reshape((-1, 4 * group, channels))
        residual[frame, these] = value if first else residual[frame, these] + value

    def haar(g):
        bands = [
            residual[a, g, pl.ds((2 * b + c) * group, group)] + cells_of(feat, a, g, b, c)
            for a in range(2) for b in range(2) for c in range(2)
        ]
        for bit in (4, 2, 1):
            bands = [
                bands[j] + bands[j | bit] if not j & bit else bands[j ^ bit] - bands[j] for j in range(8)
            ]
        bands = [split(band * (1.0 / math.sqrt(8.0))) for band in bands]
        per_quarter = wide // channels
        place = pl.ds(g * group, group)
        for quarter in range(4):
            ours = bands[quarter * per_quarter : (quarter + 1) * per_quarter]
            band_hi[quarter, place] = jnp.concatenate([band[0] for band in ours], axis=1)
            band_lo[quarter, place] = jnp.concatenate([band[1] for band in ours], axis=1)

    wide = proj_all.shape[5]

    def split_quarter(half, part):
        at = 2 * half + part
        high, low = split(proj_all[half, part].reshape(width, wide))
        proj_hi[at] = high
        proj_lo[at] = low

    def quarter_of(half, part):
        at = 2 * half + part
        return dot3((band_hi[at], band_lo[at]), (proj_hi[at], proj_lo[at]), NT)

    every = pl.ds(0, groups)
    for frame in range(frames):
        plan.run(0.7, lambda: [activate(feat, frame, g, 2 + frame) for g in range(groups)])
    plan.run(0.5, lambda: convolve(0, every, [(2, 0)], True))
    plan.run(1.0, lambda: convolve(1, every, [(3, 0), (2, 1)], True))

    def join(g):
        for frame in range(frames):
            activate(halo, frame, g, frame)
        convolve(0, pl.ds(g, 1), [(1, 1), (0, 2)])
        convolve(1, pl.ds(g, 1), [(1, 2)])
        haar(g)

    other = 1 - k.core
    for g in range(groups - 1):
        plan.run(1.2, lambda: join(g), f"halo{g}")
    plan.run(0.3, lambda: split_quarter(k.core, 0), "a far")
    plan.run(1.2, lambda: join(groups - 1), f"halo{groups - 1}")
    made = plan.run(0.5, lambda: quarter_of(k.core, 0))
    proj_w.wait(0)
    plan.run(0.3, lambda: split_quarter(other, 0))
    made = made + plan.run(0.5, lambda: quarter_of(other, 0))
    plan.run(0.3, lambda: split_quarter(k.core, 1), "b")
    made = made + plan.run(0.5, lambda: quarter_of(k.core, 1))
    proj_w.wait(1)
    plan.run(0.3, lambda: split_quarter(other, 1))
    made = made + plan.run(0.5, lambda: quarter_of(other, 1))
    tokens_out[...] = made.reshape(tokens_out.shape)
    keys[z] = made
    queries[x] = made

    part_rows = count // 2
    key_chunks = 4
    key_rows = count // key_chunks
    key_ring = Ring(z, z_count, k.z_device, lambda at, c: keys.at[at, pl.ds(c * key_rows, key_rows)],
                    key_s, key_r, (steps, steps), key_chunks)
    query_ring = Ring(x, X, k.x_device, lambda at, c: queries.at[at], query_s, query_r, (X // 2, X // 2), 1,
                      lambda ref, way: ref.at[pl.ds(way * part_rows, part_rows)])
    token_group = width // GROUPS
    sums = jnp.concatenate(
        [jnp.sum(made, axis=0, keepdims=True), jnp.sum(made * made, axis=0, keepdims=True), jnp.zeros((6, width), f32)],
        axis=0,
    )
    fold = (iota((width, 128), 1) % GROUPS == iota((width, 128), 0) // token_group).astype(f32)
    token_z[z] = lanes_of(sums, fold)
    tokens_z.start()
    for way in BOTH:
        query_ring.start(way, 0)
    for chunk in range(key_chunks):
        for way in BOTH:
            key_ring.start(way, chunk)
    begin = plan.now
    for step, way, chunk in key_ring.each():
        turn = chunk if step < steps else chunk % (key_chunks // 2)
        plan.expect(begin + 2.0 + 1.5 * (key_chunks * (step - 1) + turn + 1), f"key{step}",
                    functools.partial(key_ring.step, step, way, chunk))

    def token_summed_z():
        tokens_z.wait()
        token_x[x] = jnp.sum(token_z[...], axis=0)
        tokens_x.start()

    plan.expect(begin + 2.5, "tokens z", token_summed_z)
    plan.expect(begin + 7.7, "tokens x", tokens_x.wait)
    for step, way, chunk in query_ring.each():
        plan.expect(begin + 4.9 * step + 2.9, ("near", "far")[step - 1], functools.partial(query_ring.step, step, way, chunk))

    def token_statistics():
        all_sums = jnp.sum(token_x[...], axis=0)
        unfold = (iota((128, width), 0) % GROUPS == iota((128, width), 1) // token_group).astype(f32)
        spread_sums = exact(jnp.where(lane // GROUPS == row, all_sums, 0.0), unfold)
        token_count = float(rows_count * count * token_group)
        mean = spread_sums[0:1] / token_count
        return mean, rsqrt(spread_sums[1:2] / token_count - mean * mean)

    def columns_of(block):
        first = block * width // per_block
        owners = range(first, min(rows_count, (block + 1) * width // per_block + 1))
        skip = block * width - first * per_block
        lanes = [
            jnp.concatenate([qkv_all[at // X % 2, quarter, at // X // 2, at % X] for at in owners], axis=0)[skip : skip + width]
            for quarter in range(4)
        ]
        return split(jnp.concatenate(lanes, axis=1))

    def query_key_weight():
        query_weight = tuple(jnp.transpose(part.astype(f32)).astype(bf16) for part in columns_of(0))
        return split(dot3(query_weight, columns_of(1)) * (1.0 / math.sqrt(float(width))))

    order = (2, 1, 3, 0)

    def ask(first, last):
        asking = jnp.concatenate([queries[mod(x + by, X)] for by in (2, 1, 3, 0)[first:last]], axis=0)
        for ref, value in zip((q_hi, q_lo), split(dot3(normed(asking), query_key))):
            ref[first:last] = value.reshape((last - first, count, width))

    query_key = plan.run(2.0, query_key_weight, "qkv")
    token_mean, token_scale = plan.run(0.6, token_statistics, "tokens x")
    token_gain = attn_gain[...]

    def normed(value):
        return split((value - token_mean) * token_scale * token_gain)

    plan.run(1.3, lambda: ask(1, X), "near")

    sets = [(0, -1, 1)] + [(-step, step) for step in range(2, steps)] + [(steps,)]

    def key_block(at):
        return normed(jnp.concatenate([keys[mod(z + away, z_count)] for away in sets[at]], axis=0))

    def rows_of(ref, at):
        return ref[at].reshape(-1, ref.shape[-1])

    def scores_of(at, block):
        return dot3((rows_of(q_hi, at), rows_of(q_lo, at)), block, NT)

    def attend(first, at, block, scores):
        here = jnp.max(scores, axis=1, keepdims=True)
        if first:
            weights = jnp.exp(scores - here)
            return here, jnp.sum(weights, axis=1, keepdims=True), dot3(split(weights), block)
        new_top = jnp.maximum(rows_of(top, at), here)
        fade = jnp.exp(rows_of(top, at) - new_top)
        weights = jnp.exp(scores - new_top)
        new_mass = rows_of(mass, at) * fade + jnp.sum(weights, axis=1, keepdims=True)
        return new_top, new_mass, rows_of(total, at) * fade + dot3(split(weights), block)

    def attend_all(first, at, block, scores):
        for ref, value in zip((top, mass, total), attend(first, at, block, scores)):
            ref[at] = value.reshape(-1, count, value.shape[-1])

    near, far, both = slice(1, X), slice(0, 1), slice(0, X)
    block = plan.run(0.2, lambda: key_block(0), "key1")
    scores = plan.run(1.0, lambda: scores_of(near, block))
    plan.run(1.4, lambda: attend_all(True, near, block, scores))
    plan.run(0.6, lambda: ask(0, 1), "far")
    scores = plan.run(0.5, lambda: scores_of(far, block))
    plan.run(0.6, lambda: attend_all(True, far, block, scores))
    for step in range(1, len(sets) - 1):
        block = plan.run(0.2, lambda: key_block(step), f"key{step + 1}")
        scores = plan.run(0.9, lambda: scores_of(both, block))
        plan.run(1.2, lambda: attend_all(False, both, block, scores))

    half_rows = [pl.ds(way * part_rows, part_rows) for way in BOTH]
    toward = (1, -1)

    def send(kind, way, src, dst):
        return copy(src, dst, part_s.at[kind, way], part_r.at[kind, way], k.x_device(toward[way]))

    def opposite(way):
        return (send(0, way, partial.at[0, half_rows[way]], relay.at[way]),
                send(1, way, lse_mine.at[0], relay_lse.at[way]))

    def plain(way):
        return (send(2, way, partial.at[1 + way, half_rows[1 - way]], parts.at[way, half_rows[1 - way]]),)

    def joined(way):
        return (send(3, way, joint.at[way], parts.at[way, half_rows[way]]), send(4, way, joint_lse.at[way], parts_lse.at[way]))

    def as_column(lanes):
        return jnp.transpose(jnp.broadcast_to(lanes, (count, 128)))

    def across(column):
        return jnp.concatenate([column] * (width // 128), axis=1)

    plan.need(f"key{steps}")
    block = key_block(-1)
    for first, last in ((0, 1), (1, X)):
        at = slice(first, last)
        last_top, last_mass, value = attend(False, at, block, scores_of(at, block))
        partial[at] = (value / last_mass).reshape(last - first, count, width)
        lse = last_top + jnp.log(last_mass)
        for i in range(first, last):
            column = lse[(i - first) * count : (i + 1 - first) * count]
            lse_mine[i] = jnp.transpose(jnp.broadcast_to(column, (count, 128)))[0:1]
        for way in BOTH:
            for one in opposite(way) if first == 0 else plain(way):
                one.start()
    plan.now += 1.5

    def value_to_out():
        weight_loads[1].wait()
        value_weight = tuple(jnp.transpose(part.astype(f32)).astype(bf16) for part in columns_of(2))
        return split(dot3(value_weight, split(out_in[...])))

    value_out = plan.run(2.0, value_to_out, "qkv last")
    plan.upto(1e9)
    lane_row = iota((1, 128), 1)
    for way in BOTH:
        for one in opposite(way):
            one.wait_recv()
        at = 1 + way
        own, theirs = lse_mine[at], relay_lse[way]
        both = jnp.maximum(own, theirs)
        both = both + jnp.log(jnp.exp(own - both) + jnp.exp(theirs - both))
        rows_of_way = slice(way * part_rows, (way + 1) * part_rows)
        joint[way] = (
            partial[at, half_rows[way]] * across(as_column(jnp.exp(own - both))[rows_of_way])
            + relay[way] * across(as_column(jnp.exp(theirs - both))[rows_of_way])
        )
        joint_lse[way] = jnp.where(lane_row // part_rows == way, both, own)
        for one in joined(way):
            one.start()

    proj_w.finish()
    qkv_w.finish()
    for one in halo_copies:
        one.wait_send()
    for one in (over_tm, over_x, over_z, tokens_x, tokens_z):
        one.finish()
    key_ring.finish()
    query_ring.finish()
    for way in BOTH:
        for one in (*plain(way), *joined(way)):
            one.wait_recv()
    given = [(lse_mine[3], partial[3])] + [(parts_lse[way], parts[way]) for way in BOTH]
    highest_lse = functools.reduce(jnp.maximum, [lse for lse, _ in given])
    shares = [jnp.exp(lse - highest_lse) for lse, _ in given]
    whole = functools.reduce(jnp.add, shares)
    merged = jnp.zeros((count, width), f32)
    for share, (_, value) in zip(shares, given):
        merged = merged + value * across(as_column(share / whole))
    out[...] = dot3(split(merged), value_out).reshape(out.shape)

    for way in BOTH:
        for one in (*opposite(way), *plain(way), *joined(way)):
            one.wait_send()


def shards(z_count, tm_count, features, norm_gain, conv_weight, proj_weight, attn_gain, qkv_weight, out_weight):
    frames, height, columns, channels = features.shape
    width = out_weight.shape[0]
    half_h, half_w = height // 2, columns // 2
    count = half_h * half_w
    steps = z_count // 2
    rows_count = z_count * X
    proj_rows, qkv_rows = proj_weight.shape[1], qkv_weight.shape[1]
    wide, narrow = proj_weight.shape[0] // 4, qkv_weight.shape[0] // 4
    far = 2
    vmem = pltpu.VMEM
    dma = pltpu.SemaphoreType.DMA
    proj_sems = [dma((2, steps)), dma((2, steps)), dma((3, z_count)), dma((3, z_count)), dma((X,)), dma((X,)), dma((4, steps)),
                 dma((4, steps)), dma((2,)), dma((2,))]
    qkv_sems = [dma((1,)), dma((2, X // 2)), dma((2, X // 2)), dma((z_count,)), dma((1,)), dma((4, far)), dma((4, far)), dma((2, far)),
                dma((2, far)), dma((2,)), dma((2,))]
    scratch = [
        vmem((2, frames, height, columns, 128), f32), vmem((2, frames, height, columns, 128), f32),
        vmem(conv_weight.shape, f32), vmem(out_weight.shape, f32),
        vmem((X, tm_count, 128), f32), vmem((z_count, tm_count, 128), f32), vmem((tm_count, 1, 128), f32),
        vmem((X, 1, 128), f32), vmem((z_count, 1, 128), f32),
        vmem((2, 2, z_count, X, proj_rows, wide), f32),
        vmem((2, 4, z_count // 2, X, qkv_rows, narrow), f32),
        vmem((4, 2 * half_h, 2 * half_w, channels), bf16), vmem((4, 2 * half_h, 2 * half_w, channels), bf16),
        vmem((frames, 2 * half_h, 2 * half_w, channels), f32),
        vmem((4, count, wide), bf16), vmem((4, count, wide), bf16),
        vmem((4, width, wide), bf16), vmem((4, width, wide), bf16),
        vmem((z_count, count, width), f32),
        vmem((X, count, width), f32),
        vmem((X, count, width), bf16), vmem((X, count, width), bf16),
        vmem((X, count, width), f32), vmem((X, count, 1), f32), vmem((X, count, 1), f32),
        vmem((X, count, width), f32), vmem((X, 1, 128), f32),
        vmem((2, count // 2, width), f32), vmem((2, 1, 128), f32),
        vmem((2, count // 2, width), f32), vmem((2, 1, 128), f32),
        vmem((2, count, width), f32), vmem((2, 1, 128), f32),
        dma((6,)), dma((frames, 2 * half_h)), dma((frames, 2 * half_h)), dma((6,)), dma((6,)),
        *proj_sems, *qkv_sems,
        dma((8, steps)), dma((8, steps)), dma((2, X // 2)), dma((2, X // 2)), dma((5, 2)), dma((5, 2)),
    ]
    whole = pl.BlockSpec(memory_space=vmem)
    anywhere = pl.BlockSpec(memory_space=pl.ANY)
    given = jax.ShapeDtypeStruct((frames // 2, half_h, half_w, width), f32)
    tokens, attended = pl.pallas_call(
        functools.partial(kernel, z_count, tm_count),
        out_shape=(given, given),
        in_specs=[anywhere, whole, anywhere, anywhere, whole, anywhere, anywhere],
        out_specs=(whole, whole),
        scratch_shapes=scratch,
        compiler_params=pltpu.CompilerParams(collective_id=0, has_side_effects=True, vmem_limit_bytes=56 * 2**20),
    )(features, norm_gain[None], conv_weight, proj_weight.T, attn_gain[None], qkv_weight.T, out_weight)
    return tokens + attended


def solution(mesh):
    in_specs = (P("tm", "rows", None, None), P(), P(), P(None, "rows"), P(), P(None, "rows"), P())
    out_specs = P("tm", "rows", None, None)
    body = functools.partial(shards, mesh.shape["rows"] // X, mesh.shape["tm"])
    return jax.shard_map(body, mesh=mesh, in_specs=in_specs, out_specs=out_specs, check_vma=False)
```
